32 devices in a mesh: dp: 16 (over z, y, x), tensor: 2 (over core).
Axes of the slice: x: 2, y: 2, z: 4, core: 2. Of those that a mesh axis runs over, the one named last changes fastest.
Arguments:
- latents: bfloat16 [65536, 512], P('dp'), may hold values from -6 to 6
- scene_len: int32 [128], P('dp'), may hold values from 65 to 512, as said below
- attn_gain: bfloat16 [512], replicated, may hold values from 0.25 to 1.75
- attn_shift: bfloat16 [512], replicated, may hold values from -1.75 to 1.75
- qkv_weight: bfloat16 [3, 512, 512], P(None, 'tensor'), may hold values from -0.25 to 0.25
- out_weight: bfloat16 [512, 512], P('tensor'), may hold values from -1 to 1
- out_bias: bfloat16 [512], replicated, may hold values from -1.75 to 1.75
- mlp_gain: bfloat16 [512], replicated, may hold values from 0.25 to 1.75
- mlp_shift: bfloat16 [512], replicated, may hold values from -1.75 to 1.75
- up_weight: bfloat16 [2048, 512], P('tensor'), may hold values from -0.25 to 0.25
- up_bias: bfloat16 [2048], P('tensor'), may hold values from -3 to 3
- down_weight: bfloat16 [2048, 512], P('tensor'), may hold values from -0.1875 to 0.1875
- down_bias: bfloat16 [512], replicated, may hold values from -1.75 to 1.75
- cotangent: bfloat16 [65536, 512], P('dp'), may hold values from -6 to 6
Outputs:
- block_out: bfloat16 [65536, 512], P(('dp', 'tensor'))
- grad_latents: float32 [65536, 512], P(('dp', 'tensor'))
- grad_attn_gain: float32 [512], replicated
- grad_attn_shift: float32 [512], replicated
- grad_qkv: float32 [3, 512, 512], P(None, 'tensor')
- grad_out_weight: float32 [512, 512], P('tensor')
- grad_out_bias: float32 [512], replicated
- grad_mlp_gain: float32 [512], replicated
- grad_mlp_shift: float32 [512], replicated
- grad_up_weight: float32 [2048, 512], P('tensor')
- grad_up_bias: float32 [2048], P('tensor')
- grad_down_weight: float32 [2048, 512], P('tensor')
- grad_down_bias: float32 [512], replicated
The draws below stay inside these ranges and needn't reach their ends.
Inputs may be any that keep to these rules, and one draw needn't show every extreme that they name: `scene_len`: count of valid latents of each scene; the scene's key mask keeps keys below it and masks those at or beyond it, queries are not masked. Some scene has all 512 valid.
All inputs are finite; a program needn't handle non-finite values.
Results may differ from the reference program's by a relative error of at most 0.011.
Values may be sent and summed in bfloat16 or wider, within the bound.
No kernel may reach another device: no remote copies, remote signals or barrier semaphores. Data moves between devices by JAX's collectives and lax.ppermute only.
A program may use at most 192 MiB of HBM per device.

```python
import math
import jax
import jax.numpy as jnp
from jax import lax

D = 512
H = 8
HD = 64
FF = 2048
LAT = 512
SC_DEV = 8
SCENES = 128
ROWS = 65536


def draw_scene_len(key, part):
    key = jax.random.fold_in(key, 11)
    key_level, key_cut, key_pick = jax.random.split(key, 3)
    blocks = SCENES // SC_DEV
    level = jax.random.randint(key_level, (blocks, 1), 2, 9)
    ceiling = jnp.broadcast_to(level * (LAT // 8), (blocks, SC_DEV)).reshape(SCENES)
    cut = jax.random.randint(key_cut, (SCENES,), 0, LAT // 8)
    lengths = ceiling - cut
    chosen = jax.random.randint(key_pick, (), 0, SCENES)
    lengths = jnp.where(jnp.arange(SCENES) == chosen, LAT, lengths)
    return lengths.astype(jnp.int32)


def level_of(rng, dims, shards, smallest, high):
    gain, own = 1.0, jax.random.fold_in(rng, 6)
    for axis_at, blocks in shards:
        draws = jnp.exp(jax.random.uniform(jax.random.fold_in(own, axis_at), (blocks,), jnp.float32, smallest / len(shards), high / len(shards)))
        gain = gain * jnp.repeat(draws, dims[axis_at] // blocks).reshape([-1 if axis == axis_at else 1 for axis in range(len(dims))])
    return gain


def normal_values(key, shape, width, reach, cuts=(), dtype=jnp.bfloat16):
    gain = level_of(key, shape, cuts, -0.22, 0.18) if cuts else 1.0
    drawn = jax.random.normal(key, shape, jnp.float32) * width * gain
    return jnp.minimum(jnp.maximum(drawn, -reach), reach).astype(dtype)


def setup_inputs(seed: int = 0) -> dict:
    key_list = jax.random.split(jax.random.key(seed), 15)
    return {
        "latents": normal_values(key_list[0], (ROWS, D), 1.0, 6.0, ((0, 16),)),
        "scene_len": draw_scene_len(jax.random.fold_in(key_list[14], 71), 0),
        "attn_gain": jnp.clip(1.0 + 0.15 * jax.random.normal(key_list[2], (D,), jnp.float32), 0.25, 1.75).astype(jnp.bfloat16),
        "attn_shift": normal_values(key_list[3], (D,), 0.3, 1.75),
        "qkv_weight": normal_values(key_list[4], (3, D, D), D ** -0.5, 0.25, ((1, 2),)),
        "out_weight": normal_values(key_list[5], (D, D), (D // 16) ** -0.5, 1.0, ((0, 2),)),
        "out_bias": normal_values(key_list[6], (D,), 0.3, 1.75),
        "mlp_gain": jnp.clip(1.0 + 0.15 * jax.random.normal(key_list[7], (D,), jnp.float32), 0.25, 1.75).astype(jnp.bfloat16),
        "mlp_shift": normal_values(key_list[8], (D,), 0.3, 1.75),
        "up_weight": normal_values(key_list[9], (FF, D), D ** -0.5, 0.25, ((0, 2),)),
        "up_bias": normal_values(key_list[10], (FF,), 0.5, 3.0, ((0, 2),)),
        "down_weight": normal_values(key_list[11], (FF, D), (FF // 2) ** -0.5, 0.1875, ((0, 2),)),
        "down_bias": normal_values(key_list[12], (D,), 0.3, 1.75),
        "cotangent": normal_values(key_list[13], (ROWS, D), 1.0, 6.0, ((0, 16),)),
    }


@jax.custom_vjp
def low(v):
    return lax.optimization_barrier(v.astype(jnp.bfloat16)).astype(jnp.float32)

@jax.custom_vjp
def low_back(v):
    return v

def low_keep(v):
    return (low(v), None)

def low_pass(kept, grad):
    return (grad,)

def back_keep(v):
    return (v, None)

def back_low(kept, grad):
    return (low(grad),)
low.defvjp(low_keep, low_pass)
low_back.defvjp(back_keep, back_low)
EPS = 1e-05
HIGHEST = lax.Precision.HIGHEST

def layer_norm(values, gain_row, shift_row):
    centre = lax.optimization_barrier(jnp.mean(values, -1, keepdims=True))
    centred = values - centre
    spread = lax.optimization_barrier(jnp.mean(centred * centred, -1, keepdims=True))
    return centred * lax.rsqrt(spread + EPS) * gain_row + shift_row

def scene_attention(pieces):
    q_rows, k_rows, v_rows, length = pieces
    scores = jnp.einsum('qhd,khd->hqk', q_rows, k_rows, precision=HIGHEST) * HD ** (-0.5)
    scores = low_back(scores)
    allowed = jnp.arange(LAT) < length
    scores = jnp.where(allowed[None, None, :], scores, -1e+30)
    weights = low(jax.nn.softmax(scores, axis=-1))
    return jnp.einsum('hqk,khd->qhd', weights, v_rows, precision=HIGHEST)

def block(rows, lengths, attn_gain, attn_shift, qkv_weight, out_weight, out_bias, mlp_gain, mlp_shift, up_weight, up_bias, down_weight, down_bias):
    normed_one = low(layer_norm(rows, attn_gain, attn_shift))
    projected = low_back(low(jnp.einsum('rd,thd->trh', normed_one, qkv_weight, precision=HIGHEST)))
    layout = (lengths.shape[0], LAT, H, HD)
    attended = lax.map(jax.checkpoint(scene_attention), (projected[0].reshape(layout), projected[1].reshape(layout), projected[2].reshape(layout), lengths))
    attended = low_back(low(attended.reshape(rows.shape[0], D)))
    hidden_one = rows + low_back(jnp.dot(attended, out_weight, precision=HIGHEST)) + out_bias
    normed_two = low(layer_norm(hidden_one, mlp_gain, mlp_shift))
    pre_act = low_back(jnp.einsum('rd,fd->rf', normed_two, up_weight, precision=HIGHEST) + up_bias)
    activated = low(jax.nn.gelu(pre_act, approximate=False))
    return hidden_one + low_back(jnp.dot(activated, down_weight, precision=HIGHEST)) + down_bias

def reference(latents, scene_len, attn_gain, attn_shift, qkv_weight, out_weight, out_bias, mlp_gain, mlp_shift, up_weight, up_bias, down_weight, down_bias, cotangent):
    params = tuple((p.astype(jnp.float32) for p in (attn_gain, attn_shift, qkv_weight, out_weight, out_bias, mlp_gain, mlp_shift, up_weight, up_bias, down_weight, down_bias)))
    group_size = math.gcd(SCENES, 8)
    group_count = SCENES // group_size
    rows_in = latents.astype(jnp.float32).reshape(group_count, group_size * LAT, D)
    cot_in = cotangent.astype(jnp.float32).reshape(group_count, group_size * LAT, D)
    lengths = scene_len.reshape(group_count, group_size)

    def one_group(totals, pieces):
        rows, length_row, cot_rows = pieces

        def forward(rows_arg, *weights):
            return block(rows_arg, length_row, *weights)
        output, pull = jax.vjp(forward, rows, *params)
        grads = pull(cot_rows)
        summed = tuple((a + b for a, b in zip(totals, grads[1:])))
        return (summed, (output.astype(jnp.bfloat16), grads[0]))
    start_totals = tuple((jnp.zeros(p.shape, jnp.float32) for p in params))
    totals, (outputs, grad_rows) = lax.scan(one_group, start_totals, (rows_in, lengths, cot_in))
    return (outputs.reshape(ROWS, D), grad_rows.reshape(ROWS, D), totals[0], totals[1], totals[2], totals[3], totals[4], totals[5], totals[6], totals[7], totals[8], totals[9], totals[10])
```

```python
import jax
import jax.numpy as jnp
from jax import lax
from jax.experimental import pallas as pl
from jax.experimental.pallas import tpu as pltpu
from jax.sharding import PartitionSpec as P

D = 512
HD = 64
LAT = 512
AUG = 16
EPS = 1e-05
NEG = -1e30
BF = jnp.bfloat16
F32 = jnp.float32
VMEM_LIMIT = 58 * 2**20
SWAP = [(0, 1), (1, 0)]


def _dot(a, b, ca, cb):
    return lax.dot_general(a, b, (((ca,), (cb,)), ((), ())), preferred_element_type=F32)


def nn(a, b):
    return _dot(a, b, 1, 0)


def nt(a, b):
    return _dot(a, b, 1, 1)


def tn(a, b):
    return _dot(a, b, 0, 0)


def normalised(v):
    c = v - jnp.mean(v, -1, keepdims=True)
    r = lax.rsqrt(jnp.mean(c * c, -1, keepdims=True) + EPS)
    return c * r, r


def norm_back(e, xh, r):
    return r * (e - jnp.mean(e, -1, keepdims=True) - xh * jnp.mean(e * xh, -1, keepdims=True))


def forward_kernel(
    tens, lens, x_ref, vecs, wq_own, wq_oth, wo_own, wo_oth,
    n1_ref, qkv_ref, p_ref, att_ref, rl_ref, h1_ref, n2_ref,
):
    scenes = pl.num_programs(0)
    length = lens[tens[0] * scenes + pl.program_id(0)]
    x = x_ref[...].astype(F32)
    n1 = (normalised(x)[0] * vecs[0:1] + vecs[1:2]).astype(BF)
    n1_ref[...] = n1
    half = wo_own.shape[0]
    for side, w in enumerate((wq_own, wq_oth)):
        for t in range(3):
            part = nt(w[t * half:(t + 1) * half], n1)
            if t == 0:
                part = part * HD**-0.5
            qkv_ref[0, side, t] = part.astype(BF)
    heads = wo_own.shape[0] // HD
    key_at = lax.broadcasted_iota(jnp.int32, (AUG, LAT), 1)
    row_at = lax.broadcasted_iota(jnp.int32, (AUG, LAT), 0)
    bias = jnp.where((key_at >= length) & (row_at == 0), NEG, 0.0).astype(BF)
    ones = jnp.ones((AUG, LAT), BF)
    for side in range(2):
        for h in range(heads):
            at = pl.ds(h * HD, HD)
            ka = jnp.concatenate([qkv_ref[0, side, 1, at], bias], 0)
            qa = jnp.concatenate([qkv_ref[0, side, 0, at], ones], 0)
            va = jnp.concatenate([qkv_ref[0, side, 2, at], ones], 0)
            hh = side * heads + h
            for qb in range(2):
                cols = slice(qb * 256, qb * 256 + 256)
                s = tn(ka, qa[:, cols])
                p = jnp.exp(s - jnp.max(s, 0, keepdims=True)).astype(BF)
                p_ref[0, hh, :, cols] = p
                o = nn(va, p)
                rl = 1.0 / o[HD:HD + 1]
                rl_ref[0, hh:hh + 1, cols] = rl
                att_ref[0, hh * HD:hh * HD + HD, cols] = (o[:HD] * rl).astype(BF)
    h1 = x + (tn(att_ref[0, :half], wo_own[...]) + tn(att_ref[0, half:], wo_oth[...])) + vecs[2:3]
    h1_ref[...] = h1
    n2_ref[...] = (normalised(h1)[0] * vecs[3:4] + vecs[4:5]).astype(BF)


def whole(shape, row=0):
    at = (row,) + (0,) * (len(shape) - 1)
    return pl.BlockSpec(shape, lambda i, *_: at, pipeline_mode=pl.Buffered(1))


def params():
    return pltpu.CompilerParams(vmem_limit_bytes=VMEM_LIMIT, dimension_semantics=("arbitrary",))


def vecs_spec():
    return whole((6, D))


def attention_forward(tens, lens, x, vecs, wq_own, theirs, wo_own, rows):
    scenes = rows // LAT
    rowblock = pl.BlockSpec((LAT, D), lambda i, *_: (i, 0))
    half = wo_own.shape[0]
    return pl.pallas_call(
        forward_kernel,
        grid_spec=pltpu.PrefetchScalarGridSpec(
            num_scalar_prefetch=2,
            grid=(scenes,),
            in_specs=[
                pl.BlockSpec((LAT, D), lambda i, tens, lens: (tens[0] * scenes + i, 0)),
                vecs_spec(), whole((3 * half, D)), whole((3 * half, D)), whole((half, D)), whole((half, D), 3),
            ],
            out_specs=[
                rowblock,
                pl.BlockSpec((1, 2, 3, half, LAT), lambda i, *_: (i, 0, 0, 0, 0)),
                pl.BlockSpec((1, 2 * half // HD, LAT, LAT), lambda i, *_: (i, 0, 0, 0)),
                pl.BlockSpec((1, D, LAT), lambda i, *_: (i, 0, 0)),
                pl.BlockSpec((1, 2 * half // HD, LAT), lambda i, *_: (i, 0, 0)),
                rowblock,
                rowblock,
            ],
        ),
        out_shape=[
            jax.ShapeDtypeStruct((rows, D), BF),
            jax.ShapeDtypeStruct((scenes, 2, 3, half, LAT), BF),
            jax.ShapeDtypeStruct((scenes, 2 * half // HD, LAT, LAT), BF),
            jax.ShapeDtypeStruct((scenes, D, LAT), BF),
            jax.ShapeDtypeStruct((scenes, 2 * half // HD, LAT), F32),
            jax.ShapeDtypeStruct((rows, D), F32),
            jax.ShapeDtypeStruct((rows, D), BF),
        ],
        compiler_params=params(),
        name="attention_forward",
    )(tens, lens, x, vecs, wq_own, theirs, wo_own, theirs)


ERF_P = 0.3275911 / 2**0.5
ERF_A = tuple(0.5 * a for a in (0.254829592, -0.284496736, 1.421413741, -1.453152027, 1.061405429))
LOG2E = 1.4426950408889634


def gelu_parts(z):
    t = 1.0 / (1.0 + ERF_P * jnp.abs(z))
    density = jnp.exp2(z * z * (-0.5 * LOG2E))
    poly = t * (ERF_A[0] + t * (ERF_A[1] + t * (ERF_A[2] + t * (ERF_A[3] + t * ERF_A[4]))))
    tail = poly * density
    cdf = jnp.where(z >= 0, 1.0 - tail, tail)
    return z * cdf, cdf + z * (density * 0.3989422804014327)


SUB = 256


def mlp_step(n2, cot, up, ub, down, acc_up, acc_down, acc_ub):
    out, back = 0.0, 0.0
    first = pl.program_id(0) == 0

    @pl.when(first)
    def _():
        acc_up[...] = jnp.zeros_like(acc_up)
        acc_down[...] = jnp.zeros_like(acc_down)
        acc_ub[...] = jnp.zeros_like(acc_ub)

    for j in range(up.shape[0] // SUB):
        at = slice(j * SUB, j * SUB + SUB)
        u, d = up[at], down[at]
        pre = nt(n2, u) + ub[:, at].astype(F32)
        act, slope = gelu_parts(pre)
        act = act.astype(BF)
        dpre = (nt(cot, d) * slope).astype(BF)
        out += nn(act, d)
        back += nn(dpre, u)
        acc_down[at] += tn(act, cot)
        acc_up[at] += tn(dpre, n2)
        acc_ub[:, at] += jnp.sum(dpre.astype(F32), 0, keepdims=True)
    return out, back


def mlp_first_kernel(
    tens, n2_ref, cot_ref, up, ub, down, h1_ref, vecs,
    out_ref, back_ref, grads_ref, acc_up, acc_down, acc_ub,
):
    out, back = mlp_step(n2_ref[...], cot_ref[...], up, ub, down, acc_up, acc_down, acc_ub)
    out_ref[...] = out + h1_ref[...] + vecs[5:6]
    back_ref[...] = back

    @pl.when(pl.program_id(0) == pl.num_programs(0) - 1)
    def _():
        units = acc_up.shape[0]
        put_slabs(grads_ref, 0, acc_up)
        put_slabs(grads_ref, 4 * units, acc_down)
        put_row(grads_ref, 8 * units, acc_ub, 16)


def put_slabs(out, at, values):
    n = values.shape[0]
    for c in range(D // 128):
        out[at + c * n:at + (c + 1) * n] = values[:, c * 128:c * 128 + 128].astype(out.dtype)


def put_row(out, at, row, count):
    parts = [row[:, c * 128:c * 128 + 128] for c in range(row.shape[1] // 128)]
    parts += [jnp.zeros((1, 128), F32)] * (count - len(parts))
    out[at:at + count] = jnp.concatenate(parts, 0).astype(out.dtype)


def mlp_second_kernel(
    tens, n2_ref, cot_ref, up, ub, down, h1_ref, out_in, back_in, vecs, att_ref, rl_ref, wo_own, wo_oth,
    block_ref, gh_ref, doa_ref, grads_ref, wo_oth_ref, cols_ref, acc_up, acc_down, acc_ub, acc_wo,
):
    cot = cot_ref[...]
    out, back = mlp_step(n2_ref[...], cot, up, ub, down, acc_up, acc_down, acc_ub)
    block_ref[...] = (out + out_in[...]).astype(BF)
    g = back + back_in[...]
    xh, r = normalised(h1_ref[...])
    cot32 = cot.astype(F32)
    gh = cot32 + norm_back(g * vecs[3:4], xh, r)
    gh_ref[...] = gh
    gb = gh.astype(BF)
    half = wo_own.shape[0]
    heads = half // HD
    zeros = jnp.zeros((AUG - 3, LAT), F32)
    for side, w in enumerate((wo_own, wo_oth)):
        do = nt(w[...], gb)
        for h in range(heads):
            hh = side * heads + h
            scaled = (do[h * HD:h * HD + HD] * rl_ref[0, hh:hh + 1]).astype(BF)
            doa_ref[0, hh, :HD] = scaled
            delta = -jnp.sum(scaled.astype(F32) * att_ref[0, hh * HD:hh * HD + HD].astype(F32), 0, keepdims=True)
            high = delta.astype(BF).astype(F32)
            low = (delta - high).astype(BF).astype(F32)
            doa_ref[0, hh, HD:] = jnp.concatenate([high, low, delta - high - low, zeros], 0).astype(BF)
    wo_term = nn(att_ref[0], gb)
    sums = jnp.concatenate(
        [jnp.sum(v, 0, keepdims=True) for v in (g * xh, g, gh, cot32)] + [jnp.zeros((4, D), F32)], 0
    )

    @pl.when(pl.program_id(0) == 0)
    def _():
        acc_wo[...] = wo_term
        cols_ref[...] = sums

    @pl.when(pl.program_id(0) > 0)
    def _():
        acc_wo[...] += wo_term
        cols_ref[...] += sums

    @pl.when(pl.program_id(0) == pl.num_programs(0) - 1)
    def _():
        units = acc_up.shape[0]
        put_slabs(grads_ref, 0, acc_up)
        put_slabs(grads_ref, 4 * units, acc_down)
        put_slabs(grads_ref, 8 * units, acc_wo.at[:half])
        put_slabs(wo_oth_ref, 0, acc_wo.at[half:])
        base = 8 * units + 4 * half
        put_row(grads_ref, base, acc_ub, 8)
        grads_ref[base + 8:] = jnp.zeros((grads_ref.shape[0] - base - 8, 128), F32)


def mlp_first(tens, n2, cot, theirs, ub, h1, vecs):
    rows = n2.shape[0]
    scenes = rows // LAT
    units = ub.shape[1]
    rowblock = pl.BlockSpec((LAT, D), lambda i, *_: (i, 0))
    cotblock = pl.BlockSpec((LAT, D), lambda i, tens: (tens[0] * scenes + i, 0))
    return pl.pallas_call(
        mlp_first_kernel,
        grid_spec=pltpu.PrefetchScalarGridSpec(
            num_scalar_prefetch=1,
            grid=(scenes,),
            in_specs=[
                rowblock, cotblock, whole((units, D)), whole((1, units)), whole((units, D), 1), rowblock, vecs_spec(),
            ],
            out_specs=[rowblock, rowblock, whole((8 * units + 16, 128))],
            scratch_shapes=[pltpu.VMEM((units, D), F32), pltpu.VMEM((units, D), F32), pltpu.VMEM((1, units), F32)],
        ),
        out_shape=[
            jax.ShapeDtypeStruct((rows, D), F32),
            jax.ShapeDtypeStruct((rows, D), F32),
            jax.ShapeDtypeStruct((8 * units + 16, 128), BF),
        ],
        compiler_params=params(),
        name="mlp_first",
    )(tens, n2, cot, theirs, ub, theirs, h1, vecs)


def mlp_second(tens, n2, cot, up, ub, down, h1, out_in, back_in, vecs, att, rl, wo_own, theirs, total_rows):
    rows = n2.shape[0]
    scenes = rows // LAT
    units = up.shape[0]
    half = wo_own.shape[0]
    heads = 2 * half // HD
    rowblock = pl.BlockSpec((LAT, D), lambda i, *_: (i, 0))
    cotblock = pl.BlockSpec((LAT, D), lambda i, tens: (tens[0] * scenes + i, 0))
    return pl.pallas_call(
        mlp_second_kernel,
        grid_spec=pltpu.PrefetchScalarGridSpec(
            num_scalar_prefetch=1,
            grid=(scenes,),
            in_specs=[
                rowblock, cotblock, whole((units, D)), whole((1, units)), whole((units, D)), rowblock, rowblock, rowblock,
                vecs_spec(),
                pl.BlockSpec((1, D, LAT), lambda i, *_: (i, 0, 0)),
                pl.BlockSpec((1, heads, LAT), lambda i, *_: (i, 0, 0)),
                whole((half, D)), whole((half, D), 3),
            ],
            out_specs=[
                rowblock, rowblock,
                pl.BlockSpec((1, heads, HD + AUG, LAT), lambda i, *_: (i, 0, 0, 0)),
                whole((total_rows, 128)), whole((4 * half, 128)), whole((8, D)),
            ],
            scratch_shapes=[
                pltpu.VMEM((units, D), F32), pltpu.VMEM((units, D), F32), pltpu.VMEM((1, units), F32),
                pltpu.VMEM((2 * half, D), F32),
            ],
        ),
        out_shape=[
            jax.ShapeDtypeStruct((rows, D), BF),
            jax.ShapeDtypeStruct((rows, D), F32),
            jax.ShapeDtypeStruct((scenes, heads, HD + AUG, LAT), BF),
            jax.ShapeDtypeStruct((total_rows, 128), F32),
            jax.ShapeDtypeStruct((4 * half, 128), BF),
            jax.ShapeDtypeStruct((8, D), F32),
        ],
        compiler_params=params(),
        name="mlp_second",
    )(tens, n2, cot, up, ub, down, h1, out_in, back_in, vecs, att, rl, wo_own, theirs)


def back_head_kernel(tens, p_ref, doa_ref, qkv_ref, n1_ref, *refs):
    dqkv_ref, dw_ref, dw_acc = refs[-3:]
    ones = jnp.ones((AUG, LAT), BF)
    q, k = qkv_ref[0, 0, 0], qkv_ref[0, 0, 1]
    va = jnp.concatenate([qkv_ref[0, 0, 2], ones], 0)
    doa = doa_ref[0, 0]
    p = p_ref[0, 0]
    ds = (p.astype(F32) * tn(va, doa)).astype(BF)
    dqkv_ref[0, 0, 0] = (nn(k, ds) * HD**-0.5).astype(BF)
    dqkv_ref[0, 0, 1] = nt(q, ds).astype(BF)
    dqkv_ref[0, 0, 2] = nt(doa[:HD], p).astype(BF)
    term = nn(dqkv_ref[...].reshape(3 * HD, LAT), n1_ref[...])

    @pl.when(pl.program_id(0) == 0)
    def _():
        dw_acc[...] = term

    @pl.when(pl.program_id(0) > 0)
    def _():
        dw_acc[...] += term

    @pl.when(pl.program_id(0) == pl.num_programs(0) - 1)
    def _():
        put_slabs(dw_ref.at[0], 0, dw_acc)


def back_head(tens, p, doa, qkv, n1, dqkv, dw, side, h):
    scenes, heads = p.shape[0], p.shape[1] // 2
    hh = side * heads + h
    head_at = lambda i, *_: (i, side, 0, h, 0)
    carried = [v for v in (dqkv, dw) if v is not None]
    places = [j for j, v in enumerate((dqkv, dw)) if v is not None]
    return pl.pallas_call(
        back_head_kernel,
        grid_spec=pltpu.PrefetchScalarGridSpec(
            num_scalar_prefetch=1,
            grid=(scenes,),
            in_specs=[
                pl.BlockSpec((1, 1, LAT, LAT), lambda i, *_: (i, hh, 0, 0)),
                pl.BlockSpec((1, 1, HD + AUG, LAT), lambda i, *_: (i, hh, 0, 0)),
                pl.BlockSpec((1, 1, 3, HD, LAT), head_at),
                pl.BlockSpec((LAT, D), lambda i, *_: (i, 0)),
            ] + [pl.BlockSpec(memory_space=pl.ANY)] * len(carried),
            out_specs=[
                pl.BlockSpec((1, 1, 3, HD, LAT), head_at),
                pl.BlockSpec((1, 12 * HD, 128), lambda i, *_: (h, 0, 0)),
            ],
            scratch_shapes=[pltpu.VMEM((3 * HD, D), F32)],
        ),
        out_shape=[
            jax.ShapeDtypeStruct(qkv.shape, BF),
            jax.ShapeDtypeStruct((heads, 12 * HD, 128), BF if side else F32),
        ],
        input_output_aliases={5 + n: j for n, j in enumerate(places)},
        compiler_params=params(),
        name="attention_back",
    )(tens, p, doa, qkv, n1, *carried)


def norm_one_back_kernel(tens, dqkv, wq_own, wq_oth, x_ref, vecs, gh_ref, gl_ref, cols_ref):
    feats = wq_own.shape[0]
    g = tn(dqkv[0, 0].reshape(feats, LAT), wq_own[...]) + tn(dqkv[0, 1].reshape(feats, LAT), wq_oth[...])
    xh, r = normalised(x_ref[...].astype(F32))
    gl_ref[...] = gh_ref[...] + norm_back(g * vecs[0:1], xh, r)
    sums = jnp.concatenate([jnp.sum(v, 0, keepdims=True) for v in (g * xh, g)] + [jnp.zeros((6, D), F32)], 0)

    @pl.when(pl.program_id(0) == 0)
    def _():
        cols_ref[...] = sums

    @pl.when(pl.program_id(0) > 0)
    def _():
        cols_ref[...] += sums


def norm_one_back(tens, dqkv, wq_own, theirs, x, vecs, gh):
    scenes, half = dqkv.shape[0], dqkv.shape[3]
    rowblock = pl.BlockSpec((LAT, D), lambda i, *_: (i, 0))
    return pl.pallas_call(
        norm_one_back_kernel,
        grid_spec=pltpu.PrefetchScalarGridSpec(
            num_scalar_prefetch=1,
            grid=(scenes,),
            in_specs=[
                pl.BlockSpec((1, 2, 3, half, LAT), lambda i, *_: (i, 0, 0, 0, 0)),
                whole((3 * half, D)), whole((3 * half, D)),
                pl.BlockSpec((LAT, D), lambda i, tens: (tens[0] * scenes + i, 0)),
                vecs_spec(),
                rowblock,
            ],
            out_specs=[rowblock, whole((8, D))],
        ),
        out_shape=[jax.ShapeDtypeStruct((scenes * LAT, D), F32), jax.ShapeDtypeStruct((8, D), F32)],
        compiler_params=params(),
        name="norm_one_back",
    )(tens, dqkv, wq_own, theirs, x, vecs, gh)


def tie(value, *after):
    return lax.optimization_barrier((value, *after))[0]


def swap(v):
    return lax.ppermute(v, "tensor", SWAP)


class Cube:
    def __init__(self):
        self.count = lax.axis_size("dp")
        self.steps = self.count.bit_length() - 1
        assert 1 << self.steps == self.count
        first = list(range(self.steps))
        second = [b ^ 1 if b ^ 1 < self.steps else b for b in first]
        self.order = (first, second)
        self.at = lax.axis_index("dp")
        self.core = lax.axis_index("tensor")

    def bit(self, s):
        which = jnp.where(self.core == 0, self.order[0][s], self.order[1][s])
        return (jnp.right_shift(self.at, which) & 1).astype(jnp.int32)

    def exchange(self, v, s):
        pairs = []
        for i in range(self.count):
            for t in range(2):
                pairs.append((i * 2 + t, (i ^ (1 << self.order[t][s])) * 2 + t))
        return lax.ppermute(v, ("dp", "tensor"), pairs)


def small_call(kernel, out_shape, name, scalars, *arrays, scratch=()):
    return pl.pallas_call(
        kernel,
        in_specs=[pl.BlockSpec(memory_space=pltpu.SMEM)] + [pl.BlockSpec(memory_space=pltpu.VMEM)] * len(arrays),
        out_specs=[pl.BlockSpec(memory_space=pltpu.VMEM)] * len(out_shape),
        out_shape=out_shape,
        scratch_shapes=list(scratch),
        compiler_params=pltpu.CompilerParams(vmem_limit_bytes=VMEM_LIMIT),
        name=name,
    )(scalars, *arrays)


def halves(bit, m):
    return pl.ds(pl.multiple_of(bit * m, 16), m), pl.ds(pl.multiple_of((1 - bit) * m, 16), m)


def split_kernel(bits, keep, recv, keep_out, send_out):
    m = keep_out.shape[0]
    mine, other = halves(bits[0], m)
    send_out[...] = (keep[other] + recv[other].astype(F32)).astype(BF)
    keep_out[...] = keep[mine] + recv[mine].astype(F32)


def split(keep, recv, bits):
    m = keep.shape[0] // 2
    return small_call(
        split_kernel, [jax.ShapeDtypeStruct((m, 128), F32), jax.ShapeDtypeStruct((m, 128), BF)], "split", bits, keep, recv
    )


def settle_kernel(bits, keep, recv, out):
    out[...] = (keep[...] + recv[...].astype(F32)).astype(BF)


def settle(keep, recv, bits):
    return small_call(settle_kernel, [jax.ShapeDtypeStruct(keep.shape, BF)], "settle", bits, keep, recv)[0]


def join_kernel(bits, own, recv, out):
    mine, other = halves(bits[0], own.shape[0])
    out[mine] = own[...]
    out[other] = recv[...]


def join(own, recv, bits):
    return small_call(
        join_kernel, [jax.ShapeDtypeStruct((2 * own.shape[0], 128), BF)], "join", bits, own, recv
    )[0]


def split_mlp_kernel(bits, own, recv, recv_wo, keep_out, send_out, full):
    big, wo = recv.shape[0] - 16, recv_wo.shape[0]
    ub = big // 1024
    full[...] = own[...]
    full[:big] += recv[:big].astype(F32)
    full[big:big + wo] += recv_wo[...].astype(F32)
    full[big + wo:big + wo + ub] += recv[big:big + ub].astype(F32)
    m = keep_out.shape[0]
    mine, other = halves(bits[0], m)
    send_out[...] = full[other].astype(BF)
    keep_out[...] = full[mine]


def split_mlp(own, recv, recv_wo, bits):
    m = own.shape[0] // 2
    return small_call(
        split_mlp_kernel, [jax.ShapeDtypeStruct((m, 128), F32), jax.ShapeDtypeStruct((m, 128), BF)], "split_mlp",
        bits, own, recv, recv_wo, scratch=[pltpu.VMEM(own.shape, F32)],
    )


def finish_mlp_kernel(bits, own, recv, dup, ddown, dwo, dub, full):
    mine, other = halves(bits[0], own.shape[0])
    full[mine] = own[...]
    full[other] = recv[...]
    units, half = dup.shape[0], dwo.shape[0]
    for c in range(D // 128):
        at = slice(c * 128, c * 128 + 128)
        dup[:, at] = full[c * units:(c + 1) * units].astype(F32)
        ddown[:, at] = full[(4 + c) * units:(5 + c) * units].astype(F32)
        dwo[:, at] = full[8 * units + c * half:8 * units + (c + 1) * half].astype(F32)
    base = 8 * units + 4 * half
    dub[...] = full[base:base + dub.shape[0]].astype(F32)


def finish_mlp(own, recv, bits, units, half):
    return small_call(
        finish_mlp_kernel,
        [
            jax.ShapeDtypeStruct((units, D), F32), jax.ShapeDtypeStruct((units, D), F32),
            jax.ShapeDtypeStruct((half, D), F32), jax.ShapeDtypeStruct((units // 128, 128), F32),
        ],
        "finish_mlp", bits, own, recv, scratch=[pltpu.VMEM((2 * own.shape[0], 128), BF)],
    )


def finish_qkv_kernel(bits, own, recv, out, full):
    mine, other = halves(bits[0], own.shape[0])
    full[mine] = own[...]
    full[other] = recv[...]
    for h in range(out.shape[1] // HD):
        for c in range(D // 128):
            for t in range(3):
                row = h * 12 * HD + c * 3 * HD + t * HD
                out[t, h * HD:h * HD + HD, c * 128:c * 128 + 128] = full[row:row + HD].astype(F32)


def finish_qkv(own, recv, bits, half):
    return small_call(
        finish_qkv_kernel, [jax.ShapeDtypeStruct((3, half, D), F32)], "finish_qkv", bits, own, recv,
        scratch=[pltpu.VMEM((2 * own.shape[0], 128), BF)],
    )[0]


def body(
    latents, scene_len, attn_gain, attn_shift, qkv_weight, out_weight, out_bias, mlp_gain, mlp_shift,
    up_weight, up_bias, down_weight, down_bias, cotangent,
):
    rows = latents.shape[0] // lax.axis_size("tensor")
    units, half = up_weight.shape[0], out_weight.shape[0]
    heads = half // HD
    tens = lax.axis_index("tensor").astype(jnp.int32).reshape(1)
    cube = Cube()
    bits = [cube.bit(s).reshape(1) for s in range(cube.steps)]

    ours = jnp.concatenate([qkv_weight.reshape(3 * half, D), out_weight], 0)
    theirs = swap(ours)
    wq_oth, wo_oth = theirs, theirs
    vecs = jnp.stack([attn_gain, attn_shift, out_bias, mlp_gain, mlp_shift, down_bias]).astype(F32)
    ours_mlp = jnp.concatenate([up_weight, down_weight, jnp.pad(up_bias.reshape(units // D, D), ((0, 16 - units // D), (0, 0)))], 0)
    theirs_mlp = swap(ours_mlp)

    n1, qkv, p, att, rl, h1, n2 = attention_forward(
        tens, scene_len, latents, vecs, qkv_weight.reshape(3 * half, D), theirs, out_weight, rows
    )
    ub_oth = theirs_mlp[2 * units:2 * units + units // D].reshape(1, units)
    out_part, back_part, grads_oth = mlp_first(tens, n2, cotangent, theirs_mlp, ub_oth, h1, vecs)
    from_peer = swap(grads_oth)
    count = cube.count
    need = 8 * units + 4 * half + units // 128
    total_rows = -(-need // (16 * count)) * 16 * count
    block_out, gh, doa, grads_own, wo_oth_grad, cols_two = mlp_second(
        tens, n2, cotangent, up_weight, up_bias.reshape(1, units), down_weight, h1, out_part, back_part, vecs, att, rl,
        out_weight, theirs, total_rows,
    )
    keep, send = split_mlp(grads_own, from_peer, swap(wo_oth_grad), bits[0])

    queue = []
    state = {"keep": keep, "send": send, "recv": None}

    def reduce_steps(keep, send):
        for s in range(cube.steps):
            recv = cube.exchange(send, s)
            token = yield send
            recv = tie(recv, token)
            if s + 1 < cube.steps:
                keep, send = split(keep, recv, bits[s + 1])
            else:
                have = settle(keep, recv, bits[s])
        for s in range(cube.steps - 1, -1, -1):
            recv = cube.exchange(have, s)
            token = yield have
            recv = tie(recv, token)
            if s:
                have = join(have, recv, bits[s])
        return have, recv

    def advance(steps, token):
        try:
            return steps.send(token), None
        except StopIteration as end:
            return None, end.value

    mlp_steps = reduce_steps(keep, send)
    token = next(mlp_steps)
    mlp_result = None
    dqkv, dw_oth, dw_own = None, None, None
    calls = 0
    for side in (1, 0):
        for h in range(heads):
            dw = dw_oth if side else dw_own
            dqkv, dw = back_head(tie(tens, token), p, doa, qkv, n1, dqkv, dw, side, h)
            if side:
                dw_oth = dw
            else:
                dw_own = dw
            calls += 1
            if mlp_result is None and calls != 1:
                token, mlp_result = advance(mlp_steps, dw)
                if mlp_result is not None:
                    token = dw
            else:
                token = dw
        if side:
            qkv_peer = swap(dw_oth.reshape(heads * 12 * HD, 128))
    keep, send = split(tie(dw_own.reshape(heads * 12 * HD, 128), token), qkv_peer, bits[0])
    qkv_steps = reduce_steps(keep, send)
    token = next(qkv_steps)
    grad_latents, cols_one = norm_one_back(tie(tens, token), dqkv, qkv_weight.reshape(3 * half, D), theirs, latents, vecs, gh)
    cols = jnp.concatenate([cols_one[:2], cols_two[:4]], 0).reshape(24, 128)
    qkv_result = None
    token = cols
    todo = [lambda v: swap(v)] + [lambda v, s=s: cube.exchange(v, s) for s in range(cube.steps)]
    while qkv_result is None:
        _, qkv_result = advance(qkv_steps, token)
        if todo:
            cols = cols + todo.pop(0)(cols)
            token = cols
        if mlp_result is None:
            token, mlp_result = advance(mlp_steps, token)
            token = cols
    while todo:
        cols = cols + todo.pop(0)(cols)
    while mlp_result is None:
        _, mlp_result = advance(mlp_steps, cols)
    dup, ddown, dwo, dub = finish_mlp(*mlp_result, bits[0], units, half)
    dwq = finish_qkv(*qkv_result, bits[0], half)
    shared = cols.reshape(6, D)
    return (
        block_out, grad_latents, shared[0], shared[1], dwq, dwo, shared[4],
        shared[2], shared[3], dup, dub.reshape(units), ddown, shared[5],
    )


def solution(mesh):
    placed = (
        P("dp", None), P("dp"), P(), P(), P(None, "tensor", None), P("tensor", None), P(), P(), P(),
        P("tensor", None), P("tensor"), P("tensor", None), P(), P("dp", None),
    )
    return jax.shard_map(
        body,
        mesh=mesh,
        in_specs=placed,
        out_specs=(
            P(("dp", "tensor"), None), P(("dp", "tensor"), None), P(), P(), P(None, "tensor", None),
            P("tensor", None), P(), P(), P(), P("tensor", None), P("tensor"), P("tensor", None), P(),
        ),
        check_vma=False,
    )
```

```python
import functools

import jax
import jax.numpy as jnp
from jax import lax
from jax.experimental import pallas as pl
from jax.experimental.pallas import tpu as pltpu
from jax.sharding import PartitionSpec as P

D = 512
HD = 64
LAT = 512
AUG = 16
EPS = 1e-05
NEG = -1e30
BF = jnp.bfloat16
F32 = jnp.float32
MIB = 2**20
SWAP = [(0, 1), (1, 0)]
GO_ON = (1, 2, 3)
BACK_SCENES = 2


def _dot(a, b, ca, cb):
    return lax.dot_general(a, b, (((ca,), (cb,)), ((), ())), preferred_element_type=F32)


def hbm(*values):
    return tuple(pltpu.with_memory_space_constraint(v, pltpu.HBM) for v in values)


def nn(a, b):
    return _dot(a, b, 1, 0)


def nt(a, b):
    return _dot(a, b, 1, 1)


def tn(a, b):
    return _dot(a, b, 0, 0)


def normalised(v):
    c = v - jnp.mean(v, -1, keepdims=True)
    r = lax.rsqrt(jnp.mean(c * c, -1, keepdims=True) + EPS)
    return c * r, r


def norm_back(e, xh, r):
    return r * (e - jnp.mean(e, -1, keepdims=True) - xh * jnp.mean(e * xh, -1, keepdims=True))


def forward_kernel(
    tens, lens, x_ref, vecs, wq_own, wq_oth, wo_own, wo_oth,
    n1_ref, qkv_ref, p_ref, att_ref, rl_ref, h1_ref, n2_ref,
):
    scenes = pl.num_programs(0)
    length = lens[tens[0] * scenes + pl.program_id(0)]
    x = x_ref[...].astype(F32)
    n1 = (normalised(x)[0] * vec(vecs, 0) + vec(vecs, 1)).astype(BF)
    n1_ref[...] = n1
    half = wo_own.shape[0]
    heads = half // HD

    def project(side, t):
        part = nt((wq_own, wq_oth)[side][t * half:(t + 1) * half], n1)
        if t == 0:
            part = part * HD**-0.5
        qkv_ref[0, side, t] = part.astype(BF)

    key_at = lax.broadcasted_iota(jnp.int32, (AUG, LAT), 1)
    row_at = lax.broadcasted_iota(jnp.int32, (AUG, LAT), 0)
    bias = jnp.where((key_at >= length) & (row_at == 0), NEG, 0.0).astype(BF)
    ones = jnp.ones((AUG, LAT), BF)

    def part_of(t, h):
        return qkv_ref[0, h // heads, t, h % heads * HD:h % heads * HD + HD]

    def scores(h):
        return tn(jnp.concatenate([part_of(1, h), bias], 0), jnp.concatenate([part_of(0, h), ones], 0))

    def weights(h, s):
        p = jnp.exp(s - jnp.max(s, 0, keepdims=True)).astype(BF)
        p_ref[0, h] = p
        return p

    def attend(h, p):
        o = nn(jnp.concatenate([part_of(2, h), ones], 0), p)
        rl = 1.0 / o[HD:HD + 1]
        rl_ref[0, h:h + 1] = rl
        att_ref[0, h * HD:h * HD + HD] = (o[:HD] * rl).astype(BF)

    for t in (1, 0, 2):
        project(0, t)
    scored, weighed = [], []
    total = None
    for h in range(2 * heads + 2):
        if h < 2 * heads:
            scored.append(scores(h))
        if h in (1, 2, 3):
            project(1, (1, 0, 2)[h - 1])
        if h >= 2:
            attend(h - 2, weighed.pop(0))
        if 1 <= h <= 2 * heads:
            weighed.append(weights(h - 1, scored.pop(0)))
        if h == heads + 2:
            total = tn(att_ref[0, :half], wo_own[...])
    h1 = x + (total + tn(att_ref[0, half:], wo_oth[...])) + vec(vecs, 2)
    h1_ref[...] = h1
    n2_ref[...] = (normalised(h1)[0] * vec(vecs, 3) + vec(vecs, 4)).astype(BF)


def whole(shape, row=0):
    at = (row,) + (0,) * (len(shape) - 1)
    return pl.BlockSpec(shape, lambda i, *_: at, pipeline_mode=pl.Buffered(1))


def params(mib):
    return pltpu.CompilerParams(vmem_limit_bytes=mib * MIB, dimension_semantics=("arbitrary",))


def vec(vecs, i):
    return vecs[i:i + 1].astype(F32)


def vecs_spec(row=0):
    return whole((16, D), row)


def attention_forward(tens, lens, x, vecs, wq_own, theirs, wo_own, rows):
    scenes = rows // LAT
    rowblock = pl.BlockSpec((LAT, D), lambda i, *_: (i, 0))
    half = wo_own.shape[0]
    return pl.pallas_call(
        forward_kernel,
        grid_spec=pltpu.PrefetchScalarGridSpec(
            num_scalar_prefetch=2,
            grid=(scenes,),
            in_specs=[
                pl.BlockSpec((LAT, D), lambda i, tens, lens: (tens[0] * scenes + i, 0)),
                vecs_spec(), whole((3 * half, D)), whole((3 * half, D)), whole((half, D)), whole((half, D), 3),
            ],
            out_specs=[
                rowblock,
                pl.BlockSpec((1, 2, 3, half, LAT), lambda i, *_: (i, 0, 0, 0, 0)),
                pl.BlockSpec((1, 2 * half // HD, LAT, LAT), lambda i, *_: (i, 0, 0, 0)),
                pl.BlockSpec((1, D, LAT), lambda i, *_: (i, 0, 0)),
                pl.BlockSpec((1, 2 * half // HD, LAT), lambda i, *_: (i, 0, 0)),
                rowblock,
                rowblock,
            ],
        ),
        out_shape=[
            pltpu.HBM((rows, D), BF),
            pltpu.HBM((scenes, 2, 3, half, LAT), BF),
            pltpu.HBM((scenes, 2 * half // HD, LAT, LAT), BF),
            pltpu.HBM((scenes, D, LAT), BF),
            pltpu.HBM((scenes, 2 * half // HD, LAT), F32),
            pltpu.HBM((rows, D), F32),
            pltpu.HBM((rows, D), BF),
        ],
        compiler_params=params(40),
        name="attention_forward",
    )(tens, lens, *hbm(x, vecs, wq_own, theirs, wo_own, theirs))


LOG2E = 1.4426950408889634
SUB = 256


def gelu_parts(z):
    cdf = 0.5 + 0.5 * lax.erf(z * 0.7071067811865476)
    return z * cdf, cdf + z * (0.3989422804014327 * jnp.exp2(z * z * (-0.5 * LOG2E)))


def put_slabs(out, at, values):
    n = values.shape[0]
    for c in range(D // 128):
        out[at + c * n:at + (c + 1) * n] = values[:, c * 128:c * 128 + 128].astype(out.dtype)


def put_row(out, at, row, count):
    parts = [row[:, c * 128:c * 128 + 128] for c in range(row.shape[1] // 128)]
    parts += [jnp.zeros((1, 128), F32)] * (count - len(parts))
    out[at:at + count] = jnp.concatenate(parts, 0).astype(out.dtype)


def mlp_kernel(
    tens, n2_ref, cot_ref, up_own, down_own, up_oth, down_oth, vecs_oth, vecs, h1_ref, att_ref, rl_ref, wo_own, wo_oth,
    block_ref, gh_ref, doa_ref, own_ref, oth_ref, cols_ref, acc_up, acc_down, acc_ub, acc_wo,
):
    @pl.when(pl.program_id(0) == 0)
    def _():
        acc_up[...] = jnp.zeros_like(acc_up)
        acc_down[...] = jnp.zeros_like(acc_down)
        acc_ub[...] = jnp.zeros_like(acc_ub)
        acc_wo[...] = jnp.zeros_like(acc_wo)
        cols_ref[...] = jnp.zeros_like(cols_ref)

    n2, cot = n2_ref[...], cot_ref[...]
    units = up_own.shape[0]
    per = units // SUB

    def place(j):
        side, at = divmod(j, per)
        ups, downs, rows = ((up_own, down_own, vecs), (up_oth, down_oth, vecs_oth))[side]
        at = slice(at * SUB, at * SUB + SUB)
        first = at.start // D
        return ups[at], downs[at], vec(rows, 6 + first)[:, at.start - first * D:at.stop - first * D]

    def before(j):
        u, d, b = place(j)
        return nt(n2, u) + b, nt(cot, d)

    def between(pre, grad_act):
        act, slope = gelu_parts(pre)
        return act.astype(BF), (grad_act * slope).astype(BF)

    def after(j, act, dpre):
        u, d, _ = place(j)
        at = slice(j * SUB, j * SUB + SUB)
        acc_down[at] += tn(act, cot)
        acc_up[at] += tn(dpre, n2)
        acc_ub[:, at] += jnp.sum(dpre.astype(F32), 0, keepdims=True)
        return nn(act, d), nn(dpre, u)

    out, back = 0.0, 0.0
    first, second = [], []
    for j in range(2 * per + 2):
        if j < 2 * per:
            first.append(before(j))
        if j >= 2:
            o, b = after(j - 2, *second.pop(0))
            out, back = out + o, back + b
        if 1 <= j <= 2 * per:
            second.append(between(*first.pop(0)))
    h1 = h1_ref[...]
    block_ref[...] = (h1 + out + vec(vecs, 5)).astype(BF)
    xh, r = normalised(h1)
    cot32 = cot.astype(F32)
    gh = cot32 + norm_back(back * vec(vecs, 3), xh, r)
    gh_ref[...] = gh
    gb = gh.astype(BF)
    half = wo_own.shape[0]
    heads = half // HD
    zeros = jnp.zeros((AUG - 3, LAT), F32)
    for side, w in enumerate((wo_own, wo_oth)):
        do = nt(w[...], gb)
        for h in range(heads):
            hh = side * heads + h
            scaled = (do[h * HD:h * HD + HD] * rl_ref[0, hh:hh + 1]).astype(BF)
            doa_ref[0, hh, :HD] = scaled
            delta = -jnp.sum(scaled.astype(F32) * att_ref[0, hh * HD:hh * HD + HD].astype(F32), 0, keepdims=True)
            high = delta.astype(BF).astype(F32)
            low = (delta - high).astype(BF).astype(F32)
            doa_ref[0, hh, HD:] = jnp.concatenate([high, low, delta - high - low, zeros], 0).astype(BF)
    acc_wo[...] += nn(att_ref[0], gb)
    cols_ref[...] += jnp.concatenate(
        [jnp.sum(v, 0, keepdims=True) for v in (back * xh, back, gh, cot32)] + [jnp.zeros((4, D), F32)], 0
    )

    @pl.when(pl.program_id(0) == pl.num_programs(0) - 1)
    def _():
        base = 8 * units + 4 * half
        for side, ref in enumerate((own_ref, oth_ref)):
            put_slabs(ref, 0, acc_up.at[side * units:(side + 1) * units])
            put_slabs(ref, 4 * units, acc_down.at[side * units:(side + 1) * units])
            put_slabs(ref, 8 * units, acc_wo.at[side * half:(side + 1) * half])
            put_row(ref, base, acc_ub[:, side * units:(side + 1) * units], 16)
            if ref.shape[0] > base + 16:
                ref[base + 16:] = jnp.zeros((ref.shape[0] - base - 16, 128), ref.dtype)


def mlp(tens, n2, cot, up, down, up_oth, down_oth, theirs, vecs, h1, att, rl, wo, total_rows):
    rows = n2.shape[0]
    scenes = rows // LAT
    units, half = up.shape[0], wo.shape[0]
    heads = 2 * half // HD
    rowblock = pl.BlockSpec((LAT, D), lambda i, *_: (i, 0))
    weights = whole((units, D))
    return pl.pallas_call(
        mlp_kernel,
        grid_spec=pltpu.PrefetchScalarGridSpec(
            num_scalar_prefetch=1,
            grid=(scenes,),
            in_specs=[
                rowblock,
                pl.BlockSpec((LAT, D), lambda i, tens: (tens[0] * scenes + i, 0)),
                weights, weights, weights, weights, vecs_spec(theirs.shape[0] // 16 - 1), vecs_spec(), rowblock,
                pl.BlockSpec((1, D, LAT), lambda i, *_: (i, 0, 0)),
                pl.BlockSpec((1, heads, LAT), lambda i, *_: (i, 0, 0)),
                whole((half, D)), whole((half, D), 3),
            ],
            out_specs=[
                rowblock, rowblock,
                pl.BlockSpec((1, heads, HD + AUG, LAT), lambda i, *_: (i, 0, 0, 0)),
                whole((total_rows, 128)), whole((total_rows, 128)), whole((8, D)),
            ],
            scratch_shapes=[
                pltpu.VMEM((2 * units, D), F32), pltpu.VMEM((2 * units, D), F32), pltpu.VMEM((1, 2 * units), F32),
                pltpu.VMEM((2 * half, D), F32),
            ],
        ),
        out_shape=[
            pltpu.HBM((rows, D), BF),
            pltpu.HBM((rows, D), F32),
            pltpu.HBM((scenes, heads, HD + AUG, LAT), BF),
            pltpu.HBM((total_rows, 128), BF),
            pltpu.HBM((total_rows, 128), BF),
            pltpu.HBM((8, D), F32),
        ],
        compiler_params=params(56),
        name="mlp",
    )(tens, *hbm(n2, cot, up, down, up_oth, down_oth, theirs, vecs, h1, att, rl, wo, theirs))


def back_kernel(tens, p_ref, doa_ref, qkv_ref, n1_ref, *refs, ends):
    starts, stops = ends
    dqkv_ref, dw_ref, acc = refs[-3:]
    groups = acc.shape[0]
    ones = jnp.ones((AUG, LAT), BF)
    count = p_ref.shape[1]

    @pl.when((pl.program_id(0) == 0) & (pl.program_id(1) == 0))
    def _():
        if starts:
            acc[...] = jnp.zeros_like(acc)
        else:
            acc[...] = refs[0][...]

    def part_of(t, h):
        return qkv_ref[0, 0, t, h * HD:h * HD + HD]

    def first(h):
        return tn(jnp.concatenate([part_of(2, h), ones], 0), doa_ref[0, h])

    def second(h, grad):
        return (p_ref[0, h].astype(F32) * grad).astype(BF)

    def third(h, ds):
        at = slice(h * HD, h * HD + HD)
        dqkv_ref[0, 0, 0, at] = (nn(part_of(1, h), ds) * HD**-0.5).astype(BF)
        dqkv_ref[0, 0, 1, at] = nt(part_of(0, h), ds).astype(BF)

    def values(h):
        dqkv_ref[0, 0, 2, h * HD:h * HD + HD] = nt(doa_ref[0, h, :HD], p_ref[0, h]).astype(BF)

    grads, scores = [], []
    for h in range(count + 1):
        if h < count:
            grads.append(first(h))
            values(h)
        if h >= 1:
            third(h - 1, scores.pop(0))
        if h < count:
            scores.append(second(h, grads.pop(0)))
    feats = count * HD
    group = pl.program_id(1)
    term = nn(dqkv_ref[0, 0].reshape(3 * feats, LAT), n1_ref[...])
    acc[group] += term.reshape(3, feats, D)

    @pl.when((pl.program_id(0) == pl.num_programs(0) - 1) & (pl.program_id(1) == groups - 1))
    def _():
        if not stops:
            dw_ref[...] = acc[...]
            return
        for c in range(D // 128):
            for t in range(3):
                for g in range(groups):
                    row = ((c * 3 + t) * groups + g) * feats
                    dw_ref[row:row + feats] = acc[g, t, :, c * 128:c * 128 + 128].astype(dw_ref.dtype)
        used = 12 * groups * feats
        if used < dw_ref.shape[0]:
            dw_ref[used:] = jnp.zeros((dw_ref.shape[0] - used, 128), dw_ref.dtype)


BACK_HEADS = 2


def attention_back(tens, p, doa, qkv, n1, dqkv, partial, side, first, count, total_rows):
    scenes, heads = p.shape[0], p.shape[1] // 2
    steps = heads // BACK_HEADS
    feats = BACK_HEADS * HD
    block = lambda i, j, *_: (first + i, side, 0, j, 0)
    head_block = lambda i, j, *_: (first + i, side * steps + j, 0, 0)
    ends = (first == 0, first + count == scenes)
    sums = (steps, 3, feats, D)
    zeros = lambda i, j, *_: (0, 0, 0, 0)
    carried, specs, aliases = [], [], {}
    if not ends[0]:
        carried.append(partial)
        specs.append(pl.BlockSpec(sums, zeros, pipeline_mode=pl.Buffered(1)))
    if dqkv is not None:
        aliases = {5 + len(carried): 0}
        carried.append(dqkv)
        specs.append(pl.BlockSpec(memory_space=pl.ANY))
    if ends[1]:
        dw = jax.ShapeDtypeStruct((total_rows, 128), BF if side else F32)
        dw_spec = pl.BlockSpec((total_rows, 128), lambda i, j, *_: (0, 0), pipeline_mode=pl.Buffered(1))
    else:
        dw = pltpu.HBM(sums, F32)
        dw_spec = pl.BlockSpec(sums, zeros, pipeline_mode=pl.Buffered(1))
    return pl.pallas_call(
        functools.partial(back_kernel, ends=ends),
        grid_spec=pltpu.PrefetchScalarGridSpec(
            num_scalar_prefetch=1,
            grid=(count, steps),
            in_specs=[
                pl.BlockSpec((1, BACK_HEADS, LAT, LAT), head_block),
                pl.BlockSpec((1, BACK_HEADS, HD + AUG, LAT), head_block),
                pl.BlockSpec((1, 1, 3, feats, LAT), block),
                pl.BlockSpec((LAT, D), lambda i, j, *_: (first + i, 0)),
            ] + specs,
            out_specs=[pl.BlockSpec((1, 1, 3, feats, LAT), block), dw_spec],
            scratch_shapes=[pltpu.VMEM(sums, F32)],
        ),
        out_shape=[pltpu.HBM(qkv.shape, BF), dw],
        input_output_aliases=aliases,
        compiler_params=pltpu.CompilerParams(vmem_limit_bytes=24 * MIB, dimension_semantics=("arbitrary", "arbitrary")),
        name="attention_back",
    )(tens, *hbm(p, doa, qkv, n1, *carried))


def norm_one_back_kernel(tens, dqkv, wq_own, wq_oth, x_ref, vecs, gh_ref, gl_ref, cols_ref):
    feats = wq_own.shape[0]
    g = tn(dqkv[0, 0].reshape(feats, LAT), wq_own[...]) + tn(dqkv[0, 1].reshape(feats, LAT), wq_oth[...])
    xh, r = normalised(x_ref[...].astype(F32))
    gl_ref[...] = gh_ref[...] + norm_back(g * vec(vecs, 0), xh, r)
    sums = jnp.concatenate([jnp.sum(v, 0, keepdims=True) for v in (g * xh, g)] + [jnp.zeros((6, D), F32)], 0)

    @pl.when(pl.program_id(0) == 0)
    def _():
        cols_ref[...] = sums

    @pl.when(pl.program_id(0) > 0)
    def _():
        cols_ref[...] += sums


def norm_one_back(tens, dqkv, wq_own, theirs, x, vecs, gh):
    scenes, half = dqkv.shape[0], dqkv.shape[3]
    rowblock = pl.BlockSpec((LAT, D), lambda i, *_: (i, 0))
    return pl.pallas_call(
        norm_one_back_kernel,
        grid_spec=pltpu.PrefetchScalarGridSpec(
            num_scalar_prefetch=1,
            grid=(scenes,),
            in_specs=[
                pl.BlockSpec((1, 2, 3, half, LAT), lambda i, *_: (i, 0, 0, 0, 0)),
                whole((3 * half, D)), whole((3 * half, D)),
                pl.BlockSpec((LAT, D), lambda i, tens: (tens[0] * scenes + i, 0)),
                vecs_spec(),
                rowblock,
            ],
            out_specs=[rowblock, whole((8, D))],
        ),
        out_shape=[pltpu.HBM((scenes * LAT, D), F32), pltpu.HBM((8, D), F32)],
        compiler_params=params(28),
        name="norm_one_back",
    )(tens, *hbm(dqkv), wq_own, theirs, *hbm(x), vecs, *hbm(gh))


def tie(value, *after):
    return lax.optimization_barrier((value, *after))[0]


def swap(v):
    return lax.ppermute(v, "tensor", SWAP)


class Stage:
    def __init__(self, count, bits, distances=None):
        self.count, self.bits = count, bits
        self.size = 1 << len(bits[0])
        each = list(range(1, self.size))
        self.distances = distances or (each, each)
        at = lax.axis_index("dp")
        core = lax.axis_index("tensor")

        def value(t, v):
            return sum((jnp.right_shift(v, b) & 1) << k for k, b in enumerate(bits[t]))

        self.place = jnp.where(core == 0, value(0, at), value(1, at)).astype(jnp.int32)
        met = [jnp.where(core == 0, self.distances[0][k], self.distances[1][k]) ^ self.place for k in range(self.size - 1)]
        self.scalars = jnp.stack([self.place] + met).astype(jnp.int32)

    def exchange(self, values):
        out = []
        for k, v in enumerate(values):
            pairs = []
            for i in range(self.count):
                for t in range(2):
                    d = self.distances[t][k]
                    flip = sum(((d >> j) & 1) << b for j, b in enumerate(self.bits[t]))
                    pairs.append((i * 2 + t, (i ^ flip) * 2 + t))
            out.append(lax.ppermute(v, ("dp", "tensor"), pairs))
        return out


def small_call(kernel, out_shape, name, scalars, *arrays, scratch=(), mib=16):
    return pl.pallas_call(
        kernel,
        in_specs=[pl.BlockSpec(memory_space=pltpu.SMEM)] + [pl.BlockSpec(memory_space=pltpu.VMEM)] * len(arrays),
        out_specs=[pl.BlockSpec(memory_space=pltpu.VMEM)] * len(out_shape),
        out_shape=out_shape,
        scratch_shapes=list(scratch),
        compiler_params=pltpu.CompilerParams(vmem_limit_bytes=mib * MIB),
        name=name,
    )(scalars, *arrays)


def pack_kernel(*refs):
    (*rows, up_bias, wq, wo), (packed, vecs), scratch = refs[:9], refs[9:11], refs[11:]
    *held, whole_sem, sem = scratch
    first = wq.shape[0]
    everything = held[-1]
    last = everything.shape[0] - 16
    big = [
        pltpu.make_async_copy(wq, everything.at[pl.ds(0, first)], sem.at[0]),
        pltpu.make_async_copy(wo, everything.at[pl.ds(first, last - first)], sem.at[1]),
    ]
    small = [pltpu.make_async_copy(r, h, sem.at[2 + k]) for k, (r, h) in enumerate(zip((*rows, up_bias), held))]
    for c in big + small:
        c.start()
    for c in small:
        c.wait()
    parts = [h[...].astype(F32).reshape(1, D) for h in held[:-2]]
    bias = held[-2][...].astype(F32)
    parts += [bias[i:i + D].reshape(1, D) for i in range(0, bias.shape[0], D)]
    everything[last:] = jnp.concatenate(parts + [jnp.zeros((16 - len(parts), D), F32)], 0).astype(BF)
    for c in big:
        c.wait()
    out = [
        pltpu.make_async_copy(everything, packed, whole_sem.at[0]),
        pltpu.make_async_copy(everything.at[pl.ds(last, 16)], vecs, whole_sem.at[1]),
    ]
    for c in out:
        c.start()
    for c in out:
        c.wait()


def pack(rows, up_bias, wq, wo):
    shape = (wq.shape[0] + wo.shape[0] + 16, D)
    return pl.pallas_call(
        pack_kernel,
        in_specs=[pl.BlockSpec(memory_space=pl.ANY)] * 9,
        out_specs=[pl.BlockSpec(memory_space=pl.ANY)] * 2,
        out_shape=[pltpu.HBM(shape, BF), pltpu.HBM((16, D), BF)],
        scratch_shapes=[pltpu.VMEM((D,), BF)] * 6 + [
            pltpu.VMEM(up_bias.shape, BF), pltpu.VMEM(shape, BF), pltpu.SemaphoreType.DMA((2,)),
            pltpu.SemaphoreType.DMA((9,)),
        ],
        compiler_params=pltpu.CompilerParams(vmem_limit_bytes=16 * MIB),
        name="pack",
    )(*hbm(*rows, up_bias, wq, wo))


def chunk(place, m):
    return pl.ds(pl.multiple_of(place * m, 16), m)


def hand_out(total, scalars, keep_out, sends):
    m = keep_out.shape[0]
    keep_out[...] = total[chunk(scalars[0], m)]
    for k, out in enumerate(sends):
        out[...] = total[chunk(scalars[1 + k], m)].astype(BF)


def split_kernel(scalars, *refs, count):
    (keep, *recvs), (keep_out, *sends), total = refs[:count], refs[count:-1], refs[-1]
    v = keep[...]
    for r in recvs:
        v = v + r[...].astype(F32)
    total[...] = v
    hand_out(total, scalars, keep_out, sends)


def pieces(stage, rows):
    m = rows // stage.size
    return [jax.ShapeDtypeStruct((m, 128), F32)] + [jax.ShapeDtypeStruct((m, 128), BF)] * (stage.size - 1)


def split(keep, recvs, stage):
    keep, *sends = small_call(
        functools.partial(split_kernel, count=1 + len(recvs)), pieces(stage, keep.shape[0]), "split", stage.scalars, keep,
        *recvs, scratch=[pltpu.VMEM(keep.shape, F32)],
    )
    return keep, sends


def settle_kernel(scalars, keep, *refs):
    v = keep[...]
    for r in refs[:-1]:
        v = v + r[...].astype(F32)
    refs[-1][...] = v.astype(BF)


def settle(keep, recvs, stage):
    return small_call(settle_kernel, [jax.ShapeDtypeStruct(keep.shape, BF)], "settle", stage.scalars, keep, *recvs)[0]


def fill(full, scalars, own, recvs):
    m = full.shape[0] // (1 + len(recvs))
    full[chunk(scalars[0], m)] = own[:m]
    for k, r in enumerate(recvs):
        full[chunk(scalars[1 + k], m)] = r[:m]


def join_kernel(scalars, own, *refs):
    fill(refs[-1], scalars, own, refs[:-1])


def join(own, recvs, stage):
    return small_call(
        join_kernel, [jax.ShapeDtypeStruct((stage.size * own.shape[0], 128), BF)], "join", stage.scalars, own, *recvs
    )[0]


def split_mlp_kernel(scalars, own, recv, keep_out, *sends):
    m = keep_out.shape[0]
    at = chunk(scalars[0], m)
    keep_out[...] = own[at].astype(F32) + recv[at].astype(F32)
    for k, out in enumerate(sends):
        at = chunk(scalars[1 + k], m)
        out[...] = (own[at].astype(F32) + recv[at].astype(F32)).astype(BF)


def split_mlp(own, recv, stage):
    keep, *sends = small_call(
        split_mlp_kernel, pieces(stage, own.shape[0]), "split_mlp", stage.scalars, *hbm(own), recv, mib=24,
    )
    return keep, sends


def finish_mlp_kernel(scalars, *refs):
    (own, *recvs), (dup, ddown, dwo, dub), full = refs[:-5], refs[-5:-1], refs[-1]
    fill(full, scalars, own, recvs)
    units, half = dup.shape[0], dwo.shape[0]
    for c in range(D // 128):
        at = slice(c * 128, c * 128 + 128)
        dup[:, at] = full[c * units:(c + 1) * units].astype(F32)
        ddown[:, at] = full[(4 + c) * units:(5 + c) * units].astype(F32)
        dwo[:, at] = full[8 * units + c * half:8 * units + (c + 1) * half].astype(F32)
    base = 8 * units + 4 * half
    dub[...] = full[base:base + dub.shape[0]].astype(F32)


def finish_mlp(own, recvs, stage, units, half):
    return small_call(
        finish_mlp_kernel,
        [
            jax.ShapeDtypeStruct((units, D), F32), jax.ShapeDtypeStruct((units, D), F32),
            jax.ShapeDtypeStruct((half, D), F32), jax.ShapeDtypeStruct((units // 128, 128), F32),
        ],
        "finish_mlp", stage.scalars, own, *recvs, scratch=[pltpu.VMEM((stage.size * own.shape[0], 128), BF)],
    )


def parts_of(v):
    high = v.astype(BF)
    return jnp.concatenate([high, (v - high.astype(F32)).astype(BF)], 0)


def whole_of(v):
    m = v.shape[0] // 2
    return v[:m].astype(F32) + v[m:].astype(F32)


def settle_cols_kernel(scalars, keep, *refs):
    *recvs, cols, cols_recv, out = refs
    m = keep.shape[0]
    v = keep[...]
    for r in recvs:
        v = v + r[...].astype(F32)
    out[:m] = v.astype(BF)
    out[m:] = parts_of(cols[...] + cols_recv[...])


def settle_cols(keep, recvs, cols, cols_recv, stage):
    shape = (keep.shape[0] + 2 * cols.shape[0], 128)
    return small_call(
        settle_cols_kernel, [jax.ShapeDtypeStruct(shape, BF)], "settle_cols", stage.scalars, keep, *recvs, cols, cols_recv
    )[0]


def sum_cols(scalars, own, recvs, m, held):
    held[scalars[0]] = whole_of(own[m:])
    for k, r in enumerate(recvs):
        held[scalars[1 + k]] = whole_of(r[m:])
    total = held[0]
    for k in range(1, held.shape[0]):
        total = total + held[k]
    return total


def join_cols_kernel(scalars, *refs):
    (own, *recvs), out, held = refs[:-2], refs[-2], refs[-1]
    size = 1 + len(recvs)
    m = own.shape[0] - 2 * held.shape[1]
    fill(out.at[pl.ds(0, size * m)], scalars, own, recvs)
    out[size * m:] = parts_of(sum_cols(scalars, own, recvs, m, held))


def join_cols(own, recvs, stage, extra):
    m = own.shape[0] - extra
    return small_call(
        join_cols_kernel, [jax.ShapeDtypeStruct((stage.size * m + extra, 128), BF)], "join_cols", stage.scalars, own, *recvs,
        scratch=[pltpu.VMEM((stage.size, extra // 2, 128), F32)],
    )[0]


def finish_qkv_kernel(scalars, *refs):
    (own, *recvs), (out, cols), (full, held) = refs[:-4], refs[-4:-2], refs[-2:]
    m = full.shape[0] // (1 + len(recvs))
    fill(full, scalars, own, recvs)
    cols[...] = sum_cols(scalars, own, recvs, m, held)
    half = out.shape[1]
    for c in range(D // 128):
        for t in range(3):
            row = (c * 3 + t) * half
            out[t, :, c * 128:c * 128 + 128] = full[row:row + half].astype(F32)


def finish_qkv(own, recvs, stage, half, extra):
    m = own.shape[0] - extra
    return small_call(
        finish_qkv_kernel,
        [jax.ShapeDtypeStruct((3, half, D), F32), jax.ShapeDtypeStruct((extra // 2, 128), F32)],
        "finish_qkv", stage.scalars, own, *recvs,
        scratch=[pltpu.VMEM((stage.size * m, 128), BF), pltpu.VMEM((stage.size, extra // 2, 128), F32)],
    )


def advance(steps, token):
    try:
        return steps.send(token), None
    except StopIteration as end:
        return token, end.value


def body(
    latents, scene_len, attn_gain, attn_shift, qkv_weight, out_weight, out_bias, mlp_gain, mlp_shift,
    up_weight, up_bias, down_weight, down_bias, cotangent,
):
    rows = latents.shape[0] // lax.axis_size("tensor")
    units, half = up_weight.shape[0], out_weight.shape[0]
    heads = half // HD
    tens = lax.axis_index("tensor").astype(jnp.int32).reshape(1)
    count = lax.axis_size("dp")
    steps = count.bit_length() - 1
    assert 1 << steps == count and steps > 1
    lower, upper = list(range(steps - 2)), [steps - 2, steps - 1]
    turned = [b ^ 1 if b ^ 1 < steps - 2 else b for b in lower]
    group = Stage(count, (upper, upper), ([1, 2, 3], [2, 1, 3]))
    pairs = [Stage(count, ([a], [b])) for a, b in zip(lower, turned)]
    mlp_stages = pairs + [group]
    if len(lower) % 2:
        qkv_stages = mlp_stages
    else:
        qkv_stages = [
            Stage(count, (lower[i:i + 2],) * 2, ([1, 2, 3], [2, 1, 3])) for i in range(0, len(lower), 2)
        ] + [group]

    packed, vecs = pack(
        (attn_gain, attn_shift, out_bias, mlp_gain, mlp_shift, down_bias), up_bias, qkv_weight.reshape(3 * half, D), out_weight
    )
    theirs = swap(packed)
    up_oth, down_oth = swap(up_weight), swap(down_weight)

    n1, qkv, p, att, rl, h1, n2 = attention_forward(
        tens, scene_len, latents, vecs, qkv_weight.reshape(3 * half, D), theirs, out_weight, rows
    )
    need = 8 * units + 4 * half + 16
    total_rows = -(-need // (16 * count)) * 16 * count
    block_out, gh, doa, grads_own, grads_oth, cols_two = mlp(
        tens, n2, cotangent, up_weight, down_weight, up_oth, down_oth, theirs, vecs, h1, att, rl, out_weight, total_rows
    )
    from_peer = swap(grads_oth)

    def exchanges(stages, keep, sends, settled, joined):
        for s, stage in enumerate(stages):
            recvs = stage.exchange(sends)
            token = yield sends[-1]
            recvs = [tie(r, token) for r in recvs]
            if s + 1 < len(stages):
                keep, sends = split(keep, recvs, stages[s + 1])
            else:
                have = settled(keep, recvs, stage)
        for s in range(len(stages) - 1, -1, -1):
            recvs = stages[s].exchange([have] * (stages[s].size - 1))
            token = yield have
            recvs = [tie(r, token) for r in recvs]
            if s:
                have = joined(have, recvs, stages[s])
        return have, recvs

    scenes = rows // LAT
    qkv_rows = -(-12 * half // (16 * count)) * 16 * count
    dqkv, dw = None, None
    token = grads_oth
    mlp_steps, mlp_result = None, None
    calls = 0
    for side in (1, 0):
        for scene in range(0, scenes, BACK_SCENES):
            dqkv, dw = attention_back(tie(tens, token), p, doa, qkv, n1, dqkv, dw, side, scene, BACK_SCENES, qkv_rows)
            token = dw
            if calls == 0:
                mlp_steps = exchanges(mlp_stages, *split_mlp(grads_own, tie(from_peer, token), mlp_stages[0]), settle, join)
                token = next(mlp_steps)
            elif calls in GO_ON and mlp_result is None:
                token, mlp_result = advance(mlp_steps, token)
            calls += 1
        if side:
            qkv_peer = swap(dw)
    keep, sends = split(dw, [qkv_peer], qkv_stages[0])
    cols = []
    extra = 48
    qkv_steps = exchanges(
        qkv_stages, keep, sends, lambda keep, recvs, stage: settle_cols(keep, recvs, *cols, stage),
        lambda own, recvs, stage: join_cols(own, recvs, stage, extra),
    )
    token = next(qkv_steps)
    grad_latents, cols_one = norm_one_back(tie(tens, token), dqkv, qkv_weight.reshape(3 * half, D), theirs, latents, vecs, gh)
    cols.append(jnp.concatenate([cols_one[:2], cols_two[:4]], 0).reshape(24, 128))
    cols.append(swap(cols[0]))
    token, qkv_result = advance(qkv_steps, cols_one)
    while mlp_result is None:
        token, mlp_result = advance(mlp_steps, token)
    dup, ddown, dwo, dub = finish_mlp(tie(mlp_result[0], token), *mlp_result[1:], mlp_stages[0], units, half)
    token = dub
    while qkv_result is None:
        token, qkv_result = advance(qkv_steps, token)
    dwq, shared = finish_qkv(*qkv_result, qkv_stages[0], half, extra)
    shared = shared.reshape(6, D)
    return (
        block_out, grad_latents, shared[0], shared[1], dwq, dwo, shared[4],
        shared[2], shared[3], dup, dub.reshape(units), ddown, shared[5],
    )


def solution(mesh):
    placed = (
        P("dp", None), P("dp"), P(), P(), P(None, "tensor", None), P("tensor", None), P(), P(), P(),
        P("tensor", None), P("tensor"), P("tensor", None), P(), P("dp", None),
    )
    return jax.shard_map(
        body,
        mesh=mesh,
        in_specs=placed,
        out_specs=(
            P(("dp", "tensor"), None), P(("dp", "tensor"), None), P(), P(), P(None, "tensor", None),
            P("tensor", None), P(), P(), P(), P("tensor", None), P("tensor"), P("tensor", None), P(),
        ),
        check_vma=False,
    )
```

```python
import functools

import jax
import jax.numpy as jnp
from jax import lax
from jax.experimental import pallas as pl
from jax.experimental.pallas import tpu as pltpu
from jax.sharding import PartitionSpec as P

D = 512
HD = 64
LAT = 512
AUG = 16
EPS = 1e-05
NEG = -1e30
BF = jnp.bfloat16
F32 = jnp.float32
MIB = 2**20
SWAP = [(0, 1), (1, 0)]
PLAN = (
("back", 1, 0, 1), ("mlp",), ("back", 1, 1, 3), ("mlp+",), ("back", 0, 0, 1), ("mlp+",), ("back", 0, 1, 3), ("mlp+",), ("qkv",), ("norm",), ("qkv+",), ("mlp+",), ("qkv+",), ("mlp+",), ("qkv+",), ("out",), ("end",), ("qkv+",),
)


def _dot(a, b, ca, cb):
    return lax.dot_general(a, b, (((ca,), (cb,)), ((), ())), preferred_element_type=F32)


def hbm(*values):
    return tuple(pltpu.with_memory_space_constraint(v, pltpu.HBM) for v in values)


def nn(a, b):
    return _dot(a, b, 1, 0)


def nt(a, b):
    return _dot(a, b, 1, 1)


def tn(a, b):
    return _dot(a, b, 0, 0)


def normalised(v):
    c = v - jnp.mean(v, -1, keepdims=True)
    r = lax.rsqrt(jnp.mean(c * c, -1, keepdims=True) + EPS)
    return c * r, r


def norm_back(e, xh, r):
    return r * (e - jnp.mean(e, -1, keepdims=True) - xh * jnp.mean(e * xh, -1, keepdims=True))


def forward_kernel(
    tens, lens, x_ref, vecs, wq_own, wq_oth, wo_own, wo_oth,
    n1_ref, qkv_ref, p_ref, att_ref, rl_ref, h1_ref, n2_ref,
):
    scenes = pl.num_programs(0)
    length = lens[tens[0] * scenes + pl.program_id(0)]
    x = x_ref[...].astype(F32)
    n1 = (normalised(x)[0] * vec(vecs, 0) + vec(vecs, 1)).astype(BF)
    n1_ref[...] = n1
    half = wo_own.shape[0]
    heads = half // HD

    def project(side, t):
        part = nt((wq_own, wq_oth)[side][t * half:(t + 1) * half], n1)
        if t == 0:
            part = part * HD**-0.5
        qkv_ref[0, side, t] = part.astype(BF)

    key_at = lax.broadcasted_iota(jnp.int32, (AUG, LAT), 1)
    row_at = lax.broadcasted_iota(jnp.int32, (AUG, LAT), 0)
    bias = jnp.where((key_at >= length) & (row_at == 0), NEG, 0.0).astype(BF)
    ones = jnp.ones((AUG, LAT), BF)

    def part_of(t, h):
        return qkv_ref[0, h // heads, t, h % heads * HD:h % heads * HD + HD]

    def scores(h):
        return tn(jnp.concatenate([part_of(1, h), bias], 0), jnp.concatenate([part_of(0, h), ones], 0))

    def weights(h, s):
        p = jnp.exp(s - jnp.max(s, 0, keepdims=True)).astype(BF)
        p_ref[0, h] = p
        return p

    def attend(h, p):
        o = nn(jnp.concatenate([part_of(2, h), ones], 0), p)
        rl = 1.0 / o[HD:HD + 1]
        rl_ref[0, h:h + 1] = rl
        att_ref[0, h * HD:h * HD + HD] = (o[:HD] * rl).astype(BF)

    for t in (1, 0, 2):
        project(0, t)
    scored, weighed = [], []
    total = None
    for h in range(2 * heads + 2):
        if h < 2 * heads:
            scored.append(scores(h))
        if h in (1, 2, 3):
            project(1, (1, 0, 2)[h - 1])
        if h >= 2:
            attend(h - 2, weighed.pop(0))
        if 1 <= h <= 2 * heads:
            weighed.append(weights(h - 1, scored.pop(0)))
        if h == heads + 2:
            total = tn(att_ref[0, :half], wo_own[...])
    h1 = x + (total + tn(att_ref[0, half:], wo_oth[...])) + vec(vecs, 2)
    h1_ref[...] = h1
    n2_ref[...] = (normalised(h1)[0] * vec(vecs, 3) + vec(vecs, 4)).astype(BF)


def whole(shape, row=0):
    at = (row,) + (0,) * (len(shape) - 1)
    return pl.BlockSpec(shape, lambda i, *_: at, pipeline_mode=pl.Buffered(1))


def takes(microseconds):
    return pl.CostEstimate(flops=int(microseconds * 1e9), bytes_accessed=0, transcendentals=0)


def params(mib):
    return pltpu.CompilerParams(vmem_limit_bytes=mib * MIB, dimension_semantics=("arbitrary",))


def vec(vecs, i):
    return vecs[i:i + 1].astype(F32)


def vecs_spec(row=0):
    return whole((16, D), row)


def attention_forward(tens, lens, x, vecs, wq_own, theirs, wo_own, rows):
    scenes = rows // LAT
    rowblock = pl.BlockSpec((LAT, D), lambda i, *_: (i, 0))
    half = wo_own.shape[0]
    return pl.pallas_call(
        forward_kernel,
        grid_spec=pltpu.PrefetchScalarGridSpec(
            num_scalar_prefetch=2,
            grid=(scenes,),
            in_specs=[
                pl.BlockSpec((LAT, D), lambda i, tens, lens: (tens[0] * scenes + i, 0)),
                vecs_spec(), whole((3 * half, D)), whole((3 * half, D)), whole((half, D)), whole((half, D), 3),
            ],
            out_specs=[
                rowblock,
                pl.BlockSpec((1, 2, 3, half, LAT), lambda i, *_: (i, 0, 0, 0, 0)),
                pl.BlockSpec((1, 2 * half // HD, LAT, LAT), lambda i, *_: (i, 0, 0, 0)),
                pl.BlockSpec((1, D, LAT), lambda i, *_: (i, 0, 0)),
                pl.BlockSpec((1, 2 * half // HD, LAT), lambda i, *_: (i, 0, 0)),
                rowblock,
                rowblock,
            ],
        ),
        out_shape=[
            pltpu.HBM((rows, D), BF),
            pltpu.HBM((scenes, 2, 3, half, LAT), BF),
            pltpu.HBM((scenes, 2 * half // HD, LAT, LAT), BF),
            pltpu.HBM((scenes, D, LAT), BF),
            pltpu.HBM((scenes, 2 * half // HD, LAT), F32),
            pltpu.HBM((rows, D), F32),
            pltpu.HBM((rows, D), BF),
        ],
        compiler_params=params(40),
        cost_estimate=takes(23),
        name="attention_forward",
    )(tens, *hbm(lens, x, vecs, wq_own), theirs, *hbm(wo_own), theirs)


LOG2E = 1.4426950408889634
SUB = 256


def gelu_parts(z):
    cdf = 0.5 + 0.5 * lax.erf(z * 0.7071067811865476)
    return z * cdf, cdf + z * (0.3989422804014327 * jnp.exp2(z * z * (-0.5 * LOG2E)))


def put_slabs(out, at, values):
    n = values.shape[0]
    for c in range(D // 128):
        out[at + c * n:at + (c + 1) * n] = values[:, c * 128:c * 128 + 128].astype(out.dtype)


def put_row(out, at, row, count):
    parts = [row[:, c * 128:c * 128 + 128] for c in range(row.shape[1] // 128)]
    parts += [jnp.zeros((1, 128), F32)] * (count - len(parts))
    out[at:at + count] = jnp.concatenate(parts, 0).astype(out.dtype)


def mlp_kernel(
    tens, n2_ref, cot_ref, up_own, down_own, up_oth, down_oth, vecs_oth, vecs, h1_ref, att_ref, rl_ref, wo_own, wo_oth,
    act_ref, gh_ref, doa_ref, own_ref, oth_ref, cols_ref, acc_up, acc_down, acc_ub, acc_wo,
):
    @pl.when(pl.program_id(0) == 0)
    def _():
        acc_up[...] = jnp.zeros_like(acc_up)
        acc_down[...] = jnp.zeros_like(acc_down)
        acc_ub[...] = jnp.zeros_like(acc_ub)
        acc_wo[...] = jnp.zeros_like(acc_wo)
        cols_ref[...] = jnp.zeros_like(cols_ref)

    n2, cot = n2_ref[...], cot_ref[...]
    units = up_own.shape[0]
    per = units // SUB

    def place(j):
        side, at = divmod(j, per)
        ups, downs, rows = ((up_own, down_own, vecs), (up_oth, down_oth, vecs_oth))[side]
        at = slice(at * SUB, at * SUB + SUB)
        first = at.start // D
        return ups[at], downs[at], vec(rows, 6 + first)[:, at.start - first * D:at.stop - first * D]

    def before(j):
        u, d, b = place(j)
        return nt(n2, u) + b, nt(cot, d)

    def between(pre, grad_act):
        act, slope = gelu_parts(pre)
        return act.astype(BF), (grad_act * slope).astype(BF)

    def after(j, act, dpre):
        u, _, _ = place(j)
        at = slice(j * SUB, j * SUB + SUB)
        act_ref[:, at] = act
        acc_down[at] += tn(act, cot)
        acc_up[at] += tn(dpre, n2)
        acc_ub[:, at] += jnp.sum(dpre.astype(F32), 0, keepdims=True)
        return nn(dpre, u)

    back = 0.0
    first, second = [], []
    for j in range(2 * per + 2):
        if j < 2 * per:
            first.append(before(j))
        if j >= 2:
            back += after(j - 2, *second.pop(0))
        if 1 <= j <= 2 * per:
            second.append(between(*first.pop(0)))
    xh, r = normalised(h1_ref[...])
    cot32 = cot.astype(F32)
    gh = cot32 + norm_back(back * vec(vecs, 3), xh, r)
    gh_ref[...] = gh
    gb = gh.astype(BF)
    half = wo_own.shape[0]
    heads = half // HD
    zeros = jnp.zeros((AUG - 3, LAT), F32)
    for side, w in enumerate((wo_own, wo_oth)):
        do = nt(w[...], gb)
        for h in range(heads):
            hh = side * heads + h
            scaled = (do[h * HD:h * HD + HD] * rl_ref[0, hh:hh + 1]).astype(BF)
            doa_ref[0, hh, :HD] = scaled
            delta = -jnp.sum(scaled.astype(F32) * att_ref[0, hh * HD:hh * HD + HD].astype(F32), 0, keepdims=True)
            high = delta.astype(BF).astype(F32)
            low = (delta - high).astype(BF).astype(F32)
            doa_ref[0, hh, HD:] = jnp.concatenate([high, low, delta - high - low, zeros], 0).astype(BF)
    acc_wo[...] += nn(att_ref[0], gb)
    cols_ref[...] += jnp.concatenate(
        [jnp.sum(v, 0, keepdims=True) for v in (back * xh, back, gh, cot32)] + [jnp.zeros((4, D), F32)], 0
    )

    @pl.when(pl.program_id(0) == pl.num_programs(0) - 1)
    def _():
        base = 8 * units + 4 * half
        for side, ref in enumerate((own_ref, oth_ref)):
            put_slabs(ref, 0, acc_up.at[side * units:(side + 1) * units])
            put_slabs(ref, 4 * units, acc_down.at[side * units:(side + 1) * units])
            put_slabs(ref, 8 * units, acc_wo.at[side * half:(side + 1) * half])
            put_row(ref, base, acc_ub[:, side * units:(side + 1) * units], 16)
            if ref.shape[0] > base + 16:
                ref[base + 16:] = jnp.zeros((ref.shape[0] - base - 16, 128), ref.dtype)


def mlp(tens, n2, cot, up, down, up_oth, down_oth, theirs, vecs, h1, att, rl, wo, total_rows):
    rows = n2.shape[0]
    scenes = rows // LAT
    units, half = up.shape[0], wo.shape[0]
    heads = 2 * half // HD
    rowblock = pl.BlockSpec((LAT, D), lambda i, *_: (i, 0))
    weights = whole((units, D))
    return pl.pallas_call(
        mlp_kernel,
        grid_spec=pltpu.PrefetchScalarGridSpec(
            num_scalar_prefetch=1,
            grid=(scenes,),
            in_specs=[
                rowblock,
                pl.BlockSpec((LAT, D), lambda i, tens: (tens[0] * scenes + i, 0)),
                weights, weights, weights, weights, vecs_spec(theirs.shape[0] // 16 - 1), vecs_spec(), rowblock,
                pl.BlockSpec((1, D, LAT), lambda i, *_: (i, 0, 0)),
                pl.BlockSpec((1, heads, LAT), lambda i, *_: (i, 0, 0)),
                whole((half, D)), whole((half, D), 3),
            ],
            out_specs=[
                pl.BlockSpec((LAT, 2 * units), lambda i, *_: (i, 0)), rowblock,
                pl.BlockSpec((1, heads, HD + AUG, LAT), lambda i, *_: (i, 0, 0, 0)),
                whole((total_rows, 128)), whole((total_rows, 128)), whole((8, D)),
            ],
            scratch_shapes=[
                pltpu.VMEM((2 * units, D), F32), pltpu.VMEM((2 * units, D), F32), pltpu.VMEM((1, 2 * units), F32),
                pltpu.VMEM((2 * half, D), F32),
            ],
        ),
        out_shape=[
            pltpu.HBM((rows, 2 * units), BF),
            pltpu.HBM((rows, D), F32),
            pltpu.HBM((scenes, heads, HD + AUG, LAT), BF),
            pltpu.HBM((total_rows, 128), BF),
            pltpu.HBM((total_rows, 128), BF),
            pltpu.HBM((8, D), F32),
        ],
        compiler_params=params(56),
        cost_estimate=takes(39),
        name="mlp",
    )(tens, *hbm(n2, cot, up, down, up_oth, down_oth, theirs, vecs, h1, att, rl, wo, theirs))


def block_out_kernel(tens, act_ref, down_own, down_oth, vecs, h1_ref, out_ref):
    units = down_own.shape[0]
    term = nn(act_ref[:, :units], down_own[...]) + nn(act_ref[:, units:], down_oth[...])
    out_ref[...] = (h1_ref[...] + term + vec(vecs, 5)).astype(BF)


def block_out(tens, act, down, down_oth, vecs, h1):
    rows = h1.shape[0]
    units = down.shape[0]
    rowblock = pl.BlockSpec((LAT, D), lambda i, *_: (i, 0))
    return pl.pallas_call(
        block_out_kernel,
        grid_spec=pltpu.PrefetchScalarGridSpec(
            num_scalar_prefetch=1,
            grid=(rows // LAT,),
            in_specs=[
                pl.BlockSpec((LAT, 2 * units), lambda i, *_: (i, 0)), whole((units, D)), whole((units, D)), vecs_spec(), rowblock,
            ],
            out_specs=[rowblock],
        ),
        out_shape=[pltpu.HBM((rows, D), BF)],
        compiler_params=params(24),
        cost_estimate=takes(7),
        name="block_out",
    )(tens, *hbm(act, down, down_oth, vecs, h1))[0]


def back_kernel(tens, p_ref, doa_ref, qkv_ref, n1_ref, *refs, ends):
    starts, stops = ends
    dqkv_ref, dw_ref, acc = refs[-3:]
    groups = acc.shape[0]
    ones = jnp.ones((AUG, LAT), BF)
    count = p_ref.shape[1]

    @pl.when((pl.program_id(0) == 0) & (pl.program_id(1) == 0))
    def _():
        if starts:
            acc[...] = jnp.zeros_like(acc)
        else:
            acc[...] = refs[0][...]

    def part_of(t, h):
        return qkv_ref[0, 0, t, h * HD:h * HD + HD]

    def first(h):
        return tn(jnp.concatenate([part_of(2, h), ones], 0), doa_ref[0, h])

    def second(h, grad):
        return (p_ref[0, h].astype(F32) * grad).astype(BF)

    def third(h, ds):
        at = slice(h * HD, h * HD + HD)
        dqkv_ref[0, 0, 0, at] = (nn(part_of(1, h), ds) * HD**-0.5).astype(BF)
        dqkv_ref[0, 0, 1, at] = nt(part_of(0, h), ds).astype(BF)

    def values(h):
        dqkv_ref[0, 0, 2, h * HD:h * HD + HD] = nt(doa_ref[0, h, :HD], p_ref[0, h]).astype(BF)

    grads, scores = [], []
    for h in range(count + 1):
        if h < count:
            grads.append(first(h))
            values(h)
        if h >= 1:
            third(h - 1, scores.pop(0))
        if h < count:
            scores.append(second(h, grads.pop(0)))
    feats = count * HD
    group = pl.program_id(1)
    term = nn(dqkv_ref[0, 0].reshape(3 * feats, LAT), n1_ref[...])
    acc[group] += term.reshape(3, feats, D)

    @pl.when((pl.program_id(0) == pl.num_programs(0) - 1) & (pl.program_id(1) == groups - 1))
    def _():
        if not stops:
            dw_ref[...] = acc[...]
            return
        for c in range(D // 128):
            for t in range(3):
                for g in range(groups):
                    row = ((c * 3 + t) * groups + g) * feats
                    dw_ref[row:row + feats] = acc[g, t, :, c * 128:c * 128 + 128].astype(dw_ref.dtype)
        used = 12 * groups * feats
        if used < dw_ref.shape[0]:
            dw_ref[used:] = jnp.zeros((dw_ref.shape[0] - used, 128), dw_ref.dtype)


BACK_HEADS = 2


def attention_back(tens, p, doa, qkv, n1, dqkv, partial, side, first, count, total_rows):
    scenes, heads = p.shape[0], p.shape[1] // 2
    steps = heads // BACK_HEADS
    feats = BACK_HEADS * HD
    block = lambda i, j, *_: (first + i, side, 0, j, 0)
    head_block = lambda i, j, *_: (first + i, side * steps + j, 0, 0)
    ends = (first == 0, first + count == scenes)
    sums = (steps, 3, feats, D)
    zeros = lambda i, j, *_: (0, 0, 0, 0)
    carried, specs, aliases = [], [], {}
    if not ends[0]:
        carried.append(partial)
        specs.append(pl.BlockSpec(sums, zeros, pipeline_mode=pl.Buffered(1)))
    if dqkv is not None:
        aliases = {5 + len(carried): 0}
        carried.append(dqkv)
        specs.append(pl.BlockSpec(memory_space=pl.ANY))
    if ends[1]:
        dw = jax.ShapeDtypeStruct((total_rows, 128), BF if side else F32)
        dw_spec = pl.BlockSpec((total_rows, 128), lambda i, j, *_: (0, 0), pipeline_mode=pl.Buffered(1))
    else:
        dw = pltpu.HBM(sums, F32)
        dw_spec = pl.BlockSpec(sums, zeros, pipeline_mode=pl.Buffered(1))
    return pl.pallas_call(
        functools.partial(back_kernel, ends=ends),
        grid_spec=pltpu.PrefetchScalarGridSpec(
            num_scalar_prefetch=1,
            grid=(count, steps),
            in_specs=[
                pl.BlockSpec((1, BACK_HEADS, LAT, LAT), head_block),
                pl.BlockSpec((1, BACK_HEADS, HD + AUG, LAT), head_block),
                pl.BlockSpec((1, 1, 3, feats, LAT), block),
                pl.BlockSpec((LAT, D), lambda i, j, *_: (first + i, 0)),
            ] + specs,
            out_specs=[pl.BlockSpec((1, 1, 3, feats, LAT), block), dw_spec],
            scratch_shapes=[pltpu.VMEM(sums, F32)],
        ),
        out_shape=[pltpu.HBM(qkv.shape, BF), dw],
        input_output_aliases=aliases,
        compiler_params=pltpu.CompilerParams(vmem_limit_bytes=24 * MIB, dimension_semantics=("arbitrary", "arbitrary")),
        cost_estimate=takes(4.5 * count),
        name="attention_back",
    )(tens, *hbm(p, doa, qkv, n1, *carried))


def norm_one_back_kernel(tens, dqkv, wq_own, wq_oth, x_ref, vecs, gh_ref, cols_two, gl_ref, cols_ref, acc):
    feats = wq_own.shape[0]
    g = tn(dqkv[0, 0].reshape(feats, LAT), wq_own[...]) + tn(dqkv[0, 1].reshape(feats, LAT), wq_oth[...])
    xh, r = normalised(x_ref[...].astype(F32))
    gl_ref[...] = gh_ref[...] + norm_back(g * vec(vecs, 0), xh, r)
    sums = jnp.concatenate([jnp.sum(v, 0, keepdims=True) for v in (g * xh, g)] + [cols_two[:4], cols_two[6:]], 0)

    @pl.when(pl.program_id(0) == 0)
    def _():
        acc[...] = sums

    @pl.when(pl.program_id(0) > 0)
    def _():
        acc[:2] += sums[:2]

    @pl.when(pl.program_id(0) == pl.num_programs(0) - 1)
    def _():
        total = acc[...]
        for c in range(D // 128):
            cols_ref[c * 8:c * 8 + 8] = total[:, c * 128:c * 128 + 128]


def norm_one_back(tens, dqkv, wq_own, theirs, x, vecs, gh, cols_two):
    scenes, half = dqkv.shape[0], dqkv.shape[3]
    rowblock = pl.BlockSpec((LAT, D), lambda i, *_: (i, 0))
    return pl.pallas_call(
        norm_one_back_kernel,
        grid_spec=pltpu.PrefetchScalarGridSpec(
            num_scalar_prefetch=1,
            grid=(scenes,),
            in_specs=[
                pl.BlockSpec((1, 2, 3, half, LAT), lambda i, *_: (i, 0, 0, 0, 0)),
                whole((3 * half, D)), whole((3 * half, D)),
                pl.BlockSpec((LAT, D), lambda i, tens: (tens[0] * scenes + i, 0)),
                vecs_spec(),
                rowblock,
                whole((8, D)),
            ],
            out_specs=[rowblock, whole((32, 128))],
            scratch_shapes=[pltpu.VMEM((8, D), F32)],
        ),
        out_shape=[pltpu.HBM((scenes * LAT, D), F32), jax.ShapeDtypeStruct((32, 128), F32)],
        compiler_params=params(28),
        cost_estimate=takes(10),
        name="norm_one_back",
    )(tens, *hbm(dqkv, wq_own, theirs, x, vecs, gh, cols_two))


def tie(value, *after):
    return lax.optimization_barrier((value, *after))[0]


def swap(v):
    return lax.ppermute(v, "tensor", SWAP)


class Stage:
    def __init__(self, count, bits, distances=None):
        self.count, self.bits = count, bits
        self.size = 1 << len(bits[0])
        each = list(range(1, self.size))
        self.distances = distances or (each, each)
        at = lax.axis_index("dp")
        core = lax.axis_index("tensor")

        def value(t, v):
            return sum((jnp.right_shift(v, b) & 1) << k for k, b in enumerate(bits[t]))

        self.place = jnp.where(core == 0, value(0, at), value(1, at)).astype(jnp.int32)
        met = [jnp.where(core == 0, self.distances[0][k], self.distances[1][k]) ^ self.place for k in range(self.size - 1)]
        self.scalars = jnp.stack([self.place] + met).astype(jnp.int32)

    def exchange(self, values):
        out = []
        for k, v in enumerate(values):
            pairs = []
            for i in range(self.count):
                for t in range(2):
                    d = self.distances[t][k]
                    flip = sum(((d >> j) & 1) << b for j, b in enumerate(self.bits[t]))
                    pairs.append((i * 2 + t, (i ^ flip) * 2 + t))
            out.append(lax.ppermute(v, ("dp", "tensor"), pairs))
        return out


def small_call(kernel, out_shape, name, scalars, *arrays, scratch=(), mib=16):
    return pl.pallas_call(
        kernel,
        in_specs=[pl.BlockSpec(memory_space=pltpu.SMEM)] + [pl.BlockSpec(memory_space=pltpu.VMEM)] * len(arrays),
        out_specs=[pl.BlockSpec(memory_space=pltpu.VMEM)] * len(out_shape),
        out_shape=out_shape,
        scratch_shapes=list(scratch),
        compiler_params=pltpu.CompilerParams(vmem_limit_bytes=mib * MIB),
        name=name,
    )(scalars, *arrays)


def pack_kernel(*refs):
    (*rows, up_bias, wq, wo), (packed, vecs), scratch = refs[:9], refs[9:11], refs[11:]
    *held, whole_sem, sem = scratch
    first = wq.shape[0]
    everything = held[-1]
    last = everything.shape[0] - 16
    big = [
        pltpu.make_async_copy(wq, everything.at[pl.ds(0, first)], sem.at[0]),
        pltpu.make_async_copy(wo, everything.at[pl.ds(first, last - first)], sem.at[1]),
    ]
    small = [pltpu.make_async_copy(r, h, sem.at[2 + k]) for k, (r, h) in enumerate(zip((*rows, up_bias), held))]
    for c in big + small:
        c.start()
    for c in small:
        c.wait()
    parts = [h[...].astype(F32).reshape(1, D) for h in held[:-2]]
    bias = held[-2][...].astype(F32)
    parts += [bias[i:i + D].reshape(1, D) for i in range(0, bias.shape[0], D)]
    everything[last:] = jnp.concatenate(parts + [jnp.zeros((16 - len(parts), D), F32)], 0).astype(BF)
    for c in big:
        c.wait()
    out = [
        pltpu.make_async_copy(everything, packed, whole_sem.at[0]),
        pltpu.make_async_copy(everything.at[pl.ds(last, 16)], vecs, whole_sem.at[1]),
    ]
    for c in out:
        c.start()
    for c in out:
        c.wait()


def pack(rows, up_bias, wq, wo):
    shape = (wq.shape[0] + wo.shape[0] + 16, D)
    return pl.pallas_call(
        pack_kernel,
        in_specs=[pl.BlockSpec(memory_space=pl.ANY)] * 9,
        out_specs=[pl.BlockSpec(memory_space=pl.ANY)] * 2,
        out_shape=[pltpu.HBM(shape, BF), pltpu.HBM((16, D), BF)],
        scratch_shapes=[pltpu.VMEM((D,), BF)] * 6 + [
            pltpu.VMEM(up_bias.shape, BF), pltpu.VMEM(shape, BF), pltpu.SemaphoreType.DMA((2,)),
            pltpu.SemaphoreType.DMA((9,)),
        ],
        compiler_params=pltpu.CompilerParams(vmem_limit_bytes=16 * MIB),
        name="pack",
    )(*hbm(*rows, up_bias, wq, wo))


def chunk(place, m):
    return pl.ds(pl.multiple_of(place * m, 16), m)


def hand_out(total, scalars, keep_out, sends):
    m = keep_out.shape[0]
    keep_out[...] = total[chunk(scalars[0], m)]
    for k, out in enumerate(sends):
        out[...] = total[chunk(scalars[1 + k], m)].astype(BF)


def split_kernel(scalars, *refs, count):
    (keep, *recvs), (keep_out, *sends), total = refs[:count], refs[count:-1], refs[-1]
    v = keep[...]
    for r in recvs:
        v = v + r[...].astype(F32)
    total[...] = v
    hand_out(total, scalars, keep_out, sends)


def pieces(stage, rows):
    m = rows // stage.size
    return [jax.ShapeDtypeStruct((m, 128), F32)] + [jax.ShapeDtypeStruct((m, 128), BF)] * (stage.size - 1)


def split(keep, recvs, stage):
    keep, *sends = small_call(
        functools.partial(split_kernel, count=1 + len(recvs)), pieces(stage, keep.shape[0]), "split", stage.scalars, keep,
        *recvs, scratch=[pltpu.VMEM(keep.shape, F32)],
    )
    return keep, sends


def settle_kernel(scalars, keep, *refs):
    v = keep[...]
    for r in refs[:-1]:
        v = v + r[...].astype(F32)
    refs[-1][...] = v.astype(BF)


def settle(keep, recvs, stage):
    return small_call(settle_kernel, [jax.ShapeDtypeStruct(keep.shape, BF)], "settle", stage.scalars, keep, *recvs)[0]


def fill(full, scalars, own, recvs):
    m = full.shape[0] // (1 + len(recvs))
    full[chunk(scalars[0], m)] = own[:m]
    for k, r in enumerate(recvs):
        full[chunk(scalars[1 + k], m)] = r[:m]


def join_kernel(scalars, own, *refs):
    fill(refs[-1], scalars, own, refs[:-1])


def join(own, recvs, stage):
    return small_call(
        join_kernel, [jax.ShapeDtypeStruct((stage.size * own.shape[0], 128), BF)], "join", stage.scalars, own, *recvs
    )[0]


def split_mlp_kernel(scalars, own, recv, keep_out, *sends):
    m = keep_out.shape[0]
    at = chunk(scalars[0], m)
    keep_out[...] = own[at].astype(F32) + recv[at].astype(F32)
    for k, out in enumerate(sends):
        at = chunk(scalars[1 + k], m)
        out[...] = (own[at].astype(F32) + recv[at].astype(F32)).astype(BF)


def split_mlp(own, recv, stage):
    keep, *sends = small_call(
        split_mlp_kernel, pieces(stage, own.shape[0]), "split_mlp", stage.scalars, *hbm(own), recv, mib=24,
    )
    return keep, sends


def finish_mlp_kernel(scalars, *refs):
    (own, *recvs), (dup, ddown, dwo, dub), full = refs[:-5], refs[-5:-1], refs[-1]
    fill(full, scalars, own, recvs)
    units, half = dup.shape[0], dwo.shape[0]
    for c in range(D // 128):
        at = slice(c * 128, c * 128 + 128)
        dup[:, at] = full[c * units:(c + 1) * units].astype(F32)
        ddown[:, at] = full[(4 + c) * units:(5 + c) * units].astype(F32)
        dwo[:, at] = full[8 * units + c * half:8 * units + (c + 1) * half].astype(F32)
    base = 8 * units + 4 * half
    dub[...] = full[base:base + dub.shape[0]].astype(F32)


def finish_mlp(own, recvs, stage, units, half):
    return small_call(
        finish_mlp_kernel,
        [
            jax.ShapeDtypeStruct((units, D), F32), jax.ShapeDtypeStruct((units, D), F32),
            jax.ShapeDtypeStruct((half, D), F32), jax.ShapeDtypeStruct((units // 128, 128), F32),
        ],
        "finish_mlp", stage.scalars, own, *recvs, scratch=[pltpu.VMEM((stage.size * own.shape[0], 128), BF)],
    )


def parts_of(v):
    high = v.astype(BF)
    return jnp.concatenate([high, (v - high.astype(F32)).astype(BF)], 0)


def whole_of(v):
    m = v.shape[0] // 2
    return v[:m].astype(F32) + v[m:].astype(F32)


def settle_cols_kernel(scalars, keep, *refs):
    *recvs, cols, cols_recv, out = refs
    m = keep.shape[0]
    v = keep[...]
    for r in recvs:
        v = v + r[...].astype(F32)
    out[:m] = v.astype(BF)
    out[m:] = parts_of(cols[...] + cols_recv[...])


def settle_cols(keep, recvs, cols, cols_recv, stage):
    shape = (keep.shape[0] + 2 * cols.shape[0], 128)
    return small_call(
        settle_cols_kernel, [jax.ShapeDtypeStruct(shape, BF)], "settle_cols", stage.scalars, keep, *recvs, cols, cols_recv
    )[0]


def sum_cols(scalars, own, recvs, m, held):
    held[scalars[0]] = whole_of(own[m:])
    for k, r in enumerate(recvs):
        held[scalars[1 + k]] = whole_of(r[m:])
    total = held[0]
    for k in range(1, held.shape[0]):
        total = total + held[k]
    return total


def join_cols_kernel(scalars, *refs):
    (own, *recvs), out, held = refs[:-2], refs[-2], refs[-1]
    size = 1 + len(recvs)
    m = own.shape[0] - 2 * held.shape[1]
    fill(out.at[pl.ds(0, size * m)], scalars, own, recvs)
    out[size * m:] = parts_of(sum_cols(scalars, own, recvs, m, held))


def join_cols(own, recvs, stage, extra):
    m = own.shape[0] - extra
    return small_call(
        join_cols_kernel, [jax.ShapeDtypeStruct((stage.size * m + extra, 128), BF)], "join_cols", stage.scalars, own, *recvs,
        scratch=[pltpu.VMEM((stage.size, extra // 2, 128), F32)],
    )[0]


def finish_qkv_kernel(scalars, *refs):
    (own, *recvs), (out, cols), (full, held) = refs[:-4], refs[-4:-2], refs[-2:]
    m = full.shape[0] // (1 + len(recvs))
    fill(full, scalars, own, recvs)
    cols[...] = sum_cols(scalars, own, recvs, m, held)
    half = out.shape[1]
    for c in range(D // 128):
        for t in range(3):
            row = (c * 3 + t) * half
            out[t, :, c * 128:c * 128 + 128] = full[row:row + half].astype(F32)


def finish_qkv(own, recvs, stage, half, extra):
    m = own.shape[0] - extra
    return small_call(
        finish_qkv_kernel,
        [jax.ShapeDtypeStruct((3, half, D), F32), jax.ShapeDtypeStruct((extra // 2, 128), F32)],
        "finish_qkv", stage.scalars, own, *recvs,
        scratch=[pltpu.VMEM((stage.size * m, 128), BF), pltpu.VMEM((stage.size, extra // 2, 128), F32)],
    )


def advance(steps, token):
    try:
        return steps.send(token), None
    except StopIteration as end:
        return token, end.value


def body(
    latents, scene_len, attn_gain, attn_shift, qkv_weight, out_weight, out_bias, mlp_gain, mlp_shift,
    up_weight, up_bias, down_weight, down_bias, cotangent,
):
    rows = latents.shape[0] // lax.axis_size("tensor")
    units, half = up_weight.shape[0], out_weight.shape[0]
    heads = half // HD
    tens = lax.axis_index("tensor").astype(jnp.int32).reshape(1)
    count = lax.axis_size("dp")
    steps = count.bit_length() - 1
    assert 1 << steps == count and steps > 1
    lower, upper = list(range(steps - 2)), [steps - 2, steps - 1]
    turned = [b ^ 1 if b ^ 1 < steps - 2 else b for b in lower]
    group = Stage(count, (upper, upper), ([1, 2, 3], [2, 1, 3]))
    pairs = [Stage(count, ([a], [b])) for a, b in zip(lower, turned)]
    mlp_stages = pairs + [group]
    if len(lower) % 2:
        qkv_stages = mlp_stages
    else:
        qkv_stages = [
            Stage(count, (lower[i:i + 2],) * 2, ([1, 2, 3], [2, 1, 3])) for i in range(0, len(lower), 2)
        ] + [group]

    packed, vecs = pack(
        (attn_gain, attn_shift, out_bias, mlp_gain, mlp_shift, down_bias), up_bias, qkv_weight.reshape(3 * half, D), out_weight
    )
    theirs = swap(packed)
    up_oth, down_oth = swap(up_weight), swap(down_weight)

    n1, qkv, p, att, rl, h1, n2 = attention_forward(
        tens, scene_len, latents, vecs, qkv_weight.reshape(3 * half, D), theirs, out_weight, rows
    )
    need = 8 * units + 4 * half + 16
    total_rows = -(-need // (16 * count)) * 16 * count
    act, gh, doa, grads_own, grads_oth, cols_two = mlp(
        tens, n2, cotangent, up_weight, down_weight, up_oth, down_oth, theirs, vecs, h1, att, rl, out_weight, total_rows
    )
    from_peer = swap(grads_oth)

    def exchanges(stages, keep, sends, settled, joined):
        for s, stage in enumerate(stages):
            recvs = stage.exchange(sends)
            token = yield sends[-1]
            recvs = [tie(r, token) for r in recvs]
            if s + 1 < len(stages):
                keep, sends = split(keep, recvs, stages[s + 1])
            else:
                have = settled(keep, recvs, stage)
        for s in range(len(stages) - 1, -1, -1):
            recvs = stages[s].exchange([have] * (stages[s].size - 1))
            token = yield have
            recvs = [tie(r, token) for r in recvs]
            if s:
                have = joined(have, recvs, stages[s])
        return have, recvs

    qkv_rows = -(-12 * half // (16 * count)) * 16 * count
    extra = 64
    dqkv, dw, qkv_peer = None, None, None
    token = grads_oth
    chains, results = {}, {}
    cols = []

    def step(name):
        if name not in results:
            after, result = advance(chains[name], token)
            if result is not None:
                results[name] = result
            return after
        return token

    for action, *rest in PLAN:
        if action == "back":
            side, first, number = rest
            dqkv, dw = attention_back(tie(tens, token), p, doa, qkv, n1, dqkv, dw, side, first, number, qkv_rows)
            token = dw
            if side and first + number == rows // LAT:
                qkv_peer = swap(dw)
        elif action == "mlp":
            chains["mlp"] = exchanges(
                mlp_stages, *split_mlp(grads_own, tie(from_peer, token), mlp_stages[0]), settle, join
            )
            token = next(chains["mlp"])
        elif action == "qkv":
            chains["qkv"] = exchanges(
                qkv_stages, *split(tie(dw, token), [qkv_peer], qkv_stages[0]),
                lambda keep, recvs, stage: settle_cols(keep, recvs, *cols, stage),
                lambda own, recvs, stage: join_cols(own, recvs, stage, extra),
            )
            token = next(chains["qkv"])
        elif action == "norm":
            grad_latents, cols_one = norm_one_back(
                tie(tens, token), dqkv, qkv_weight.reshape(3 * half, D), theirs, latents, vecs, gh, cols_two
            )
            cols.extend((cols_one, swap(cols_one)))
            token = cols_one
        elif action == "out":
            out = block_out(tie(tens, token), act, down_weight, down_oth, vecs, h1)
            token = out
        elif action == "end":
            while "mlp" not in results:
                token = step("mlp")
            have, recvs = results["mlp"]
            dup, ddown, dwo, dub = finish_mlp(tie(have, token), recvs, mlp_stages[0], units, half)
            token = dub
        else:
            token = step(action[:3])
    while "qkv" not in results:
        token = step("qkv")
    dwq, shared = finish_qkv(*results["qkv"], qkv_stages[0], half, extra)
    shared = shared.reshape(D // 128, 8, 128).transpose(1, 0, 2).reshape(8, D)
    return (
        out, grad_latents, shared[0], shared[1], dwq, dwo, shared[4],
        shared[2], shared[3], dup, dub.reshape(units), ddown, shared[5],
    )


def solution(mesh):
    placed = (
        P("dp", None), P("dp"), P(), P(), P(None, "tensor", None), P("tensor", None), P(), P(), P(),
        P("tensor", None), P("tensor"), P("tensor", None), P(), P("dp", None),
    )
    return jax.shard_map(
        body,
        mesh=mesh,
        in_specs=placed,
        out_specs=(
            P(("dp", "tensor"), None), P(("dp", "tensor"), None), P(), P(), P(None, "tensor", None),
            P("tensor", None), P(), P(), P(), P("tensor", None), P("tensor"), P("tensor", None), P(),
        ),
        check_vma=False,
    )
```

```python
import functools

import jax
import jax.numpy as jnp
from jax import lax
from jax.experimental import pallas as pl
from jax.experimental.pallas import tpu as pltpu
from jax.sharding import PartitionSpec as P

D = 512
HD = 64
LAT = 512
AUG = 16
EPS = 1e-05
NEG = -1e30
BF = jnp.bfloat16
F32 = jnp.float32
MIB = 2**20
SWAP = [(0, 1), (1, 0)]
PLAN = (
("back", 1, 0, 1), ("mlp",), ("back", 1, 1, 3), ("mlp+",), ("back", 0, 0, 2), ("mlp+",), ("back", 0, 2, 2), ("mlp+",), ("qkv",), ("norm",), ("qkv+",), ("mlp+",), ("qkv+",), ("mlp+",), ("qkv+",), ("out",), ("end",), ("qkv+",),
)


def _dot(a, b, ca, cb):
    return lax.dot_general(a, b, (((ca,), (cb,)), ((), ())), preferred_element_type=F32)


def hbm(*values):
    return tuple(pltpu.with_memory_space_constraint(v, pltpu.HBM) for v in values)


def vmem(*values):
    return tuple(pltpu.with_memory_space_constraint(v, pltpu.VMEM) for v in values)


def nn(a, b):
    return _dot(a, b, 1, 0)


def nt(a, b):
    return _dot(a, b, 1, 1)


def tn(a, b):
    return _dot(a, b, 0, 0)


def normalised(v):
    c = v - jnp.mean(v, -1, keepdims=True)
    r = lax.rsqrt(jnp.mean(c * c, -1, keepdims=True) + EPS)
    return c * r, r


def norm_back(e, xh, r):
    return r * (e - jnp.mean(e, -1, keepdims=True) - xh * jnp.mean(e * xh, -1, keepdims=True))


def forward_kernel(
    tens, lens, x_ref, vecs, wq_own, wq_oth, wo_own, wo_oth,
    n1_ref, qkv_ref, p_ref, att_ref, rl_ref, h1_ref, n2_ref,
):
    scenes = pl.num_programs(0)
    length = lens[tens[0] * scenes + pl.program_id(0)]
    x = x_ref[...].astype(F32)
    n1 = (normalised(x)[0] * vec(vecs, 0) + vec(vecs, 1)).astype(BF)
    n1_ref[...] = n1
    half = wo_own.shape[0]
    heads = half // HD

    def project(side, t):
        part = nt((wq_own, wq_oth)[side][t * half:(t + 1) * half], n1)
        if t == 0:
            part = part * HD**-0.5
        qkv_ref[0, side, t] = part.astype(BF)

    key_at = lax.broadcasted_iota(jnp.int32, (AUG, LAT), 1)
    row_at = lax.broadcasted_iota(jnp.int32, (AUG, LAT), 0)
    bias = jnp.where((key_at >= length) & (row_at == 0), NEG, 0.0).astype(BF)
    ones = jnp.ones((AUG, LAT), BF)

    def part_of(t, h):
        return qkv_ref[0, h // heads, t, h % heads * HD:h % heads * HD + HD]

    def scores(h):
        return tn(jnp.concatenate([part_of(1, h), bias], 0), jnp.concatenate([part_of(0, h), ones], 0))

    def weights(h, s):
        p = jnp.exp(s - jnp.max(s, 0, keepdims=True)).astype(BF)
        p_ref[0, h] = p
        return p

    def attend(h, p):
        o = nn(jnp.concatenate([part_of(2, h), ones], 0), p)
        rl = 1.0 / o[HD:HD + 1]
        rl_ref[0, h:h + 1] = rl
        att_ref[0, h * HD:h * HD + HD] = (o[:HD] * rl).astype(BF)

    for t in (1, 0, 2):
        project(0, t)
    scored, weighed = [], []
    total = None
    for h in range(2 * heads + 2):
        if h < 2 * heads:
            scored.append(scores(h))
        if h in (1, 2, 3):
            project(1, (1, 0, 2)[h - 1])
        if h >= 2:
            attend(h - 2, weighed.pop(0))
        if 1 <= h <= 2 * heads:
            weighed.append(weights(h - 1, scored.pop(0)))
        if h == heads + 2:
            total = tn(att_ref[0, :half], wo_own[...])
    h1 = x + (total + tn(att_ref[0, half:], wo_oth[...])) + vec(vecs, 2)
    h1_ref[...] = h1
    n2_ref[...] = (normalised(h1)[0] * vec(vecs, 3) + vec(vecs, 4)).astype(BF)


def whole(shape):
    at = (0,) * len(shape)
    return pl.BlockSpec(shape, lambda i, *_: at, pipeline_mode=pl.Buffered(1))


def takes(microseconds):
    return pl.CostEstimate(flops=int(microseconds * 1e9), bytes_accessed=0, transcendentals=0)


def params(mib):
    return pltpu.CompilerParams(vmem_limit_bytes=mib * MIB, dimension_semantics=("arbitrary",))


def vec(vecs, i):
    return vecs[i:i + 1]


def vecs_spec():
    return whole((8, D))


def attention_forward(tens, lens, x, vecs, wq_own, wq_oth, wo_own, wo_oth, rows):
    scenes = rows // LAT
    rowblock = pl.BlockSpec((LAT, D), lambda i, *_: (i, 0))
    half = wo_own.shape[0]
    return pl.pallas_call(
        forward_kernel,
        grid_spec=pltpu.PrefetchScalarGridSpec(
            num_scalar_prefetch=2,
            grid=(scenes,),
            in_specs=[
                pl.BlockSpec((LAT, D), lambda i, tens, lens: (tens[0] * scenes + i, 0)),
                vecs_spec(), whole((3 * half, D)), whole((3 * half, D)), whole((half, D)), whole((half, D)),
            ],
            out_specs=[
                rowblock,
                pl.BlockSpec((1, 2, 3, half, LAT), lambda i, *_: (i, 0, 0, 0, 0)),
                pl.BlockSpec((1, 2 * half // HD, LAT, LAT), lambda i, *_: (i, 0, 0, 0)),
                pl.BlockSpec((1, D, LAT), lambda i, *_: (i, 0, 0)),
                pl.BlockSpec((1, 2 * half // HD, LAT), lambda i, *_: (i, 0, 0)),
                rowblock,
                rowblock,
            ],
        ),
        out_shape=[
            pltpu.HBM((rows, D), BF),
            pltpu.HBM((scenes, 2, 3, half, LAT), BF),
            pltpu.HBM((scenes, 2 * half // HD, LAT, LAT), BF),
            pltpu.HBM((scenes, D, LAT), BF),
            pltpu.HBM((scenes, 2 * half // HD, LAT), F32),
            pltpu.HBM((rows, D), F32),
            pltpu.HBM((rows, D), BF),
        ],
        compiler_params=params(40),
        cost_estimate=takes(23),
        name="attention_forward",
    )(tens, *hbm(lens, x), vecs, *hbm(wq_own), wq_oth, *hbm(wo_own), wo_oth)


LOG2E = 1.4426950408889634
SUB = 256


def gelu_parts(z):
    cdf = 0.5 + 0.5 * lax.erf(z * 0.7071067811865476)
    return z * cdf, cdf + z * (0.3989422804014327 * jnp.exp2(z * z * (-0.5 * LOG2E)))


def put_slabs(out, at, values):
    n = values.shape[0]
    for c in range(D // 128):
        out[at + c * n:at + (c + 1) * n] = values[:, c * 128:c * 128 + 128].astype(out.dtype)


def put_row(out, at, row, count):
    parts = [row[:, c * 128:c * 128 + 128] for c in range(row.shape[1] // 128)]
    parts += [jnp.zeros((1, 128), F32)] * (count - len(parts))
    out[at:at + count] = jnp.concatenate(parts, 0).astype(out.dtype)


def mlp_kernel(
    tens, n2_ref, cot_ref, up_own, down_own, up_oth, down_oth, vecs_oth, vecs, h1_ref, att_ref, rl_ref, wo_own, wo_oth,
    act_ref, gh_ref, doa_ref, own_ref, oth_ref, cols_ref, acc_up, acc_down, acc_ub, acc_wo,
):
    @pl.when(pl.program_id(0) == 0)
    def _():
        acc_up[...] = jnp.zeros_like(acc_up)
        acc_down[...] = jnp.zeros_like(acc_down)
        acc_ub[...] = jnp.zeros_like(acc_ub)
        acc_wo[...] = jnp.zeros_like(acc_wo)
        cols_ref[...] = jnp.zeros_like(cols_ref)

    n2, cot = n2_ref[...], cot_ref[...]
    units = up_own.shape[0]
    per = units // SUB

    def place(j):
        side, at = divmod(j, per)
        ups, downs, rows = ((up_own, down_own, vecs), (up_oth, down_oth, vecs_oth))[side]
        at = slice(at * SUB, at * SUB + SUB)
        first = at.start // D
        return ups[at], downs[at], vec(rows, 6 + first)[:, at.start - first * D:at.stop - first * D]

    def before(j):
        u, d, b = place(j)
        return nt(n2, u) + b, nt(cot, d)

    def between(pre, grad_act):
        act, slope = gelu_parts(pre)
        return act.astype(BF), (grad_act * slope).astype(BF)

    def after(j, act, dpre):
        u, _, _ = place(j)
        at = slice(j * SUB, j * SUB + SUB)
        act_ref[:, at] = act
        acc_down[at] += tn(act, cot)
        acc_up[at] += tn(dpre, n2)
        acc_ub[:, at] += jnp.sum(dpre.astype(F32), 0, keepdims=True)
        return nn(dpre, u)

    back = 0.0
    first, second = [], []
    for j in range(2 * per + 2):
        if j < 2 * per:
            first.append(before(j))
        if j >= 2:
            back += after(j - 2, *second.pop(0))
        if 1 <= j <= 2 * per:
            second.append(between(*first.pop(0)))
    xh, r = normalised(h1_ref[...])
    cot32 = cot.astype(F32)
    gh = cot32 + norm_back(back * vec(vecs, 3), xh, r)
    gh_ref[...] = gh
    gb = gh.astype(BF)
    half = wo_own.shape[0]
    heads = half // HD
    zeros = jnp.zeros((AUG - 3, LAT), F32)
    for side, w in enumerate((wo_own, wo_oth)):
        do = nt(w[...], gb)
        for h in range(heads):
            hh = side * heads + h
            scaled = (do[h * HD:h * HD + HD] * rl_ref[0, hh:hh + 1]).astype(BF)
            doa_ref[0, hh, :HD] = scaled
            delta = -jnp.sum(scaled.astype(F32) * att_ref[0, hh * HD:hh * HD + HD].astype(F32), 0, keepdims=True)
            high = delta.astype(BF).astype(F32)
            low = (delta - high).astype(BF).astype(F32)
            doa_ref[0, hh, HD:] = jnp.concatenate([high, low, delta - high - low, zeros], 0).astype(BF)
    acc_wo[...] += nn(att_ref[0], gb)
    cols_ref[...] += jnp.concatenate(
        [jnp.sum(v, 0, keepdims=True) for v in (back * xh, back, gh, cot32)] + [jnp.zeros((4, D), F32)], 0
    )

    @pl.when(pl.program_id(0) == pl.num_programs(0) - 1)
    def _():
        base = 8 * units + 4 * half
        for side, ref in enumerate((own_ref, oth_ref)):
            put_slabs(ref, 0, acc_up.at[side * units:(side + 1) * units])
            put_slabs(ref, 4 * units, acc_down.at[side * units:(side + 1) * units])
            put_slabs(ref, 8 * units, acc_wo.at[side * half:(side + 1) * half])
            put_row(ref, base, acc_ub[:, side * units:(side + 1) * units], 16)
            if ref.shape[0] > base + 16:
                ref[base + 16:] = jnp.zeros((ref.shape[0] - base - 16, 128), ref.dtype)


def mlp(tens, n2, cot, up, down, up_oth, down_oth, vecs_oth, vecs, h1, att, rl, wo, wo_oth, total_rows):
    rows = n2.shape[0]
    scenes = rows // LAT
    units, half = up.shape[0], wo.shape[0]
    heads = 2 * half // HD
    rowblock = pl.BlockSpec((LAT, D), lambda i, *_: (i, 0))
    weights = whole((units, D))
    return pl.pallas_call(
        mlp_kernel,
        grid_spec=pltpu.PrefetchScalarGridSpec(
            num_scalar_prefetch=1,
            grid=(scenes,),
            in_specs=[
                rowblock,
                pl.BlockSpec((LAT, D), lambda i, tens: (tens[0] * scenes + i, 0)),
                weights, weights, weights, weights, vecs_spec(), vecs_spec(), rowblock,
                pl.BlockSpec((1, D, LAT), lambda i, *_: (i, 0, 0)),
                pl.BlockSpec((1, heads, LAT), lambda i, *_: (i, 0, 0)),
                whole((half, D)), whole((half, D)),
            ],
            out_specs=[
                pl.BlockSpec((LAT, 2 * units), lambda i, *_: (i, 0)), rowblock,
                pl.BlockSpec((1, heads, HD + AUG, LAT), lambda i, *_: (i, 0, 0, 0)),
                whole((total_rows, 128)), whole((total_rows, 128)), whole((8, D)),
            ],
            scratch_shapes=[
                pltpu.VMEM((2 * units, D), F32), pltpu.VMEM((2 * units, D), F32), pltpu.VMEM((1, 2 * units), F32),
                pltpu.VMEM((2 * half, D), F32),
            ],
        ),
        out_shape=[
            pltpu.HBM((rows, 2 * units), BF),
            pltpu.HBM((rows, D), F32),
            pltpu.HBM((scenes, heads, HD + AUG, LAT), BF),
            pltpu.HBM((total_rows, 128), BF),
            pltpu.HBM((total_rows, 128), BF),
            pltpu.HBM((8, D), F32),
        ],
        compiler_params=params(40),
        cost_estimate=takes(39),
        name="mlp",
    )(tens, *hbm(n2, cot, up, down), up_oth, down_oth, vecs_oth, vecs, *hbm(h1, att, rl, wo), wo_oth)


def block_out_kernel(tens, act_ref, down_own, down_oth, vecs, h1_ref, out_ref):
    units = down_own.shape[0]
    term = nn(act_ref[:, :units], down_own[...]) + nn(act_ref[:, units:], down_oth[...])
    out_ref[...] = (h1_ref[...] + term + vec(vecs, 5)).astype(BF)


def block_out(tens, act, down, down_oth, vecs, h1):
    rows = h1.shape[0]
    units = down.shape[0]
    rowblock = pl.BlockSpec((LAT, D), lambda i, *_: (i, 0))
    return pl.pallas_call(
        block_out_kernel,
        grid_spec=pltpu.PrefetchScalarGridSpec(
            num_scalar_prefetch=1,
            grid=(rows // LAT,),
            in_specs=[
                pl.BlockSpec((LAT, 2 * units), lambda i, *_: (i, 0)), whole((units, D)), whole((units, D)), vecs_spec(), rowblock,
            ],
            out_specs=[rowblock],
        ),
        out_shape=[pltpu.HBM((rows, D), BF)],
        compiler_params=params(24),
        cost_estimate=takes(7),
        name="block_out",
    )(tens, *vmem(act), down, down_oth, vecs, *hbm(h1))[0]


def back_kernel(tens, p_ref, doa_ref, qkv_ref, n1_ref, *refs, ends):
    starts, stops = ends
    dqkv_ref, dw_ref, acc = refs[-3:]
    groups = acc.shape[0]
    ones = jnp.ones((AUG, LAT), BF)
    count = p_ref.shape[1]

    @pl.when((pl.program_id(0) == 0) & (pl.program_id(1) == 0))
    def _():
        if starts:
            acc[...] = jnp.zeros_like(acc)
        else:
            acc[...] = refs[0][...]

    def part_of(t, h):
        return qkv_ref[0, 0, t, h * HD:h * HD + HD]

    def first(h):
        return tn(jnp.concatenate([part_of(2, h), ones], 0), doa_ref[0, h])

    def second(h, grad):
        return (p_ref[0, h].astype(F32) * grad).astype(BF)

    def third(h, ds):
        at = slice(h * HD, h * HD + HD)
        dqkv_ref[0, 0, 0, at] = (nn(part_of(1, h), ds) * HD**-0.5).astype(BF)
        dqkv_ref[0, 0, 1, at] = nt(part_of(0, h), ds).astype(BF)

    def values(h):
        dqkv_ref[0, 0, 2, h * HD:h * HD + HD] = nt(doa_ref[0, h, :HD], p_ref[0, h]).astype(BF)

    grads, scores = [], []
    for h in range(count + 1):
        if h < count:
            grads.append(first(h))
            values(h)
        if h >= 1:
            third(h - 1, scores.pop(0))
        if h < count:
            scores.append(second(h, grads.pop(0)))
    feats = count * HD
    group = pl.program_id(1)
    term = nn(dqkv_ref[0, 0].reshape(3 * feats, LAT), n1_ref[...])
    acc[group] += term.reshape(3, feats, D)

    @pl.when((pl.program_id(0) == pl.num_programs(0) - 1) & (pl.program_id(1) == groups - 1))
    def _():
        if not stops:
            dw_ref[...] = acc[...]
            return
        for c in range(D // 128):
            for t in range(3):
                for g in range(groups):
                    row = ((c * 3 + t) * groups + g) * feats
                    dw_ref[row:row + feats] = acc[g, t, :, c * 128:c * 128 + 128].astype(dw_ref.dtype)
        used = 12 * groups * feats
        if used < dw_ref.shape[0]:
            dw_ref[used:] = jnp.zeros((dw_ref.shape[0] - used, 128), dw_ref.dtype)


BACK_HEADS = 4


def attention_back(tens, p, doa, qkv, n1, dqkv, partial, side, first, count, total_rows):
    scenes, heads = p.shape[0], p.shape[1] // 2
    steps = heads // BACK_HEADS
    feats = BACK_HEADS * HD
    block = lambda i, j, *_: (first + i, side, 0, j, 0)
    head_block = lambda i, j, *_: (first + i, side * steps + j, 0, 0)
    ends = (first == 0, first + count == scenes)
    sums = (steps, 3, feats, D)
    zeros = lambda i, j, *_: (0, 0, 0, 0)
    carried, specs, aliases = [], [], {}
    if not ends[0]:
        carried.extend(hbm(partial))
        specs.append(pl.BlockSpec(sums, zeros, pipeline_mode=pl.Buffered(1)))
    if dqkv is not None:
        aliases = {5 + len(carried): 0}
        carried.extend(vmem(dqkv))
        specs.append(pl.BlockSpec(memory_space=pl.ANY))
    if ends[1]:
        dw = jax.ShapeDtypeStruct((total_rows, 128), BF if side else F32)
        dw_spec = pl.BlockSpec((total_rows, 128), lambda i, j, *_: (0, 0), pipeline_mode=pl.Buffered(1))
    else:
        dw = pltpu.HBM(sums, F32)
        dw_spec = pl.BlockSpec(sums, zeros, pipeline_mode=pl.Buffered(1))
    return pl.pallas_call(
        functools.partial(back_kernel, ends=ends),
        grid_spec=pltpu.PrefetchScalarGridSpec(
            num_scalar_prefetch=1,
            grid=(count, steps),
            in_specs=[
                pl.BlockSpec((1, BACK_HEADS, LAT, LAT), head_block),
                pl.BlockSpec((1, BACK_HEADS, HD + AUG, LAT), head_block),
                pl.BlockSpec((1, 1, 3, feats, LAT), block),
                pl.BlockSpec((LAT, D), lambda i, j, *_: (first + i, 0)),
            ] + specs,
            out_specs=[pl.BlockSpec((1, 1, 3, feats, LAT), block), dw_spec],
            scratch_shapes=[pltpu.VMEM(sums, F32)],
        ),
        out_shape=[pltpu.VMEM(qkv.shape, BF), dw],
        input_output_aliases=aliases,
        compiler_params=pltpu.CompilerParams(vmem_limit_bytes=24 * MIB, dimension_semantics=("arbitrary", "arbitrary")),
        cost_estimate=takes(4.5 * count),
        name="attention_back",
    )(tens, *hbm(p, doa, qkv, n1), *carried)


def norm_one_back_kernel(tens, dqkv, wq_own, wq_oth, x_ref, vecs, gh_ref, cols_two, gl_ref, cols_ref, acc):
    feats = wq_own.shape[0]
    g = tn(dqkv[0, 0].reshape(feats, LAT), wq_own[...]) + tn(dqkv[0, 1].reshape(feats, LAT), wq_oth[...])
    xh, r = normalised(x_ref[...].astype(F32))
    gl_ref[...] = gh_ref[...] + norm_back(g * vec(vecs, 0), xh, r)
    sums = jnp.concatenate([jnp.sum(v, 0, keepdims=True) for v in (g * xh, g)] + [cols_two[:4], cols_two[6:]], 0)

    @pl.when(pl.program_id(0) == 0)
    def _():
        acc[...] = sums

    @pl.when(pl.program_id(0) > 0)
    def _():
        acc[:2] += sums[:2]

    @pl.when(pl.program_id(0) == pl.num_programs(0) - 1)
    def _():
        total = acc[...]
        for c in range(D // 128):
            cols_ref[c * 8:c * 8 + 8] = total[:, c * 128:c * 128 + 128]


def norm_one_back(tens, dqkv, wq_own, wq_oth, x, vecs, gh, cols_two):
    scenes, half = dqkv.shape[0], dqkv.shape[3]
    rowblock = pl.BlockSpec((LAT, D), lambda i, *_: (i, 0))
    return pl.pallas_call(
        norm_one_back_kernel,
        grid_spec=pltpu.PrefetchScalarGridSpec(
            num_scalar_prefetch=1,
            grid=(scenes,),
            in_specs=[
                pl.BlockSpec((1, 2, 3, half, LAT), lambda i, *_: (i, 0, 0, 0, 0)),
                whole((3 * half, D)), whole((3 * half, D)),
                pl.BlockSpec((LAT, D), lambda i, tens: (tens[0] * scenes + i, 0)),
                vecs_spec(),
                rowblock,
                whole((8, D)),
            ],
            out_specs=[rowblock, whole((32, 128))],
            scratch_shapes=[pltpu.VMEM((8, D), F32)],
        ),
        out_shape=[pltpu.HBM((scenes * LAT, D), F32), jax.ShapeDtypeStruct((32, 128), F32)],
        compiler_params=params(28),
        cost_estimate=takes(10),
        name="norm_one_back",
    )(tens, *vmem(dqkv), wq_own, wq_oth, *hbm(x), vecs, *vmem(gh), cols_two)


def tie(value, *after):
    return lax.optimization_barrier((value, *after))[0]


def swap(v):
    return lax.ppermute(v, "tensor", SWAP)


class Stage:
    def __init__(self, count, bits, distances=None):
        self.count, self.bits = count, bits
        self.size = 1 << len(bits[0])
        each = list(range(1, self.size))
        self.distances = distances or (each, each)
        at = lax.axis_index("dp")
        core = lax.axis_index("tensor")

        def value(t, v):
            return sum((jnp.right_shift(v, b) & 1) << k for k, b in enumerate(bits[t]))

        self.place = jnp.where(core == 0, value(0, at), value(1, at)).astype(jnp.int32)
        met = [jnp.where(core == 0, self.distances[0][k], self.distances[1][k]) ^ self.place for k in range(self.size - 1)]
        self.scalars = jnp.stack([self.place] + met).astype(jnp.int32)

    def exchange(self, values):
        out = []
        for k, v in enumerate(values):
            pairs = []
            for i in range(self.count):
                for t in range(2):
                    d = self.distances[t][k]
                    flip = sum(((d >> j) & 1) << b for j, b in enumerate(self.bits[t]))
                    pairs.append((i * 2 + t, (i ^ flip) * 2 + t))
            out.append(lax.ppermute(v, ("dp", "tensor"), pairs))
        return out


def small_call(kernel, out_shape, name, scalars, *arrays, scratch=(), mib=16):
    return pl.pallas_call(
        kernel,
        in_specs=[pl.BlockSpec(memory_space=pltpu.SMEM)] + [pl.BlockSpec(memory_space=pltpu.VMEM)] * len(arrays),
        out_specs=[pl.BlockSpec(memory_space=pltpu.VMEM)] * len(out_shape),
        out_shape=out_shape,
        scratch_shapes=list(scratch),
        compiler_params=pltpu.CompilerParams(vmem_limit_bytes=mib * MIB),
        name=name,
    )(scalars, *arrays)


def rows_kernel(*refs):
    count = (len(refs) - 2) // 2
    ins, out, held, sem = refs[:count], refs[count], refs[count + 1:-1], refs[-1]
    copies = [pltpu.make_async_copy(r, h, sem.at[k]) for k, (r, h) in enumerate(zip(ins, held))]
    for c in copies:
        c.start()
    for c in copies:
        c.wait()
    parts = []
    for h in held:
        v = h[...].astype(F32)
        parts += [v[i:i + D].reshape(1, D) for i in range(0, v.shape[0], D)]
    out[...] = jnp.concatenate(parts + [jnp.zeros((1, D), F32)] * (out.shape[0] - len(parts)), 0)


def rows_of(*vectors):
    count = -(-sum(v.shape[0] for v in vectors) // (8 * D)) * 8
    return pl.pallas_call(
        rows_kernel,
        in_specs=[pl.BlockSpec(memory_space=pl.ANY)] * len(vectors),
        out_shape=jax.ShapeDtypeStruct((count, D), F32),
        scratch_shapes=[pltpu.VMEM(v.shape, BF) for v in vectors] + [pltpu.SemaphoreType.DMA((len(vectors),))],
        compiler_params=pltpu.CompilerParams(vmem_limit_bytes=16 * MIB),
        name="rows_of",
    )(*hbm(*vectors))


def chunk(place, m):
    return pl.ds(pl.multiple_of(place * m, 16), m)


def hand_out(total, scalars, keep_out, sends):
    m = keep_out.shape[0]
    keep_out[...] = total[chunk(scalars[0], m)]
    for k, out in enumerate(sends):
        out[...] = total[chunk(scalars[1 + k], m)].astype(BF)


def split_kernel(scalars, *refs, count):
    (keep, *recvs), (keep_out, *sends), total = refs[:count], refs[count:-1], refs[-1]
    v = keep[...]
    for r in recvs:
        v = v + r[...].astype(F32)
    total[...] = v
    hand_out(total, scalars, keep_out, sends)


def pieces(stage, rows):
    m = rows // stage.size
    return [jax.ShapeDtypeStruct((m, 128), F32)] + [jax.ShapeDtypeStruct((m, 128), BF)] * (stage.size - 1)


def split(keep, recvs, stage):
    keep, *sends = small_call(
        functools.partial(split_kernel, count=1 + len(recvs)), pieces(stage, keep.shape[0]), "split", stage.scalars, keep,
        *recvs, scratch=[pltpu.VMEM(keep.shape, F32)],
    )
    return keep, sends


def settle_kernel(scalars, keep, *refs):
    v = keep[...]
    for r in refs[:-1]:
        v = v + r[...].astype(F32)
    refs[-1][...] = v.astype(BF)


def settle(keep, recvs, stage):
    return small_call(settle_kernel, [jax.ShapeDtypeStruct(keep.shape, BF)], "settle", stage.scalars, keep, *recvs)[0]


def fill(full, scalars, own, recvs):
    m = full.shape[0] // (1 + len(recvs))
    full[chunk(scalars[0], m)] = own[:m]
    for k, r in enumerate(recvs):
        full[chunk(scalars[1 + k], m)] = r[:m]


def join_kernel(scalars, own, *refs):
    fill(refs[-1], scalars, own, refs[:-1])


def join(own, recvs, stage):
    return small_call(
        join_kernel, [jax.ShapeDtypeStruct((stage.size * own.shape[0], 128), BF)], "join", stage.scalars, own, *recvs
    )[0]


def split_mlp_kernel(scalars, own, recv, keep_out, *sends):
    m = keep_out.shape[0]
    at = chunk(scalars[0], m)
    keep_out[...] = own[at].astype(F32) + recv[at].astype(F32)
    for k, out in enumerate(sends):
        at = chunk(scalars[1 + k], m)
        out[...] = (own[at].astype(F32) + recv[at].astype(F32)).astype(BF)


def split_mlp(own, recv, stage):
    keep, *sends = small_call(
        split_mlp_kernel, pieces(stage, own.shape[0]), "split_mlp", stage.scalars, *hbm(own), recv, mib=24,
    )
    return keep, sends


def finish_mlp_kernel(scalars, *refs):
    (own, *recvs), (dup, ddown, dwo, dub), full = refs[:-5], refs[-5:-1], refs[-1]
    fill(full, scalars, own, recvs)
    units, half = dup.shape[0], dwo.shape[0]
    for c in range(D // 128):
        at = slice(c * 128, c * 128 + 128)
        dup[:, at] = full[c * units:(c + 1) * units].astype(F32)
        ddown[:, at] = full[(4 + c) * units:(5 + c) * units].astype(F32)
        dwo[:, at] = full[8 * units + c * half:8 * units + (c + 1) * half].astype(F32)
    base = 8 * units + 4 * half
    dub[...] = full[base:base + dub.shape[0]].astype(F32)


def finish_mlp(own, recvs, stage, units, half):
    return small_call(
        finish_mlp_kernel,
        [
            jax.ShapeDtypeStruct((units, D), F32), jax.ShapeDtypeStruct((units, D), F32),
            jax.ShapeDtypeStruct((half, D), F32), jax.ShapeDtypeStruct((units // 128, 128), F32),
        ],
        "finish_mlp", stage.scalars, own, *recvs, scratch=[pltpu.VMEM((stage.size * own.shape[0], 128), BF)],
    )


def parts_of(v):
    high = v.astype(BF)
    return jnp.concatenate([high, (v - high.astype(F32)).astype(BF)], 0)


def whole_of(v):
    m = v.shape[0] // 2
    return v[:m].astype(F32) + v[m:].astype(F32)


def settle_cols_kernel(scalars, keep, *refs):
    *recvs, cols, cols_recv, out = refs
    m = keep.shape[0]
    v = keep[...]
    for r in recvs:
        v = v + r[...].astype(F32)
    out[:m] = v.astype(BF)
    out[m:] = parts_of(cols[...] + cols_recv[...])


def settle_cols(keep, recvs, cols, cols_recv, stage):
    shape = (keep.shape[0] + 2 * cols.shape[0], 128)
    return small_call(
        settle_cols_kernel, [jax.ShapeDtypeStruct(shape, BF)], "settle_cols", stage.scalars, keep, *recvs, cols, cols_recv
    )[0]


def sum_cols(scalars, own, recvs, m, held):
    held[scalars[0]] = whole_of(own[m:])
    for k, r in enumerate(recvs):
        held[scalars[1 + k]] = whole_of(r[m:])
    total = held[0]
    for k in range(1, held.shape[0]):
        total = total + held[k]
    return total


def join_cols_kernel(scalars, *refs):
    (own, *recvs), out, held = refs[:-2], refs[-2], refs[-1]
    size = 1 + len(recvs)
    m = own.shape[0] - 2 * held.shape[1]
    fill(out.at[pl.ds(0, size * m)], scalars, own, recvs)
    out[size * m:] = parts_of(sum_cols(scalars, own, recvs, m, held))


def join_cols(own, recvs, stage, extra):
    m = own.shape[0] - extra
    return small_call(
        join_cols_kernel, [jax.ShapeDtypeStruct((stage.size * m + extra, 128), BF)], "join_cols", stage.scalars, own, *recvs,
        scratch=[pltpu.VMEM((stage.size, extra // 2, 128), F32)],
    )[0]


def finish_qkv_kernel(scalars, *refs):
    (own, *recvs), (out, cols), (full, held) = refs[:-4], refs[-4:-2], refs[-2:]
    m = full.shape[0] // (1 + len(recvs))
    fill(full, scalars, own, recvs)
    cols[...] = sum_cols(scalars, own, recvs, m, held)
    half = out.shape[1]
    for c in range(D // 128):
        for t in range(3):
            row = (c * 3 + t) * half
            out[t, :, c * 128:c * 128 + 128] = full[row:row + half].astype(F32)


def finish_qkv(own, recvs, stage, half, extra):
    m = own.shape[0] - extra
    return small_call(
        finish_qkv_kernel,
        [jax.ShapeDtypeStruct((3, half, D), F32), jax.ShapeDtypeStruct((extra // 2, 128), F32)],
        "finish_qkv", stage.scalars, own, *recvs,
        scratch=[pltpu.VMEM((stage.size * m, 128), BF), pltpu.VMEM((stage.size, extra // 2, 128), F32)],
    )


def advance(steps, token):
    try:
        return steps.send(token), None
    except StopIteration as end:
        return token, end.value


def body(
    latents, scene_len, attn_gain, attn_shift, qkv_weight, out_weight, out_bias, mlp_gain, mlp_shift,
    up_weight, up_bias, down_weight, down_bias, cotangent,
):
    rows = latents.shape[0] // lax.axis_size("tensor")
    units, half = up_weight.shape[0], out_weight.shape[0]
    heads = half // HD
    tens = lax.axis_index("tensor").astype(jnp.int32).reshape(1)
    count = lax.axis_size("dp")
    steps = count.bit_length() - 1
    assert 1 << steps == count and steps > 1
    lower, upper = list(range(steps - 2)), [steps - 2, steps - 1]
    turned = [b ^ 1 if b ^ 1 < steps - 2 else b for b in lower]
    group = Stage(count, (upper, upper), ([1, 2, 3], [2, 1, 3]))
    pairs = [Stage(count, ([a], [b])) for a, b in zip(lower, turned)]
    mlp_stages = pairs + [group]
    if len(lower) % 2:
        qkv_stages = mlp_stages
    else:
        qkv_stages = [
            Stage(count, (lower[i:i + 2],) * 2, ([1, 2, 3], [2, 1, 3])) for i in range(0, len(lower), 2)
        ] + [group]

    wq = qkv_weight.reshape(3 * half, D)
    wq_oth, wo_oth = swap(wq), swap(out_weight)
    vecs = rows_of(attn_gain, attn_shift, out_bias, mlp_gain, mlp_shift, down_bias, up_bias)
    vecs_oth = swap(vecs)
    up_oth, down_oth = swap(up_weight), swap(down_weight)

    n1, qkv, p, att, rl, h1, n2 = attention_forward(
        tens, scene_len, latents, vecs, wq, wq_oth, out_weight, wo_oth, rows
    )
    need = 8 * units + 4 * half + 16
    total_rows = -(-need // (16 * count)) * 16 * count
    act, gh, doa, grads_own, grads_oth, cols_two = mlp(
        tens, n2, cotangent, up_weight, down_weight, up_oth, down_oth, vecs_oth, vecs, h1, att, rl, out_weight, wo_oth, total_rows
    )
    from_peer = swap(grads_oth)

    def exchanges(stages, keep, sends, settled, joined):
        for s, stage in enumerate(stages):
            recvs = stage.exchange(sends)
            token = yield sends[-1]
            recvs = [tie(r, token) for r in recvs]
            if s + 1 < len(stages):
                keep, sends = split(keep, recvs, stages[s + 1])
            else:
                have = settled(keep, recvs, stage)
        for s in range(len(stages) - 1, -1, -1):
            recvs = stages[s].exchange([have] * (stages[s].size - 1))
            token = yield have
            recvs = [tie(r, token) for r in recvs]
            if s:
                have = joined(have, recvs, stages[s])
        return have, recvs

    qkv_rows = -(-12 * half // (16 * count)) * 16 * count
    extra = 64
    dqkv, dw, qkv_peer = None, None, None
    token = grads_oth
    chains, results = {}, {}
    cols = []

    def step(name):
        if name not in results:
            after, result = advance(chains[name], token)
            if result is not None:
                results[name] = result
            return after
        return token

    for action, *rest in PLAN:
        if action == "back":
            side, first, number = rest
            dqkv, dw = attention_back(tie(tens, token), p, doa, qkv, n1, dqkv, dw, side, first, number, qkv_rows)
            token = dw
            if side and first + number == rows // LAT:
                qkv_peer = swap(dw)
        elif action == "mlp":
            chains["mlp"] = exchanges(
                mlp_stages, *split_mlp(grads_own, tie(from_peer, token), mlp_stages[0]), settle, join
            )
            token = next(chains["mlp"])
        elif action == "qkv":
            chains["qkv"] = exchanges(
                qkv_stages, *split(tie(dw, token), [qkv_peer], qkv_stages[0]),
                lambda keep, recvs, stage: settle_cols(keep, recvs, *cols, stage),
                lambda own, recvs, stage: join_cols(own, recvs, stage, extra),
            )
            token = next(chains["qkv"])
        elif action == "norm":
            grad_latents, cols_one = norm_one_back(
                tie(tens, token), dqkv, wq, wq_oth, latents, vecs, gh, cols_two
            )
            cols.extend((cols_one, swap(cols_one)))
            token = cols_one
        elif action == "out":
            out = block_out(tie(tens, token), act, down_weight, down_oth, vecs, h1)
            token = out
        elif action == "end":
            while "mlp" not in results:
                token = step("mlp")
            have, recvs = results["mlp"]
            dup, ddown, dwo, dub = finish_mlp(tie(have, token), recvs, mlp_stages[0], units, half)
            token = dub
        else:
            token = step(action[:3])
    while "qkv" not in results:
        token = step("qkv")
    dwq, shared = finish_qkv(*results["qkv"], qkv_stages[0], half, extra)
    shared = shared.reshape(D // 128, 8, 128).transpose(1, 0, 2).reshape(8, D)
    return (
        out, grad_latents, shared[0], shared[1], dwq, dwo, shared[4],
        shared[2], shared[3], dup, dub.reshape(units), ddown, shared[5],
    )


def solution(mesh):
    placed = (
        P("dp", None), P("dp"), P(), P(), P(None, "tensor", None), P("tensor", None), P(), P(), P(),
        P("tensor", None), P("tensor"), P("tensor", None), P(), P("dp", None),
    )
    return jax.shard_map(
        body,
        mesh=mesh,
        in_specs=placed,
        out_specs=(
            P(("dp", "tensor"), None), P(("dp", "tensor"), None), P(), P(), P(None, "tensor", None),
            P("tensor", None), P(), P(), P(), P("tensor", None), P("tensor"), P("tensor", None), P(),
        ),
        check_vma=False,
    )
```

```python
import functools

import jax
import jax.numpy as jnp
from jax import lax
from jax.experimental import pallas as pl
from jax.experimental.pallas import tpu as pltpu
from jax.sharding import PartitionSpec as P

D = 512
HD = 64
LAT = 512
AUG = 16
EPS = 1e-05
LOG2E = 1.4426950408889634
NEG = -1e30
BF = jnp.bfloat16
F32 = jnp.float32
MIB = 2**20
SWAP = [(0, 1), (1, 0)]
PLAN = (
("back", 1, 0, 1), ("mlp",), ("back", 1, 1, 3), ("mlp+",), ("back", 0, 0, 2), ("mlp+",), ("back", 0, 2, 2), ("mlp+",), ("qkv",), ("norm",), ("qkv+",), ("mlp+",), ("qkv+",), ("mlp+",), ("qkv+",), ("out",), ("end",), ("qkv+",),
)


def _dot(a, b, ca, cb):
    return lax.dot_general(a, b, (((ca,), (cb,)), ((), ())), preferred_element_type=F32)


def hbm(*values):
    return tuple(pltpu.with_memory_space_constraint(v, pltpu.HBM) for v in values)


def vmem(*values):
    return tuple(pltpu.with_memory_space_constraint(v, pltpu.VMEM) for v in values)


def nn(a, b):
    return _dot(a, b, 1, 0)


def nt(a, b):
    return _dot(a, b, 1, 1)


def tn(a, b):
    return _dot(a, b, 0, 0)


def normalised(v):
    c = v - jnp.mean(v, -1, keepdims=True)
    r = lax.rsqrt(jnp.mean(c * c, -1, keepdims=True) + EPS)
    return c * r, r


def norm_back(e, xh, r):
    return r * (e - jnp.mean(e, -1, keepdims=True) - xh * jnp.mean(e * xh, -1, keepdims=True))


def forward_kernel(
    tens, lens, x_ref, vecs, wq_own, wq_oth, wo_own, wo_oth,
    n1_ref, qkv_ref, p_ref, att_ref, rl_ref, h1_ref, n2_ref, asked,
):
    scenes = pl.num_programs(0)
    length = lens[tens[0] * scenes + pl.program_id(0)]
    x = x_ref[...].astype(F32)
    n1 = (normalised(x)[0] * vec(vecs, 0) + vec(vecs, 1)).astype(BF)
    n1_ref[...] = n1
    half = wo_own.shape[0]
    heads = half // HD

    def project(side, t):
        part = nt((wq_own, wq_oth)[side][t * half:(t + 1) * half], n1)
        part = part.astype(BF)
        if t == 0:
            scaled = part.astype(F32) * (HD**-0.5 * LOG2E)
            high = scaled.astype(BF)
            at = slice(side * half, (side + 1) * half)
            asked[0, at] = high
            asked[1, at] = (scaled - high.astype(F32)).astype(BF)
            part = part * HD**-0.5
        qkv_ref[0, side, t] = part.astype(BF)

    key_at = lax.broadcasted_iota(jnp.int32, (AUG, LAT), 1)
    row_at = lax.broadcasted_iota(jnp.int32, (AUG, LAT), 0)
    bias = jnp.where((key_at >= length) & (row_at == 0), NEG, 0.0).astype(BF)
    ones = jnp.ones((AUG, LAT), BF)

    def part_of(t, h):
        return qkv_ref[0, h // heads, t, h % heads * HD:h % heads * HD + HD]

    def scores(h):
        k = part_of(1, h)
        at = slice(h * HD, h * HD + HD)
        return tn(jnp.concatenate([k, k, bias], 0), jnp.concatenate([asked[0, at], asked[1, at], ones], 0))

    def weights(h, s):
        p = jnp.exp2(s - jnp.max(s, 0, keepdims=True)).astype(BF)
        p_ref[0, h] = p
        return p

    def attend(h, p):
        o = nn(jnp.concatenate([part_of(2, h), ones], 0), p)
        rl = 1.0 / o[HD:HD + 1]
        rl_ref[0, h:h + 1] = rl
        att_ref[0, h * HD:h * HD + HD] = (o[:HD] * rl).astype(BF)

    for t in (1, 0, 2):
        project(0, t)
    scored, weighed = [], []
    total = None
    for h in range(2 * heads + 2):
        if h < 2 * heads:
            scored.append(scores(h))
        if h in (1, 2, 3):
            project(1, (1, 0, 2)[h - 1])
        if h >= 2:
            attend(h - 2, weighed.pop(0))
        if 1 <= h <= 2 * heads:
            weighed.append(weights(h - 1, scored.pop(0)))
        if h == heads + 2:
            total = tn(att_ref[0, :half], wo_own[...])
    h1 = x + (total + tn(att_ref[0, half:], wo_oth[...])) + vec(vecs, 2)
    h1_ref[...] = h1
    n2_ref[...] = (normalised(h1)[0] * vec(vecs, 3) + vec(vecs, 4)).astype(BF)


def whole(shape):
    at = (0,) * len(shape)
    return pl.BlockSpec(shape, lambda i, *_: at, pipeline_mode=pl.Buffered(1))


def takes(microseconds):
    return pl.CostEstimate(flops=int(microseconds * 1e9), bytes_accessed=0, transcendentals=0)


def params(mib):
    return pltpu.CompilerParams(vmem_limit_bytes=mib * MIB, dimension_semantics=("arbitrary",))


def vec(vecs, i):
    return vecs[i:i + 1]


def vecs_spec():
    return whole((8, D))


def attention_forward(tens, lens, x, vecs, wq_own, wq_oth, wo_own, wo_oth, rows):
    scenes = rows // LAT
    rowblock = pl.BlockSpec((LAT, D), lambda i, *_: (i, 0))
    half = wo_own.shape[0]
    return pl.pallas_call(
        forward_kernel,
        grid_spec=pltpu.PrefetchScalarGridSpec(
            num_scalar_prefetch=2,
            grid=(scenes,),
            in_specs=[
                pl.BlockSpec((LAT, D), lambda i, tens, lens: (tens[0] * scenes + i, 0)),
                vecs_spec(), whole((3 * half, D)), whole((3 * half, D)), whole((half, D)), whole((half, D)),
            ],
            out_specs=[
                rowblock,
                pl.BlockSpec((1, 2, 3, half, LAT), lambda i, *_: (i, 0, 0, 0, 0)),
                pl.BlockSpec((1, 2 * half // HD, LAT, LAT), lambda i, *_: (i, 0, 0, 0)),
                pl.BlockSpec((1, D, LAT), lambda i, *_: (i, 0, 0)),
                pl.BlockSpec((1, 2 * half // HD, LAT), lambda i, *_: (i, 0, 0)),
                rowblock,
                rowblock,
            ],
            scratch_shapes=[pltpu.VMEM((2, 2 * half, LAT), BF)],
        ),
        out_shape=[
            pltpu.HBM((rows, D), BF),
            pltpu.HBM((scenes, 2, 3, half, LAT), BF),
            pltpu.HBM((scenes, 2 * half // HD, LAT, LAT), BF),
            pltpu.HBM((scenes, D, LAT), BF),
            pltpu.HBM((scenes, 2 * half // HD, LAT), F32),
            pltpu.HBM((rows, D), F32),
            pltpu.HBM((rows, D), BF),
        ],
        compiler_params=params(40),
        cost_estimate=takes(23),
        name="attention_forward",
    )(tens, *hbm(lens, x), vecs, *hbm(wq_own), wq_oth, *hbm(wo_own), wo_oth)


SUB = 256


def gelu_parts(z):
    cdf = 0.5 + 0.5 * lax.erf(z * 0.7071067811865476)
    return z * cdf, cdf + z * (0.3989422804014327 * jnp.exp2(z * z * (-0.5 * LOG2E)))


def put_slabs(out, at, values):
    n = values.shape[0]
    for c in range(D // 128):
        out[at + c * n:at + (c + 1) * n] = values[:, c * 128:c * 128 + 128].astype(out.dtype)


def put_row(out, at, row, count):
    parts = [row[:, c * 128:c * 128 + 128] for c in range(row.shape[1] // 128)]
    parts += [jnp.zeros((1, 128), F32)] * (count - len(parts))
    out[at:at + count] = jnp.concatenate(parts, 0).astype(out.dtype)


def mlp_kernel(
    tens, n2_ref, cot_ref, up_own, down_own, up_oth, down_oth, vecs_oth, vecs, h1_ref, att_ref, rl_ref, wo_own, wo_oth,
    act_ref, gh_ref, doa_ref, own_ref, oth_ref, cols_ref, dub_ref, acc_up, acc_down, acc_ub, acc_wo,
):
    @pl.when(pl.program_id(0) == 0)
    def _():
        acc_up[...] = jnp.zeros_like(acc_up)
        acc_down[...] = jnp.zeros_like(acc_down)
        acc_ub[...] = jnp.zeros_like(acc_ub)
        acc_wo[...] = jnp.zeros_like(acc_wo)
        cols_ref[...] = jnp.zeros_like(cols_ref)

    n2, cot = n2_ref[...], cot_ref[...]
    units = up_own.shape[0]
    per = units // SUB

    def place(j):
        side, at = divmod(j, per)
        ups, downs, rows = ((up_own, down_own, vecs), (up_oth, down_oth, vecs_oth))[side]
        at = slice(at * SUB, at * SUB + SUB)
        first = at.start // D
        return ups[at], downs[at], vec(rows, 6 + first)[:, at.start - first * D:at.stop - first * D]

    def before(j):
        u, d, b = place(j)
        return nt(n2, u) + b, nt(cot, d)

    def between(pre, grad_act):
        act, slope = gelu_parts(pre)
        return act.astype(BF), (grad_act * slope).astype(BF)

    def after(j, act, dpre):
        u, _, _ = place(j)
        at = slice(j * SUB, j * SUB + SUB)
        act_ref[:, at] = act
        acc_down[at] += tn(act, cot)
        acc_up[at] += tn(dpre, n2)
        acc_ub[:, at] += jnp.sum(dpre.astype(F32), 0, keepdims=True)
        return nn(dpre, u)

    back = 0.0
    first, second = [], []
    for j in range(2 * per + 2):
        if j < 2 * per:
            first.append(before(j))
        if j >= 2:
            back += after(j - 2, *second.pop(0))
        if 1 <= j <= 2 * per:
            second.append(between(*first.pop(0)))
    xh, r = normalised(h1_ref[...])
    cot32 = cot.astype(F32)
    gh = cot32 + norm_back(back * vec(vecs, 3), xh, r)
    gh_ref[...] = gh
    gb = gh.astype(BF)
    half = wo_own.shape[0]
    heads = half // HD
    zeros = jnp.zeros((AUG - 3, LAT), F32)
    for side, w in enumerate((wo_own, wo_oth)):
        do = nt(w[...], gb)
        for h in range(heads):
            hh = side * heads + h
            scaled = (do[h * HD:h * HD + HD] * rl_ref[0, hh:hh + 1]).astype(BF)
            doa_ref[0, hh, :HD] = scaled
            delta = -jnp.sum(scaled.astype(F32) * att_ref[0, hh * HD:hh * HD + HD].astype(F32), 0, keepdims=True)
            high = delta.astype(BF).astype(F32)
            low = (delta - high).astype(BF).astype(F32)
            doa_ref[0, hh, HD:] = jnp.concatenate([high, low, delta - high - low, zeros], 0).astype(BF)
    acc_wo[...] += nn(att_ref[0], gb)
    cols_ref[...] += jnp.concatenate(
        [jnp.sum(v, 0, keepdims=True) for v in (back * xh, back, gh, cot32)] + [jnp.zeros((4, D), F32)], 0
    )

    @pl.when(pl.program_id(0) == pl.num_programs(0) - 1)
    def _():
        base = 8 * units + 4 * half
        for side, ref in enumerate((own_ref, oth_ref)):
            put_slabs(ref, 0, acc_up.at[side * units:(side + 1) * units])
            put_slabs(ref, 4 * units, acc_down.at[side * units:(side + 1) * units])
            put_slabs(ref, 8 * units, acc_wo.at[side * half:(side + 1) * half])
            if ref.shape[0] > base:
                ref[base:] = jnp.zeros((ref.shape[0] - base, 128), ref.dtype)
        put_row(dub_ref, 0, acc_ub, dub_ref.shape[0])


def mlp(tens, n2, cot, up, down, up_oth, down_oth, vecs_oth, vecs, h1, att, rl, wo, wo_oth, total_rows):
    rows = n2.shape[0]
    scenes = rows // LAT
    units, half = up.shape[0], wo.shape[0]
    heads = 2 * half // HD
    rowblock = pl.BlockSpec((LAT, D), lambda i, *_: (i, 0))
    weights = whole((units, D))
    return pl.pallas_call(
        mlp_kernel,
        grid_spec=pltpu.PrefetchScalarGridSpec(
            num_scalar_prefetch=1,
            grid=(scenes,),
            in_specs=[
                rowblock,
                pl.BlockSpec((LAT, D), lambda i, tens: (tens[0] * scenes + i, 0)),
                weights, weights, weights, weights, vecs_spec(), vecs_spec(), rowblock,
                pl.BlockSpec((1, D, LAT), lambda i, *_: (i, 0, 0)),
                pl.BlockSpec((1, heads, LAT), lambda i, *_: (i, 0, 0)),
                whole((half, D)), whole((half, D)),
            ],
            out_specs=[
                pl.BlockSpec((LAT, 2 * units), lambda i, *_: (i, 0)), rowblock,
                pl.BlockSpec((1, heads, HD + AUG, LAT), lambda i, *_: (i, 0, 0, 0)),
                whole((total_rows, 128)), whole((total_rows, 128)), whole((8, D)), whole((2 * units // 128, 128)),
            ],
            scratch_shapes=[
                pltpu.VMEM((2 * units, D), F32), pltpu.VMEM((2 * units, D), F32), pltpu.VMEM((1, 2 * units), F32),
                pltpu.VMEM((2 * half, D), F32),
            ],
        ),
        out_shape=[
            pltpu.HBM((rows, 2 * units), BF),
            pltpu.HBM((rows, D), F32),
            pltpu.HBM((scenes, heads, HD + AUG, LAT), BF),
            pltpu.HBM((total_rows, 128), BF),
            pltpu.HBM((total_rows, 128), BF),
            pltpu.HBM((8, D), F32),
            pltpu.HBM((2 * units // 128, 128), F32),
        ],
        compiler_params=params(40),
        cost_estimate=takes(39),
        name="mlp",
    )(tens, *hbm(n2, cot, up, down), up_oth, down_oth, vecs_oth, vecs, *hbm(h1, att, rl, wo), wo_oth)


def block_out_kernel(tens, act_ref, down_own, down_oth, vecs, h1_ref, out_ref):
    units = down_own.shape[0]
    term = nn(act_ref[:, :units], down_own[...]) + nn(act_ref[:, units:], down_oth[...])
    out_ref[...] = (h1_ref[...] + term + vec(vecs, 5)).astype(BF)


def block_out(tens, act, down, down_oth, vecs, h1):
    rows = h1.shape[0]
    units = down.shape[0]
    rowblock = pl.BlockSpec((LAT, D), lambda i, *_: (i, 0))
    return pl.pallas_call(
        block_out_kernel,
        grid_spec=pltpu.PrefetchScalarGridSpec(
            num_scalar_prefetch=1,
            grid=(rows // LAT,),
            in_specs=[
                pl.BlockSpec((LAT, 2 * units), lambda i, *_: (i, 0)), whole((units, D)), whole((units, D)), vecs_spec(), rowblock,
            ],
            out_specs=[rowblock],
        ),
        out_shape=[pltpu.HBM((rows, D), BF)],
        compiler_params=params(24),
        cost_estimate=takes(7),
        name="block_out",
    )(tens, *vmem(act), down, down_oth, vecs, *hbm(h1))[0]


def back_kernel(tens, p_ref, doa_ref, qkv_ref, n1_ref, *refs, ends):
    starts, stops = ends
    dqkv_ref, dw_ref, acc = refs[-3:]
    groups = acc.shape[0]
    ones = jnp.ones((AUG, LAT), BF)
    count = p_ref.shape[1]

    @pl.when((pl.program_id(0) == 0) & (pl.program_id(1) == 0))
    def _():
        if starts:
            acc[...] = jnp.zeros_like(acc)
        else:
            acc[...] = refs[0][...]

    def part_of(t, h):
        return qkv_ref[0, 0, t, h * HD:h * HD + HD]

    def first(h):
        return tn(jnp.concatenate([part_of(2, h), ones], 0), doa_ref[0, h])

    def second(h, grad):
        return (p_ref[0, h].astype(F32) * grad).astype(BF)

    def third(h, ds):
        at = slice(h * HD, h * HD + HD)
        dqkv_ref[0, 0, 0, at] = (nn(part_of(1, h), ds) * HD**-0.5).astype(BF)
        dqkv_ref[0, 0, 1, at] = nt(part_of(0, h), ds).astype(BF)

    def values(h):
        dqkv_ref[0, 0, 2, h * HD:h * HD + HD] = nt(doa_ref[0, h, :HD], p_ref[0, h]).astype(BF)

    grads, scores = [], []
    for h in range(count + 1):
        if h < count:
            grads.append(first(h))
            values(h)
        if h >= 1:
            third(h - 1, scores.pop(0))
        if h < count:
            scores.append(second(h, grads.pop(0)))
    feats = count * HD
    group = pl.program_id(1)
    term = nn(dqkv_ref[0, 0].reshape(3 * feats, LAT), n1_ref[...])
    acc[group] += term.reshape(3, feats, D)

    @pl.when((pl.program_id(0) == pl.num_programs(0) - 1) & (pl.program_id(1) == groups - 1))
    def _():
        if not stops:
            dw_ref[...] = acc[...]
            return
        for c in range(D // 128):
            for t in range(3):
                for g in range(groups):
                    row = ((c * 3 + t) * groups + g) * feats
                    dw_ref[row:row + feats] = acc[g, t, :, c * 128:c * 128 + 128].astype(dw_ref.dtype)
        used = 12 * groups * feats
        if used < dw_ref.shape[0]:
            dw_ref[used:] = jnp.zeros((dw_ref.shape[0] - used, 128), dw_ref.dtype)


BACK_HEADS = 4


def attention_back(tens, p, doa, qkv, n1, dqkv, partial, side, first, count, total_rows):
    scenes, heads = p.shape[0], p.shape[1] // 2
    steps = heads // BACK_HEADS
    feats = BACK_HEADS * HD
    block = lambda i, j, *_: (first + i, side, 0, j, 0)
    head_block = lambda i, j, *_: (first + i, side * steps + j, 0, 0)
    ends = (first == 0, first + count == scenes)
    sums = (steps, 3, feats, D)
    zeros = lambda i, j, *_: (0, 0, 0, 0)
    carried, specs, aliases = [], [], {}
    if not ends[0]:
        carried.extend(hbm(partial))
        specs.append(pl.BlockSpec(sums, zeros, pipeline_mode=pl.Buffered(1)))
    if dqkv is not None:
        aliases = {5 + len(carried): 0}
        carried.extend(vmem(dqkv))
        specs.append(pl.BlockSpec(memory_space=pl.ANY))
    if ends[1]:
        dw = jax.ShapeDtypeStruct((total_rows, 128), BF if side else F32)
        dw_spec = pl.BlockSpec((total_rows, 128), lambda i, j, *_: (0, 0), pipeline_mode=pl.Buffered(1))
    else:
        dw = pltpu.HBM(sums, F32)
        dw_spec = pl.BlockSpec(sums, zeros, pipeline_mode=pl.Buffered(1))
    return pl.pallas_call(
        functools.partial(back_kernel, ends=ends),
        grid_spec=pltpu.PrefetchScalarGridSpec(
            num_scalar_prefetch=1,
            grid=(count, steps),
            in_specs=[
                pl.BlockSpec((1, BACK_HEADS, LAT, LAT), head_block),
                pl.BlockSpec((1, BACK_HEADS, HD + AUG, LAT), head_block),
                pl.BlockSpec((1, 1, 3, feats, LAT), block),
                pl.BlockSpec((LAT, D), lambda i, j, *_: (first + i, 0)),
            ] + specs,
            out_specs=[pl.BlockSpec((1, 1, 3, feats, LAT), block), dw_spec],
            scratch_shapes=[pltpu.VMEM(sums, F32)],
        ),
        out_shape=[pltpu.VMEM(qkv.shape, BF), dw],
        input_output_aliases=aliases,
        compiler_params=pltpu.CompilerParams(vmem_limit_bytes=24 * MIB, dimension_semantics=("arbitrary", "arbitrary")),
        cost_estimate=takes(4.5 * count),
        name="attention_back",
    )(tens, *hbm(p, doa, qkv, n1), *carried)


def norm_one_back_kernel(tens, dqkv, wq_own, wq_oth, x_ref, vecs, gh_ref, cols_two, dub, gl_ref, cols_ref, give_ref, acc):
    feats = wq_own.shape[0]
    g = tn(dqkv[0, 0].reshape(feats, LAT), wq_own[...]) + tn(dqkv[0, 1].reshape(feats, LAT), wq_oth[...])
    xh, r = normalised(x_ref[...].astype(F32))
    gl_ref[...] = gh_ref[...] + norm_back(g * vec(vecs, 0), xh, r)
    sums = jnp.concatenate([jnp.sum(v, 0, keepdims=True) for v in (g * xh, g)] + [cols_two[:4], cols_two[6:]], 0)

    @pl.when(pl.program_id(0) == 0)
    def _():
        acc[...] = sums

    @pl.when(pl.program_id(0) > 0)
    def _():
        acc[:2] += sums[:2]

    @pl.when(pl.program_id(0) == pl.num_programs(0) - 1)
    def _():
        total = acc[...]
        units = dub.shape[0] // 2
        for ref, at in ((cols_ref, 0), (give_ref, units)):
            for c in range(D // 128):
                ref[c * 8:c * 8 + 8] = total[:, c * 128:c * 128 + 128]
            ref[32:] = dub[at:at + units]


def norm_one_back(tens, dqkv, wq_own, wq_oth, x, vecs, gh, cols_two, dub):
    cols = (4 * 8 + dub.shape[0] // 2, 128)
    scenes, half = dqkv.shape[0], dqkv.shape[3]
    rowblock = pl.BlockSpec((LAT, D), lambda i, *_: (i, 0))
    return pl.pallas_call(
        norm_one_back_kernel,
        grid_spec=pltpu.PrefetchScalarGridSpec(
            num_scalar_prefetch=1,
            grid=(scenes,),
            in_specs=[
                pl.BlockSpec((1, 2, 3, half, LAT), lambda i, *_: (i, 0, 0, 0, 0)),
                whole((3 * half, D)), whole((3 * half, D)),
                pl.BlockSpec((LAT, D), lambda i, tens: (tens[0] * scenes + i, 0)),
                vecs_spec(),
                rowblock,
                whole((8, D)), whole(dub.shape),
            ],
            out_specs=[rowblock, whole(cols), whole(cols)],
            scratch_shapes=[pltpu.VMEM((8, D), F32)],
        ),
        out_shape=[pltpu.HBM((scenes * LAT, D), F32), jax.ShapeDtypeStruct(cols, F32), jax.ShapeDtypeStruct(cols, F32)],
        compiler_params=params(28),
        cost_estimate=takes(10),
        name="norm_one_back",
    )(tens, *vmem(dqkv), wq_own, wq_oth, *hbm(x), vecs, *vmem(gh), cols_two, dub)


def tie(value, *after):
    return lax.optimization_barrier((value, *after))[0]


def swap(v):
    return lax.ppermute(v, "tensor", SWAP)


class Stage:
    def __init__(self, count, bits, distances=None):
        self.count, self.bits = count, bits
        self.size = 1 << len(bits[0])
        each = list(range(1, self.size))
        self.distances = distances or (each, each)
        at = lax.axis_index("dp")
        core = lax.axis_index("tensor")

        def value(t, v):
            return sum((jnp.right_shift(v, b) & 1) << k for k, b in enumerate(bits[t]))

        self.place = jnp.where(core == 0, value(0, at), value(1, at)).astype(jnp.int32)
        met = [jnp.where(core == 0, self.distances[0][k], self.distances[1][k]) ^ self.place for k in range(self.size - 1)]
        self.scalars = jnp.stack([self.place] + met).astype(jnp.int32)

    def exchange(self, values):
        out = []
        for k, v in enumerate(values):
            pairs = []
            for i in range(self.count):
                for t in range(2):
                    d = self.distances[t][k]
                    flip = sum(((d >> j) & 1) << b for j, b in enumerate(self.bits[t]))
                    pairs.append((i * 2 + t, (i ^ flip) * 2 + t))
            out.append(lax.ppermute(v, ("dp", "tensor"), pairs))
        return out


def small_call(kernel, out_shape, name, scalars, *arrays, scratch=(), mib=16):
    return pl.pallas_call(
        kernel,
        in_specs=[pl.BlockSpec(memory_space=pltpu.SMEM)] + [pl.BlockSpec(memory_space=pltpu.VMEM)] * len(arrays),
        out_specs=[pl.BlockSpec(memory_space=pltpu.VMEM)] * len(out_shape),
        out_shape=out_shape,
        scratch_shapes=list(scratch),
        compiler_params=pltpu.CompilerParams(vmem_limit_bytes=mib * MIB),
        cost_estimate=takes(0.5),
        name=name,
    )(scalars, *arrays)


def rows_kernel(*refs):
    count = (len(refs) - 2) // 2
    ins, out, held, sem = refs[:count], refs[count], refs[count + 1:-1], refs[-1]
    copies = [pltpu.make_async_copy(r, h, sem.at[k]) for k, (r, h) in enumerate(zip(ins, held))]
    for c in copies:
        c.start()
    for c in copies:
        c.wait()
    parts = []
    for h in held:
        v = h[...].astype(F32)
        parts += [v[i:i + D].reshape(1, D) for i in range(0, v.shape[0], D)]
    out[...] = jnp.concatenate(parts + [jnp.zeros((1, D), F32)] * (out.shape[0] - len(parts)), 0)


def rows_of(*vectors):
    count = -(-sum(v.shape[0] for v in vectors) // (8 * D)) * 8
    return pl.pallas_call(
        rows_kernel,
        in_specs=[pl.BlockSpec(memory_space=pl.ANY)] * len(vectors),
        out_shape=jax.ShapeDtypeStruct((count, D), F32),
        scratch_shapes=[pltpu.VMEM(v.shape, BF) for v in vectors] + [pltpu.SemaphoreType.DMA((len(vectors),))],
        compiler_params=pltpu.CompilerParams(vmem_limit_bytes=16 * MIB),
        name="rows_of",
    )(*hbm(*vectors))


def chunk(place, m):
    return pl.ds(pl.multiple_of(place * m, 16), m)


def hand_out(total, scalars, keep_out, sends):
    m = keep_out.shape[0]
    keep_out[...] = total[chunk(scalars[0], m)]
    for k, out in enumerate(sends):
        out[...] = total[chunk(scalars[1 + k], m)].astype(BF)


def split_kernel(scalars, *refs, count):
    (keep, *recvs), (keep_out, *sends), total = refs[:count], refs[count:-1], refs[-1]
    v = keep[...]
    for r in recvs:
        v = v + r[...].astype(F32)
    total[...] = v
    hand_out(total, scalars, keep_out, sends)


def pieces(stage, rows):
    m = rows // stage.size
    return [jax.ShapeDtypeStruct((m, 128), F32)] + [jax.ShapeDtypeStruct((m, 128), BF)] * (stage.size - 1)


def split(keep, recvs, stage):
    keep, *sends = small_call(
        functools.partial(split_kernel, count=1 + len(recvs)), pieces(stage, keep.shape[0]), "split", stage.scalars, keep,
        *recvs, scratch=[pltpu.VMEM(keep.shape, F32)],
    )
    return keep, sends


def settle_kernel(scalars, keep, *refs):
    v = keep[...]
    for r in refs[:-1]:
        v = v + r[...].astype(F32)
    refs[-1][...] = v.astype(BF)


def settle(keep, recvs, stage):
    return small_call(settle_kernel, [jax.ShapeDtypeStruct(keep.shape, BF)], "settle", stage.scalars, keep, *recvs)[0]


def fill(full, scalars, own, recvs):
    m = full.shape[0] // (1 + len(recvs))
    full[chunk(scalars[0], m)] = own[:m]
    for k, r in enumerate(recvs):
        full[chunk(scalars[1 + k], m)] = r[:m]


def join_kernel(scalars, own, *refs):
    fill(refs[-1], scalars, own, refs[:-1])


def join(own, recvs, stage):
    return small_call(
        join_kernel, [jax.ShapeDtypeStruct((stage.size * own.shape[0], 128), BF)], "join", stage.scalars, own, *recvs
    )[0]


def split_mlp_kernel(scalars, own, recv, keep_out, *sends):
    m = keep_out.shape[0]
    at = chunk(scalars[0], m)
    keep_out[...] = own[at].astype(F32) + recv[at].astype(F32)
    for k, out in enumerate(sends):
        at = chunk(scalars[1 + k], m)
        out[...] = (own[at].astype(F32) + recv[at].astype(F32)).astype(BF)


def split_mlp(own, recv, stage):
    keep, *sends = small_call(
        split_mlp_kernel, pieces(stage, own.shape[0]), "split_mlp", stage.scalars, *hbm(own), recv, mib=24,
    )
    return keep, sends


def finish_mlp_kernel(scalars, *refs):
    (own, *recvs), (dup, ddown, dwo), full = refs[:-4], refs[-4:-1], refs[-1]
    fill(full, scalars, own, recvs)
    units, half = dup.shape[0], dwo.shape[0]
    for c in range(D // 128):
        at = slice(c * 128, c * 128 + 128)
        dup[:, at] = full[c * units:(c + 1) * units].astype(F32)
        ddown[:, at] = full[(4 + c) * units:(5 + c) * units].astype(F32)
        dwo[:, at] = full[8 * units + c * half:8 * units + (c + 1) * half].astype(F32)


def finish_mlp(own, recvs, stage, units, half):
    return small_call(
        finish_mlp_kernel,
        [
            jax.ShapeDtypeStruct((units, D), F32), jax.ShapeDtypeStruct((units, D), F32),
            jax.ShapeDtypeStruct((half, D), F32),
        ],
        "finish_mlp", stage.scalars, own, *recvs, scratch=[pltpu.VMEM((stage.size * own.shape[0], 128), BF)],
    )


def parts_of(v):
    high = v.astype(BF)
    return jnp.concatenate([high, (v - high.astype(F32)).astype(BF)], 0)


def whole_of(v):
    m = v.shape[0] // 2
    return v[:m].astype(F32) + v[m:].astype(F32)


def settle_cols_kernel(scalars, keep, *refs):
    *recvs, cols, cols_recv, out = refs
    m = keep.shape[0]
    v = keep[...]
    for r in recvs:
        v = v + r[...].astype(F32)
    out[:m] = v.astype(BF)
    out[m:] = parts_of(cols[...] + cols_recv[...])


def settle_cols(keep, recvs, cols, cols_recv, stage):
    shape = (keep.shape[0] + 2 * cols.shape[0], 128)
    return small_call(
        settle_cols_kernel, [jax.ShapeDtypeStruct(shape, BF)], "settle_cols", stage.scalars, keep, *recvs, cols, cols_recv
    )[0]


def sum_cols(scalars, own, recvs, m, held):
    held[scalars[0]] = whole_of(own[m:])
    for k, r in enumerate(recvs):
        held[scalars[1 + k]] = whole_of(r[m:])
    total = held[0]
    for k in range(1, held.shape[0]):
        total = total + held[k]
    return total


def join_cols_kernel(scalars, *refs):
    (own, *recvs), out, held = refs[:-2], refs[-2], refs[-1]
    size = 1 + len(recvs)
    m = own.shape[0] - 2 * held.shape[1]
    fill(out.at[pl.ds(0, size * m)], scalars, own, recvs)
    out[size * m:] = parts_of(sum_cols(scalars, own, recvs, m, held))


def join_cols(own, recvs, stage, extra):
    m = own.shape[0] - extra
    return small_call(
        join_cols_kernel, [jax.ShapeDtypeStruct((stage.size * m + extra, 128), BF)], "join_cols", stage.scalars, own, *recvs,
        scratch=[pltpu.VMEM((stage.size, extra // 2, 128), F32)],
    )[0]


def finish_qkv_kernel(scalars, *refs):
    (own, *recvs), (out, cols), (full, held) = refs[:-4], refs[-4:-2], refs[-2:]
    m = full.shape[0] // (1 + len(recvs))
    fill(full, scalars, own, recvs)
    cols[...] = sum_cols(scalars, own, recvs, m, held)
    half = out.shape[1]
    for c in range(D // 128):
        for t in range(3):
            row = (c * 3 + t) * half
            out[t, :, c * 128:c * 128 + 128] = full[row:row + half].astype(F32)


def finish_qkv(own, recvs, stage, half, extra):
    m = own.shape[0] - extra
    return small_call(
        finish_qkv_kernel,
        [jax.ShapeDtypeStruct((3, half, D), F32), jax.ShapeDtypeStruct((extra // 2, 128), F32)],
        "finish_qkv", stage.scalars, own, *recvs,
        scratch=[pltpu.VMEM((stage.size * m, 128), BF), pltpu.VMEM((stage.size, extra // 2, 128), F32)],
    )


def advance(steps, token):
    try:
        return steps.send(token), None
    except StopIteration as end:
        return token, end.value


def body(
    latents, scene_len, attn_gain, attn_shift, qkv_weight, out_weight, out_bias, mlp_gain, mlp_shift,
    up_weight, up_bias, down_weight, down_bias, cotangent,
):
    rows = latents.shape[0] // lax.axis_size("tensor")
    units, half = up_weight.shape[0], out_weight.shape[0]
    heads = half // HD
    tens = lax.axis_index("tensor").astype(jnp.int32).reshape(1)
    count = lax.axis_size("dp")
    steps = count.bit_length() - 1
    assert 1 << steps == count and steps > 1
    lower, upper = list(range(steps - 2)), [steps - 2, steps - 1]
    turned = [b ^ 1 if b ^ 1 < steps - 2 else b for b in lower]
    group = Stage(count, (upper, upper), ([1, 2, 3], [2, 1, 3]))
    pairs = [Stage(count, ([a], [b])) for a, b in zip(lower, turned)]
    mlp_stages = pairs + [group]
    if len(lower) % 2:
        qkv_stages = mlp_stages
    else:
        qkv_stages = [
            Stage(count, (lower[i:i + 2],) * 2, ([1, 2, 3], [2, 1, 3])) for i in range(0, len(lower), 2)
        ] + [group]

    wq = qkv_weight.reshape(3 * half, D)
    wq_oth, wo_oth = swap(wq), swap(out_weight)
    vecs = rows_of(attn_gain, attn_shift, out_bias, mlp_gain, mlp_shift, down_bias, up_bias)
    vecs_oth = swap(vecs)
    up_oth, down_oth = swap(up_weight), swap(down_weight)

    n1, qkv, p, att, rl, h1, n2 = attention_forward(
        tens, scene_len, latents, vecs, wq, wq_oth, out_weight, wo_oth, rows
    )
    need = 8 * units + 4 * half
    total_rows = -(-need // (16 * count)) * 16 * count
    act, gh, doa, grads_own, grads_oth, cols_two, grad_ub = mlp(
        tens, n2, cotangent, up_weight, down_weight, up_oth, down_oth, vecs_oth, vecs, h1, att, rl, out_weight, wo_oth, total_rows
    )
    from_peer = swap(grads_oth)

    def exchanges(stages, keep, sends, settled, joined):
        for s, stage in enumerate(stages):
            recvs = stage.exchange(sends)
            token = yield sends[-1]
            recvs = [tie(r, token) for r in recvs]
            if s + 1 < len(stages):
                keep, sends = split(keep, recvs, stages[s + 1])
            else:
                have = settled(keep, recvs, stage)
        for s in range(len(stages) - 1, -1, -1):
            recvs = stages[s].exchange([have] * (stages[s].size - 1))
            token = yield have
            recvs = [tie(r, token) for r in recvs]
            if s:
                have = joined(have, recvs, stages[s])
        return have, recvs

    qkv_rows = -(-12 * half // (16 * count)) * 16 * count
    extra = 2 * (4 * 8 + units // 128)
    dqkv, dw, qkv_peer = None, None, None
    token = grads_oth
    chains, results = {}, {}
    cols = []

    def step(name):
        if name not in results:
            after, result = advance(chains[name], token)
            if result is not None:
                results[name] = result
            return after
        return token

    for action, *rest in PLAN:
        if action == "back":
            side, first, number = rest
            dqkv, dw = attention_back(tie(tens, token), p, doa, qkv, n1, dqkv, dw, side, first, number, qkv_rows)
            token = dw
            if side and first + number == rows // LAT:
                qkv_peer = swap(dw)
        elif action == "mlp":
            chains["mlp"] = exchanges(
                mlp_stages, *split_mlp(grads_own, tie(from_peer, token), mlp_stages[0]), settle, join
            )
            token = next(chains["mlp"])
        elif action == "qkv":
            chains["qkv"] = exchanges(
                qkv_stages, *split(tie(dw, token), [qkv_peer], qkv_stages[0]),
                lambda keep, recvs, stage: settle_cols(keep, recvs, *cols, stage),
                lambda own, recvs, stage: join_cols(own, recvs, stage, extra),
            )
            token = next(chains["qkv"])
        elif action == "norm":
            grad_latents, cols_one, cols_give = norm_one_back(
                tie(tens, token), dqkv, wq, wq_oth, latents, vecs, gh, cols_two, grad_ub
            )
            cols.extend((cols_one, swap(cols_give)))
            token = cols_one
        elif action == "out":
            out = block_out(tie(tens, token), act, down_weight, down_oth, vecs, h1)
            token = out
        elif action == "end":
            while "mlp" not in results:
                token = step("mlp")
            have, recvs = results["mlp"]
            dup, ddown, dwo = finish_mlp(tie(have, token), recvs, mlp_stages[0], units, half)
            token = dwo
        else:
            token = step(action[:3])
    while "qkv" not in results:
        token = step("qkv")
    dwq, shared = finish_qkv(*results["qkv"], qkv_stages[0], half, extra)
    dub = shared[32:]
    shared = shared[:32].reshape(D // 128, 8, 128).transpose(1, 0, 2).reshape(8, D)
    return (
        out, grad_latents, shared[0], shared[1], dwq, dwo, shared[4],
        shared[2], shared[3], dup, dub.reshape(units), ddown, shared[5],
    )


def solution(mesh):
    placed = (
        P("dp", None), P("dp"), P(), P(), P(None, "tensor", None), P("tensor", None), P(), P(), P(),
        P("tensor", None), P("tensor"), P("tensor", None), P(), P("dp", None),
    )
    return jax.shard_map(
        body,
        mesh=mesh,
        in_specs=placed,
        out_specs=(
            P(("dp", "tensor"), None), P(("dp", "tensor"), None), P(), P(), P(None, "tensor", None),
            P("tensor", None), P(), P(), P(), P("tensor", None), P("tensor"), P("tensor", None), P(),
        ),
        check_vma=False,
    )
```

```python
import functools

import jax
import jax.numpy as jnp
from jax import lax
from jax.experimental import pallas as pl
from jax.experimental.pallas import tpu as pltpu
from jax.sharding import PartitionSpec as P

D = 512
HD = 64
LAT = 512
AUG = 16
EPS = 1e-05
LOG2E = 1.4426950408889634
NEG = -1e30
BF = jnp.bfloat16
F32 = jnp.float32
MIB = 2**20
SWAP = [(0, 1), (1, 0)]
PLAN = (
("back", 1, 0, 1), ("mlp",), ("back", 1, 1, 3), ("mlp+",), ("back", 0, 0, 2), ("mlp+",), ("back", 0, 2, 2), ("mlp+",), ("qkv",), ("norm",), ("qkv+",), ("mlp+",), ("qkv+",), ("mlp+",), ("qkv+",), ("out",), ("end",), ("qkv+",),
)


def _dot(a, b, ca, cb):
    return lax.dot_general(a, b, (((ca,), (cb,)), ((), ())), preferred_element_type=F32)


def hbm(*values):
    return tuple(pltpu.with_memory_space_constraint(v, pltpu.HBM) for v in values)


def vmem(*values):
    return tuple(pltpu.with_memory_space_constraint(v, pltpu.VMEM) for v in values)


def nn(a, b):
    return _dot(a, b, 1, 0)


def nt(a, b):
    return _dot(a, b, 1, 1)


def tn(a, b):
    return _dot(a, b, 0, 0)


def normalised(v):
    c = v - jnp.mean(v, -1, keepdims=True)
    r = lax.rsqrt(jnp.mean(c * c, -1, keepdims=True) + EPS)
    return c * r, r


def norm_back(e, xh, r):
    return r * (e - jnp.mean(e, -1, keepdims=True) - xh * jnp.mean(e * xh, -1, keepdims=True))


def forward_kernel(
    tens, lens, x_ref, vecs, wq_own, wq_oth, wo_own, wo_oth,
    n1_ref, qkv_ref, p_ref, att_ref, rl_ref, h1_ref, n2_ref, asked,
):
    scenes = pl.num_programs(0)
    length = lens[tens[0] * scenes + pl.program_id(0)]
    x = x_ref[...].astype(F32)
    n1 = (normalised(x)[0] * vec(vecs, 0) + vec(vecs, 1)).astype(BF)
    n1_ref[...] = n1
    half = wo_own.shape[0]
    heads = half // HD

    def project(side, t):
        part = nt((wq_own, wq_oth)[side][t * half:(t + 1) * half], n1)
        part = part.astype(BF)
        if t == 0:
            scaled = part.astype(F32) * (HD**-0.5 * LOG2E)
            high = scaled.astype(BF)
            at = slice(side * half, (side + 1) * half)
            asked[0, at] = high
            asked[1, at] = (scaled - high.astype(F32)).astype(BF)
            part = part * HD**-0.5
        qkv_ref[0, side, t] = part.astype(BF)

    key_at = lax.broadcasted_iota(jnp.int32, (AUG, LAT), 1)
    row_at = lax.broadcasted_iota(jnp.int32, (AUG, LAT), 0)
    bias = jnp.where((key_at >= length) & (row_at == 0), NEG, 0.0).astype(BF)
    ones = jnp.ones((AUG, LAT), BF)

    def part_of(t, h):
        return qkv_ref[0, h // heads, t, h % heads * HD:h % heads * HD + HD]

    def scores(h):
        k = part_of(1, h)
        at = slice(h * HD, h * HD + HD)
        return tn(jnp.concatenate([k, k, bias], 0), jnp.concatenate([asked[0, at], asked[1, at], ones], 0))

    def weights(h, s):
        p = jnp.exp2(s - jnp.max(s, 0, keepdims=True)).astype(BF)
        p_ref[0, h] = p
        return p

    def attend(h, p):
        o = nn(jnp.concatenate([part_of(2, h), ones], 0), p)
        rl = 1.0 / o[HD:HD + 1]
        rl_ref[0, h:h + 1] = rl
        att_ref[0, h * HD:h * HD + HD] = (o[:HD] * rl).astype(BF)

    for t in (1, 0, 2):
        project(0, t)
    scored, weighed = [], []
    total = None
    for h in range(2 * heads + 2):
        if h < 2 * heads:
            scored.append(scores(h))
        if h in (1, 2, 3):
            project(1, (1, 0, 2)[h - 1])
        if h >= 2:
            attend(h - 2, weighed.pop(0))
        if 1 <= h <= 2 * heads:
            weighed.append(weights(h - 1, scored.pop(0)))
        if h == heads + 2:
            total = tn(att_ref[0, :half], wo_own[...])
    h1 = x + (total + tn(att_ref[0, half:], wo_oth[...])) + vec(vecs, 2)
    h1_ref[...] = h1
    n2_ref[...] = (normalised(h1)[0] * vec(vecs, 3) + vec(vecs, 4)).astype(BF)


def whole(shape):
    at = (0,) * len(shape)
    return pl.BlockSpec(shape, lambda i, *_: at, pipeline_mode=pl.Buffered(1))


def takes(microseconds):
    return pl.CostEstimate(flops=int(microseconds * 1e9), bytes_accessed=0, transcendentals=0)


def params(mib):
    return pltpu.CompilerParams(vmem_limit_bytes=mib * MIB, dimension_semantics=("arbitrary",))


def vec(vecs, i):
    return vecs[i:i + 1]


def vecs_spec():
    return whole((8, D))


def attention_forward(tens, lens, x, vecs, wq_own, wq_oth, wo_own, wo_oth, rows):
    scenes = rows // LAT
    rowblock = pl.BlockSpec((LAT, D), lambda i, *_: (i, 0))
    half = wo_own.shape[0]
    return pl.pallas_call(
        forward_kernel,
        grid_spec=pltpu.PrefetchScalarGridSpec(
            num_scalar_prefetch=2,
            grid=(scenes,),
            in_specs=[
                pl.BlockSpec((LAT, D), lambda i, tens, lens: (tens[0] * scenes + i, 0)),
                vecs_spec(), whole((3 * half, D)), whole((3 * half, D)), whole((half, D)), whole((half, D)),
            ],
            out_specs=[
                rowblock,
                pl.BlockSpec((1, 2, 3, half, LAT), lambda i, *_: (i, 0, 0, 0, 0)),
                pl.BlockSpec((1, 2 * half // HD, LAT, LAT), lambda i, *_: (i, 0, 0, 0)),
                pl.BlockSpec((1, D, LAT), lambda i, *_: (i, 0, 0)),
                pl.BlockSpec((1, 2 * half // HD, LAT), lambda i, *_: (i, 0, 0)),
                rowblock,
                rowblock,
            ],
            scratch_shapes=[pltpu.VMEM((2, 2 * half, LAT), BF)],
        ),
        out_shape=[
            pltpu.HBM((rows, D), BF),
            pltpu.HBM((scenes, 2, 3, half, LAT), BF),
            pltpu.HBM((scenes, 2 * half // HD, LAT, LAT), BF),
            pltpu.HBM((scenes, D, LAT), BF),
            pltpu.HBM((scenes, 2 * half // HD, LAT), F32),
            pltpu.HBM((rows, D), F32),
            pltpu.HBM((rows, D), BF),
        ],
        compiler_params=params(40),
        cost_estimate=takes(23),
        name="attention_forward",
    )(tens, *hbm(lens, x), vecs, *hbm(wq_own), wq_oth, *hbm(wo_own), wo_oth)


SUB = 256


def gelu_parts(z):
    cdf = 0.5 + 0.5 * lax.erf(z * 0.7071067811865476)
    return z * cdf, cdf + z * (0.3989422804014327 * jnp.exp2(z * z * (-0.5 * LOG2E)))


def put_slabs(out, at, values):
    n = values.shape[0]
    for c in range(D // 128):
        out[at + c * n:at + (c + 1) * n] = values[:, c * 128:c * 128 + 128].astype(out.dtype)


def put_row(out, at, row, count):
    parts = [row[:, c * 128:c * 128 + 128] for c in range(row.shape[1] // 128)]
    parts += [jnp.zeros((1, 128), F32)] * (count - len(parts))
    out[at:at + count] = jnp.concatenate(parts, 0).astype(out.dtype)


def mlp_kernel(
    tens, n2_ref, cot_ref, up_own, down_own, up_oth, down_oth, vecs_oth, vecs, h1_ref, att_ref, rl_ref, wo_own, wo_oth,
    act_ref, gh_ref, doa_ref, own_ref, oth_ref, cols_ref, dub_ref, acc_up, acc_down, acc_ub, acc_wo,
):
    @pl.when(pl.program_id(0) == 0)
    def _():
        acc_up[...] = jnp.zeros_like(acc_up)
        acc_down[...] = jnp.zeros_like(acc_down)
        acc_ub[...] = jnp.zeros_like(acc_ub)
        acc_wo[...] = jnp.zeros_like(acc_wo)
        cols_ref[...] = jnp.zeros_like(cols_ref)

    n2, cot = n2_ref[...], cot_ref[...]
    units = up_own.shape[0]
    per = units // SUB

    def place(j):
        side, at = divmod(j, per)
        ups, downs, rows = ((up_own, down_own, vecs), (up_oth, down_oth, vecs_oth))[side]
        at = slice(at * SUB, at * SUB + SUB)
        first = at.start // D
        return ups[at], downs[at], vec(rows, 6 + first)[:, at.start - first * D:at.stop - first * D]

    def before(j):
        u, d, b = place(j)
        return nt(n2, u) + b, nt(cot, d)

    def between(pre, grad_act):
        act, slope = gelu_parts(pre)
        return act.astype(BF), (grad_act * slope).astype(BF)

    def after(j, act, dpre):
        u, _, _ = place(j)
        at = slice(j * SUB, j * SUB + SUB)
        act_ref[:, at] = act
        acc_down[at] += tn(act, cot)
        acc_up[at] += tn(dpre, n2)
        acc_ub[:, at] += jnp.sum(dpre.astype(F32), 0, keepdims=True)
        return nn(dpre, u)

    back = 0.0
    first, second = [], []
    for j in range(2 * per + 2):
        if j < 2 * per:
            first.append(before(j))
        if j >= 2:
            back += after(j - 2, *second.pop(0))
        if 1 <= j <= 2 * per:
            second.append(between(*first.pop(0)))
    xh, r = normalised(h1_ref[...])
    cot32 = cot.astype(F32)
    gh = cot32 + norm_back(back * vec(vecs, 3), xh, r)
    gh_ref[...] = gh
    gb = gh.astype(BF)
    half = wo_own.shape[0]
    heads = half // HD
    zeros = jnp.zeros((AUG - 3, LAT), F32)
    for side, w in enumerate((wo_own, wo_oth)):
        do = nt(w[...], gb)
        for h in range(heads):
            hh = side * heads + h
            scaled = (do[h * HD:h * HD + HD] * rl_ref[0, hh:hh + 1]).astype(BF)
            doa_ref[0, hh, :HD] = scaled
            delta = -jnp.sum(scaled.astype(F32) * att_ref[0, hh * HD:hh * HD + HD].astype(F32), 0, keepdims=True)
            high = delta.astype(BF).astype(F32)
            low = (delta - high).astype(BF).astype(F32)
            doa_ref[0, hh, HD:] = jnp.concatenate([high, low, delta - high - low, zeros], 0).astype(BF)
    acc_wo[...] += nn(att_ref[0], gb)
    cols_ref[...] += jnp.concatenate(
        [jnp.sum(v, 0, keepdims=True) for v in (back * xh, back, gh, cot32)] + [jnp.zeros((4, D), F32)], 0
    )

    @pl.when(pl.program_id(0) == pl.num_programs(0) - 1)
    def _():
        base = 8 * units + 4 * half
        for side, ref in enumerate((own_ref, oth_ref)):
            put_slabs(ref, 0, acc_up.at[side * units:(side + 1) * units])
            put_slabs(ref, 4 * units, acc_down.at[side * units:(side + 1) * units])
            put_slabs(ref, 8 * units, acc_wo.at[side * half:(side + 1) * half])
            if ref.shape[0] > base:
                ref[base:] = jnp.zeros((ref.shape[0] - base, 128), ref.dtype)
        put_row(dub_ref, 0, acc_ub, dub_ref.shape[0])


def mlp(tens, n2, cot, up, down, up_oth, down_oth, vecs_oth, vecs, h1, att, rl, wo, wo_oth, total_rows):
    rows = n2.shape[0]
    scenes = rows // LAT
    units, half = up.shape[0], wo.shape[0]
    heads = 2 * half // HD
    rowblock = pl.BlockSpec((LAT, D), lambda i, *_: (i, 0))
    weights = whole((units, D))
    return pl.pallas_call(
        mlp_kernel,
        grid_spec=pltpu.PrefetchScalarGridSpec(
            num_scalar_prefetch=1,
            grid=(scenes,),
            in_specs=[
                rowblock,
                pl.BlockSpec((LAT, D), lambda i, tens: (tens[0] * scenes + i, 0)),
                weights, weights, weights, weights, vecs_spec(), vecs_spec(), rowblock,
                pl.BlockSpec((1, D, LAT), lambda i, *_: (i, 0, 0)),
                pl.BlockSpec((1, heads, LAT), lambda i, *_: (i, 0, 0)),
                whole((half, D)), whole((half, D)),
            ],
            out_specs=[
                pl.BlockSpec((LAT, 2 * units), lambda i, *_: (i, 0)), rowblock,
                pl.BlockSpec((1, heads, HD + AUG, LAT), lambda i, *_: (i, 0, 0, 0)),
                whole((total_rows, 128)), whole((total_rows, 128)), whole((8, D)), whole((2 * units // 128, 128)),
            ],
            scratch_shapes=[
                pltpu.VMEM((2 * units, D), F32), pltpu.VMEM((2 * units, D), F32), pltpu.VMEM((1, 2 * units), F32),
                pltpu.VMEM((2 * half, D), F32),
            ],
        ),
        out_shape=[
            pltpu.HBM((rows, 2 * units), BF),
            pltpu.HBM((rows, D), F32),
            pltpu.HBM((scenes, heads, HD + AUG, LAT), BF),
            pltpu.HBM((total_rows, 128), BF),
            pltpu.HBM((total_rows, 128), BF),
            pltpu.HBM((8, D), F32),
            pltpu.HBM((2 * units // 128, 128), F32),
        ],
        compiler_params=params(40),
        cost_estimate=takes(39),
        name="mlp",
    )(tens, *hbm(n2, cot, up, down), up_oth, down_oth, vecs_oth, vecs, *hbm(h1, att, rl, wo), wo_oth)


def block_out_kernel(tens, act_ref, down_own, down_oth, vecs, h1_ref, out_ref):
    units = down_own.shape[0]
    term = nn(act_ref[:, :units], down_own[...]) + nn(act_ref[:, units:], down_oth[...])
    out_ref[...] = (h1_ref[...] + term + vec(vecs, 5)).astype(BF)


def block_out(tens, act, down, down_oth, vecs, h1):
    rows = h1.shape[0]
    units = down.shape[0]
    rowblock = pl.BlockSpec((LAT, D), lambda i, *_: (i, 0))
    return pl.pallas_call(
        block_out_kernel,
        grid_spec=pltpu.PrefetchScalarGridSpec(
            num_scalar_prefetch=1,
            grid=(rows // LAT,),
            in_specs=[
                pl.BlockSpec((LAT, 2 * units), lambda i, *_: (i, 0)), whole((units, D)), whole((units, D)), vecs_spec(), rowblock,
            ],
            out_specs=[rowblock],
        ),
        out_shape=[pltpu.HBM((rows, D), BF)],
        compiler_params=params(24),
        cost_estimate=takes(7),
        name="block_out",
    )(tens, *vmem(act), down, down_oth, vecs, *hbm(h1))[0]


def back_kernel(tens, p_ref, doa_ref, qkv_ref, n1_ref, *refs, ends):
    starts, stops = ends
    dqkv_ref, dw_ref, acc = refs[-3:]
    groups = acc.shape[0]
    ones = jnp.ones((AUG, LAT), BF)
    count = p_ref.shape[1]

    @pl.when((pl.program_id(0) == 0) & (pl.program_id(1) == 0))
    def _():
        if starts:
            acc[...] = jnp.zeros_like(acc)
        else:
            acc[...] = refs[0][...]

    def part_of(t, h):
        return qkv_ref[0, 0, t, h * HD:h * HD + HD]

    def first(h):
        return tn(jnp.concatenate([part_of(2, h), ones], 0), doa_ref[0, h])

    def second(h, grad):
        return (p_ref[0, h].astype(F32) * grad).astype(BF)

    def third(h, ds):
        at = slice(h * HD, h * HD + HD)
        dqkv_ref[0, 0, 0, at] = (nn(part_of(1, h), ds) * HD**-0.5).astype(BF)
        dqkv_ref[0, 0, 1, at] = nt(part_of(0, h), ds).astype(BF)

    def values(h):
        dqkv_ref[0, 0, 2, h * HD:h * HD + HD] = nt(doa_ref[0, h, :HD], p_ref[0, h]).astype(BF)

    grads, scores = [], []
    for h in range(count + 1):
        if h < count:
            grads.append(first(h))
            values(h)
        if h >= 1:
            third(h - 1, scores.pop(0))
        if h < count:
            scores.append(second(h, grads.pop(0)))
    feats = count * HD
    group = pl.program_id(1)
    term = nn(dqkv_ref[0, 0].reshape(3 * feats, LAT), n1_ref[...])
    acc[group] += term.reshape(3, feats, D)

    @pl.when((pl.program_id(0) == pl.num_programs(0) - 1) & (pl.program_id(1) == groups - 1))
    def _():
        if not stops:
            dw_ref[...] = acc[...]
            return
        for c in range(D // 128):
            for t in range(3):
                for g in range(groups):
                    row = ((c * 3 + t) * groups + g) * feats
                    dw_ref[row:row + feats] = acc[g, t, :, c * 128:c * 128 + 128].astype(dw_ref.dtype)
        used = 12 * groups * feats
        if used < dw_ref.shape[0]:
            dw_ref[used:] = jnp.zeros((dw_ref.shape[0] - used, 128), dw_ref.dtype)


BACK_HEADS = 4


def attention_back(tens, p, doa, qkv, n1, dqkv, partial, side, first, count, total_rows):
    scenes, heads = p.shape[0], p.shape[1] // 2
    steps = heads // BACK_HEADS
    feats = BACK_HEADS * HD
    block = lambda i, j, *_: (first + i, side, 0, j, 0)
    head_block = lambda i, j, *_: (first + i, side * steps + j, 0, 0)
    ends = (first == 0, first + count == scenes)
    sums = (steps, 3, feats, D)
    zeros = lambda i, j, *_: (0, 0, 0, 0)
    carried, specs, aliases = [], [], {}
    if not ends[0]:
        carried.extend(vmem(partial))
        specs.append(pl.BlockSpec(sums, zeros, pipeline_mode=pl.Buffered(1)))
    if dqkv is not None:
        aliases = {5 + len(carried): 0}
        carried.extend(vmem(dqkv))
        specs.append(pl.BlockSpec(memory_space=pl.ANY))
    if ends[1]:
        dw = jax.ShapeDtypeStruct((total_rows, 128), BF if side else F32)
        dw_spec = pl.BlockSpec((total_rows, 128), lambda i, j, *_: (0, 0), pipeline_mode=pl.Buffered(1))
    else:
        dw = pltpu.VMEM(sums, F32)
        dw_spec = pl.BlockSpec(sums, zeros, pipeline_mode=pl.Buffered(1))
    return pl.pallas_call(
        functools.partial(back_kernel, ends=ends),
        grid_spec=pltpu.PrefetchScalarGridSpec(
            num_scalar_prefetch=1,
            grid=(count, steps),
            in_specs=[
                pl.BlockSpec((1, BACK_HEADS, LAT, LAT), head_block),
                pl.BlockSpec((1, BACK_HEADS, HD + AUG, LAT), head_block),
                pl.BlockSpec((1, 1, 3, feats, LAT), block),
                pl.BlockSpec((LAT, D), lambda i, j, *_: (first + i, 0)),
            ] + specs,
            out_specs=[pl.BlockSpec((1, 1, 3, feats, LAT), block), dw_spec],
            scratch_shapes=[pltpu.VMEM(sums, F32)],
        ),
        out_shape=[pltpu.VMEM(qkv.shape, BF), dw],
        input_output_aliases=aliases,
        compiler_params=pltpu.CompilerParams(vmem_limit_bytes=24 * MIB, dimension_semantics=("arbitrary", "arbitrary")),
        cost_estimate=takes(4.5 * count),
        name="attention_back",
    )(tens, *hbm(p, doa, qkv, n1), *carried)


def norm_one_back_kernel(tens, dqkv, wq_own, wq_oth, x_ref, vecs, gh_ref, cols_two, dub, gl_ref, cols_ref, give_ref, acc):
    feats = wq_own.shape[0]
    g = tn(dqkv[0, 0].reshape(feats, LAT), wq_own[...]) + tn(dqkv[0, 1].reshape(feats, LAT), wq_oth[...])
    xh, r = normalised(x_ref[...].astype(F32))
    gl_ref[...] = gh_ref[...] + norm_back(g * vec(vecs, 0), xh, r)
    sums = jnp.concatenate([jnp.sum(v, 0, keepdims=True) for v in (g * xh, g)] + [cols_two[:4], cols_two[6:]], 0)

    @pl.when(pl.program_id(0) == 0)
    def _():
        acc[...] = sums

    @pl.when(pl.program_id(0) > 0)
    def _():
        acc[:2] += sums[:2]

    @pl.when(pl.program_id(0) == pl.num_programs(0) - 1)
    def _():
        total = acc[...]
        units = dub.shape[0] // 2
        for ref, at in ((cols_ref, 0), (give_ref, units)):
            for c in range(D // 128):
                ref[c * 8:c * 8 + 8] = total[:, c * 128:c * 128 + 128]
            ref[32:] = dub[at:at + units]


def norm_one_back(tens, dqkv, wq_own, wq_oth, x, vecs, gh, cols_two, dub):
    cols = (4 * 8 + dub.shape[0] // 2, 128)
    scenes, half = dqkv.shape[0], dqkv.shape[3]
    rowblock = pl.BlockSpec((LAT, D), lambda i, *_: (i, 0))
    return pl.pallas_call(
        norm_one_back_kernel,
        grid_spec=pltpu.PrefetchScalarGridSpec(
            num_scalar_prefetch=1,
            grid=(scenes,),
            in_specs=[
                pl.BlockSpec((1, 2, 3, half, LAT), lambda i, *_: (i, 0, 0, 0, 0)),
                whole((3 * half, D)), whole((3 * half, D)),
                pl.BlockSpec((LAT, D), lambda i, tens: (tens[0] * scenes + i, 0)),
                vecs_spec(),
                rowblock,
                whole((8, D)), whole(dub.shape),
            ],
            out_specs=[rowblock, whole(cols), whole(cols)],
            scratch_shapes=[pltpu.VMEM((8, D), F32)],
        ),
        out_shape=[pltpu.HBM((scenes * LAT, D), F32), jax.ShapeDtypeStruct(cols, F32), jax.ShapeDtypeStruct(cols, F32)],
        compiler_params=params(28),
        cost_estimate=takes(10),
        name="norm_one_back",
    )(tens, *vmem(dqkv), wq_own, wq_oth, *hbm(x), vecs, *vmem(gh), cols_two, dub)


def tie(value, *after):
    return lax.optimization_barrier((value, *after))[0]


def swap(v):
    return lax.ppermute(v, "tensor", SWAP)


class Stage:
    def __init__(self, count, bits, distances=None):
        self.count, self.bits = count, bits
        self.size = 1 << len(bits[0])
        each = list(range(1, self.size))
        self.distances = distances or (each, each)
        at = lax.axis_index("dp")
        core = lax.axis_index("tensor")

        def value(t, v):
            return sum((jnp.right_shift(v, b) & 1) << k for k, b in enumerate(bits[t]))

        self.place = jnp.where(core == 0, value(0, at), value(1, at)).astype(jnp.int32)
        met = [jnp.where(core == 0, self.distances[0][k], self.distances[1][k]) ^ self.place for k in range(self.size - 1)]
        self.scalars = jnp.stack([self.place] + met).astype(jnp.int32)

    def exchange(self, values):
        out = []
        for k, v in enumerate(values):
            pairs = []
            for i in range(self.count):
                for t in range(2):
                    d = self.distances[t][k]
                    flip = sum(((d >> j) & 1) << b for j, b in enumerate(self.bits[t]))
                    pairs.append((i * 2 + t, (i ^ flip) * 2 + t))
            out.append(lax.ppermute(v, ("dp", "tensor"), pairs))
        return out


def small_call(kernel, out_shape, name, scalars, *arrays, scratch=(), mib=16):
    return pl.pallas_call(
        kernel,
        in_specs=[pl.BlockSpec(memory_space=pltpu.SMEM)] + [pl.BlockSpec(memory_space=pltpu.VMEM)] * len(arrays),
        out_specs=[pl.BlockSpec(memory_space=pltpu.VMEM)] * len(out_shape),
        out_shape=out_shape,
        scratch_shapes=list(scratch),
        compiler_params=pltpu.CompilerParams(vmem_limit_bytes=mib * MIB),
        cost_estimate=takes(0.5),
        name=name,
    )(scalars, *arrays)


def rows_kernel(*refs):
    count = (len(refs) - 2) // 2
    ins, out, held, sem = refs[:count], refs[count], refs[count + 1:-1], refs[-1]
    copies = [pltpu.make_async_copy(r, h, sem.at[k]) for k, (r, h) in enumerate(zip(ins, held))]
    for c in copies:
        c.start()
    for c in copies:
        c.wait()
    parts = []
    for h in held:
        v = h[...].astype(F32)
        parts += [v[i:i + D].reshape(1, D) for i in range(0, v.shape[0], D)]
    out[...] = jnp.concatenate(parts + [jnp.zeros((1, D), F32)] * (out.shape[0] - len(parts)), 0)


def rows_of(*vectors):
    count = -(-sum(v.shape[0] for v in vectors) // (8 * D)) * 8
    return pl.pallas_call(
        rows_kernel,
        in_specs=[pl.BlockSpec(memory_space=pl.ANY)] * len(vectors),
        out_shape=jax.ShapeDtypeStruct((count, D), F32),
        scratch_shapes=[pltpu.VMEM(v.shape, BF) for v in vectors] + [pltpu.SemaphoreType.DMA((len(vectors),))],
        compiler_params=pltpu.CompilerParams(vmem_limit_bytes=16 * MIB),
        name="rows_of",
    )(*hbm(*vectors))


def chunk(place, m):
    return pl.ds(pl.multiple_of(place * m, 16), m)


def hand_out(total, scalars, keep_out, sends):
    m = keep_out.shape[0]
    keep_out[...] = total[chunk(scalars[0], m)]
    for k, out in enumerate(sends):
        out[...] = total[chunk(scalars[1 + k], m)].astype(BF)


def split_kernel(scalars, *refs, count):
    (keep, *recvs), (keep_out, *sends), total = refs[:count], refs[count:-1], refs[-1]
    v = keep[...]
    for r in recvs:
        v = v + r[...].astype(F32)
    total[...] = v
    hand_out(total, scalars, keep_out, sends)


def pieces(stage, rows):
    m = rows // stage.size
    return [jax.ShapeDtypeStruct((m, 128), F32)] + [jax.ShapeDtypeStruct((m, 128), BF)] * (stage.size - 1)


def split(keep, recvs, stage):
    keep, *sends = small_call(
        functools.partial(split_kernel, count=1 + len(recvs)), pieces(stage, keep.shape[0]), "split", stage.scalars, keep,
        *recvs, scratch=[pltpu.VMEM(keep.shape, F32)],
    )
    return keep, sends


def settle_kernel(scalars, keep, *refs):
    v = keep[...]
    for r in refs[:-1]:
        v = v + r[...].astype(F32)
    refs[-1][...] = v.astype(BF)


def settle(keep, recvs, stage):
    return small_call(settle_kernel, [jax.ShapeDtypeStruct(keep.shape, BF)], "settle", stage.scalars, keep, *recvs)[0]


def fill(full, scalars, own, recvs):
    m = full.shape[0] // (1 + len(recvs))
    full[chunk(scalars[0], m)] = own[:m]
    for k, r in enumerate(recvs):
        full[chunk(scalars[1 + k], m)] = r[:m]


def join_kernel(scalars, own, *refs):
    fill(refs[-1], scalars, own, refs[:-1])


def join(own, recvs, stage):
    return small_call(
        join_kernel, [jax.ShapeDtypeStruct((stage.size * own.shape[0], 128), BF)], "join", stage.scalars, own, *recvs
    )[0]


def split_mlp_kernel(scalars, own, recv, keep_out, *sends):
    m = keep_out.shape[0]
    at = chunk(scalars[0], m)
    keep_out[...] = own[at].astype(F32) + recv[at].astype(F32)
    for k, out in enumerate(sends):
        at = chunk(scalars[1 + k], m)
        out[...] = (own[at].astype(F32) + recv[at].astype(F32)).astype(BF)


def split_mlp(own, recv, stage):
    keep, *sends = small_call(
        split_mlp_kernel, pieces(stage, own.shape[0]), "split_mlp", stage.scalars, *hbm(own), recv, mib=24,
    )
    return keep, sends


def finish_mlp_kernel(scalars, *refs):
    (own, *recvs), (dup, ddown, dwo), full = refs[:-4], refs[-4:-1], refs[-1]
    fill(full, scalars, own, recvs)
    units, half = dup.shape[0], dwo.shape[0]
    for c in range(D // 128):
        at = slice(c * 128, c * 128 + 128)
        dup[:, at] = full[c * units:(c + 1) * units].astype(F32)
        ddown[:, at] = full[(4 + c) * units:(5 + c) * units].astype(F32)
        dwo[:, at] = full[8 * units + c * half:8 * units + (c + 1) * half].astype(F32)


def finish_mlp(own, recvs, stage, units, half):
    return small_call(
        finish_mlp_kernel,
        [
            jax.ShapeDtypeStruct((units, D), F32), jax.ShapeDtypeStruct((units, D), F32),
            jax.ShapeDtypeStruct((half, D), F32),
        ],
        "finish_mlp", stage.scalars, own, *recvs, scratch=[pltpu.VMEM((stage.size * own.shape[0], 128), BF)],
    )


def parts_of(v):
    high = v.astype(BF)
    return jnp.concatenate([high, (v - high.astype(F32)).astype(BF)], 0)


def whole_of(v):
    m = v.shape[0] // 2
    return v[:m].astype(F32) + v[m:].astype(F32)


def settle_cols_kernel(scalars, keep, *refs):
    *recvs, cols, cols_recv, out = refs
    m = keep.shape[0]
    v = keep[...]
    for r in recvs:
        v = v + r[...].astype(F32)
    out[:m] = v.astype(BF)
    out[m:] = parts_of(cols[...] + cols_recv[...])


def settle_cols(keep, recvs, cols, cols_recv, stage):
    shape = (keep.shape[0] + 2 * cols.shape[0], 128)
    return small_call(
        settle_cols_kernel, [jax.ShapeDtypeStruct(shape, BF)], "settle_cols", stage.scalars, keep, *recvs, cols, cols_recv
    )[0]


def sum_cols(scalars, own, recvs, m, held):
    held[scalars[0]] = whole_of(own[m:])
    for k, r in enumerate(recvs):
        held[scalars[1 + k]] = whole_of(r[m:])
    total = held[0]
    for k in range(1, held.shape[0]):
        total = total + held[k]
    return total


def join_cols_kernel(scalars, *refs):
    (own, *recvs), out, held = refs[:-2], refs[-2], refs[-1]
    size = 1 + len(recvs)
    m = own.shape[0] - 2 * held.shape[1]
    fill(out.at[pl.ds(0, size * m)], scalars, own, recvs)
    out[size * m:] = parts_of(sum_cols(scalars, own, recvs, m, held))


def join_cols(own, recvs, stage, extra):
    m = own.shape[0] - extra
    return small_call(
        join_cols_kernel, [jax.ShapeDtypeStruct((stage.size * m + extra, 128), BF)], "join_cols", stage.scalars, own, *recvs,
        scratch=[pltpu.VMEM((stage.size, extra // 2, 128), F32)],
    )[0]


def finish_qkv_kernel(scalars, *refs):
    (own, *recvs), (out, cols), (full, held) = refs[:-4], refs[-4:-2], refs[-2:]
    m = full.shape[0] // (1 + len(recvs))
    fill(full, scalars, own, recvs)
    cols[...] = sum_cols(scalars, own, recvs, m, held)
    half = out.shape[1]
    for c in range(D // 128):
        for t in range(3):
            row = (c * 3 + t) * half
            out[t, :, c * 128:c * 128 + 128] = full[row:row + half].astype(F32)


def finish_qkv(own, recvs, stage, half, extra):
    m = own.shape[0] - extra
    return small_call(
        finish_qkv_kernel,
        [jax.ShapeDtypeStruct((3, half, D), F32), jax.ShapeDtypeStruct((extra // 2, 128), F32)],
        "finish_qkv", stage.scalars, own, *recvs,
        scratch=[pltpu.VMEM((stage.size * m, 128), BF), pltpu.VMEM((stage.size, extra // 2, 128), F32)],
    )


def advance(steps, token):
    try:
        return steps.send(token), None
    except StopIteration as end:
        return token, end.value


def body(
    latents, scene_len, attn_gain, attn_shift, qkv_weight, out_weight, out_bias, mlp_gain, mlp_shift,
    up_weight, up_bias, down_weight, down_bias, cotangent,
):
    rows = latents.shape[0] // lax.axis_size("tensor")
    units, half = up_weight.shape[0], out_weight.shape[0]
    heads = half // HD
    tens = lax.axis_index("tensor").astype(jnp.int32).reshape(1)
    count = lax.axis_size("dp")
    steps = count.bit_length() - 1
    assert 1 << steps == count and steps > 1
    lower, upper = list(range(steps - 2)), [steps - 2, steps - 1]
    turned = [b ^ 1 if b ^ 1 < steps - 2 else b for b in lower]
    group = Stage(count, (upper, upper), ([1, 2, 3], [2, 1, 3]))
    pairs = [Stage(count, ([a], [b])) for a, b in zip(lower, turned)]
    mlp_stages = pairs + [group]
    if len(lower) % 2:
        qkv_stages = mlp_stages
    else:
        qkv_stages = [
            Stage(count, (lower[i:i + 2],) * 2, ([1, 2, 3], [2, 1, 3])) for i in range(0, len(lower), 2)
        ] + [group]

    wq = qkv_weight.reshape(3 * half, D)
    wq_oth, wo_oth = swap(wq), swap(out_weight)
    vecs = rows_of(attn_gain, attn_shift, out_bias, mlp_gain, mlp_shift, down_bias, up_bias)
    vecs_oth = swap(vecs)
    up_oth, down_oth = swap(up_weight), swap(down_weight)

    n1, qkv, p, att, rl, h1, n2 = attention_forward(
        tens, scene_len, latents, vecs, wq, wq_oth, out_weight, wo_oth, rows
    )
    need = 8 * units + 4 * half
    total_rows = -(-need // (16 * count)) * 16 * count
    act, gh, doa, grads_own, grads_oth, cols_two, grad_ub = mlp(
        tens, n2, cotangent, up_weight, down_weight, up_oth, down_oth, vecs_oth, vecs, h1, att, rl, out_weight, wo_oth, total_rows
    )
    from_peer = swap(grads_oth)

    def exchanges(stages, keep, sends, settled, joined):
        for s, stage in enumerate(stages):
            recvs = stage.exchange(sends)
            token = yield sends[-1]
            recvs = [tie(r, token) for r in recvs]
            if s + 1 < len(stages):
                keep, sends = split(keep, recvs, stages[s + 1])
            else:
                have = settled(keep, recvs, stage)
        for s in range(len(stages) - 1, -1, -1):
            recvs = stages[s].exchange([have] * (stages[s].size - 1))
            token = yield have
            recvs = [tie(r, token) for r in recvs]
            if s:
                have = joined(have, recvs, stages[s])
        return have, recvs

    qkv_rows = -(-12 * half // (16 * count)) * 16 * count
    extra = 2 * (4 * 8 + units // 128)
    dqkv, dw, qkv_peer = None, None, None
    token = grads_oth
    chains, results = {}, {}
    cols = []

    def step(name):
        if name not in results:
            after, result = advance(chains[name], token)
            if result is not None:
                results[name] = result
            return after
        return token

    for action, *rest in PLAN:
        if action == "back":
            side, first, number = rest
            dqkv, dw = attention_back(tie(tens, token), p, doa, qkv, n1, dqkv, dw, side, first, number, qkv_rows)
            token = dw
            if side and first + number == rows // LAT:
                qkv_peer = swap(dw)
        elif action == "mlp":
            chains["mlp"] = exchanges(
                mlp_stages, *split_mlp(grads_own, tie(from_peer, token), mlp_stages[0]), settle, join
            )
            token = next(chains["mlp"])
        elif action == "qkv":
            chains["qkv"] = exchanges(
                qkv_stages, *split(tie(dw, token), [qkv_peer], qkv_stages[0]),
                lambda keep, recvs, stage: settle_cols(keep, recvs, *cols, stage),
                lambda own, recvs, stage: join_cols(own, recvs, stage, extra),
            )
            token = next(chains["qkv"])
        elif action == "norm":
            grad_latents, cols_one, cols_give = norm_one_back(
                tie(tens, token), dqkv, wq, wq_oth, latents, vecs, gh, cols_two, grad_ub
            )
            cols.extend((cols_one, swap(cols_give)))
            token = cols_one
        elif action == "out":
            out = block_out(tie(tens, token), act, down_weight, down_oth, vecs, h1)
            token = out
        elif action == "end":
            while "mlp" not in results:
                token = step("mlp")
            have, recvs = results["mlp"]
            dup, ddown, dwo = finish_mlp(tie(have, token), recvs, mlp_stages[0], units, half)
            token = dwo
        else:
            token = step(action[:3])
    while "qkv" not in results:
        token = step("qkv")
    dwq, shared = finish_qkv(*results["qkv"], qkv_stages[0], half, extra)
    dub = shared[32:]
    shared = shared[:32].reshape(D // 128, 8, 128).transpose(1, 0, 2).reshape(8, D)
    return (
        out, grad_latents, shared[0], shared[1], dwq, dwo, shared[4],
        shared[2], shared[3], dup, dub.reshape(units), ddown, shared[5],
    )


def solution(mesh):
    placed = (
        P("dp", None), P("dp"), P(), P(), P(None, "tensor", None), P("tensor", None), P(), P(), P(),
        P("tensor", None), P("tensor"), P("tensor", None), P(), P("dp", None),
    )
    return jax.shard_map(
        body,
        mesh=mesh,
        in_specs=placed,
        out_specs=(
            P(("dp", "tensor"), None), P(("dp", "tensor"), None), P(), P(), P(None, "tensor", None),
            P("tensor", None), P(), P(), P(), P("tensor", None), P("tensor"), P("tensor", None), P(),
        ),
        check_vma=False,
    )
```

```python
import functools

import jax
import jax.numpy as jnp
from jax import lax
from jax.experimental import pallas as pl
from jax.experimental.pallas import tpu as pltpu
from jax.sharding import PartitionSpec as P

D = 512
HD = 64
LAT = 512
AUG = 16
EPS = 1e-05
LOG2E = 1.4426950408889634
NEG = -1e30
BF = jnp.bfloat16
F32 = jnp.float32
MIB = 2**20
SWAP = [(0, 1), (1, 0)]
PLAN = (
("back", 1, 0, 1), ("mlp",), ("back", 1, 1, 3), ("mlp+",), ("back", 0, 0, 2), ("mlp+",), ("back", 0, 2, 2), ("mlp+",), ("qkv",), ("norm",), ("qkv+",), ("mlp+",), ("qkv+",), ("mlp+",), ("qkv+",), ("out",), ("end",), ("qkv+",),
)


def _dot(a, b, ca, cb):
    return lax.dot_general(a, b, (((ca,), (cb,)), ((), ())), preferred_element_type=F32)


def hbm(*values):
    return tuple(pltpu.with_memory_space_constraint(v, pltpu.HBM) for v in values)


def vmem(*values):
    return tuple(pltpu.with_memory_space_constraint(v, pltpu.VMEM) for v in values)


def nn(a, b):
    return _dot(a, b, 1, 0)


def nt(a, b):
    return _dot(a, b, 1, 1)


def tn(a, b):
    return _dot(a, b, 0, 0)


def normalised(v):
    c = v - jnp.mean(v, -1, keepdims=True)
    r = lax.rsqrt(jnp.mean(c * c, -1, keepdims=True) + EPS)
    return c * r, r


def norm_back(e, xh, r):
    return r * (e - jnp.mean(e, -1, keepdims=True) - xh * jnp.mean(e * xh, -1, keepdims=True))


def forward_kernel(
    tens, lens, x_ref, vecs, wq_own, wq_oth, wo_own, wo_oth,
    n1_ref, qkv_ref, p_ref, att_ref, rl_ref, h1_ref, n2_ref, asked,
):
    scenes = pl.num_programs(0)
    length = lens[tens[0] * scenes + pl.program_id(0)]
    x = x_ref[...].astype(F32)
    n1 = (normalised(x)[0] * vec(vecs, 0) + vec(vecs, 1)).astype(BF)
    n1_ref[...] = n1
    half = wo_own.shape[0]
    heads = half // HD

    def project(side, t):
        part = nt((wq_own, wq_oth)[side][t * half:(t + 1) * half], n1)
        part = part.astype(BF)
        if t == 0:
            scaled = part.astype(F32) * (HD**-0.5 * LOG2E)
            high = scaled.astype(BF)
            at = slice(side * half, (side + 1) * half)
            asked[0, at] = high
            asked[1, at] = (scaled - high.astype(F32)).astype(BF)
            part = part * HD**-0.5
        qkv_ref[0, side, t] = part.astype(BF)

    key_at = lax.broadcasted_iota(jnp.int32, (AUG, LAT), 1)
    row_at = lax.broadcasted_iota(jnp.int32, (AUG, LAT), 0)
    bias = jnp.where((key_at >= length) & (row_at == 0), NEG, 0.0).astype(BF)
    ones = jnp.ones((AUG, LAT), BF)

    def part_of(t, h):
        return qkv_ref[0, h // heads, t, h % heads * HD:h % heads * HD + HD]

    def scores(h):
        k = part_of(1, h)
        at = slice(h * HD, h * HD + HD)
        return tn(jnp.concatenate([k, k, bias], 0), jnp.concatenate([asked[0, at], asked[1, at], ones], 0))

    def weights(h, s):
        p = jnp.exp2(s - jnp.max(s, 0, keepdims=True)).astype(BF)
        p_ref[0, h] = p
        return p

    def attend(h, p):
        o = nn(jnp.concatenate([part_of(2, h), ones], 0), p)
        rl = 1.0 / o[HD:HD + 1]
        rl_ref[0, h:h + 1] = rl
        att_ref[0, h * HD:h * HD + HD] = (o[:HD] * rl).astype(BF)

    for t in (1, 0, 2):
        project(0, t)
    scored, weighed = [], []
    total = None
    for h in range(2 * heads + 2):
        if h < 2 * heads:
            scored.append(scores(h))
        if h in (1, 2, 3):
            project(1, (1, 0, 2)[h - 1])
        if h >= 2:
            attend(h - 2, weighed.pop(0))
        if 1 <= h <= 2 * heads:
            weighed.append(weights(h - 1, scored.pop(0)))
        if h == heads + 2:
            total = tn(att_ref[0, :half], wo_own[...])
    h1 = x + (total + tn(att_ref[0, half:], wo_oth[...])) + vec(vecs, 2)
    h1_ref[...] = h1
    n2_ref[...] = (normalised(h1)[0] * vec(vecs, 3) + vec(vecs, 4)).astype(BF)


def whole(shape):
    at = (0,) * len(shape)
    return pl.BlockSpec(shape, lambda i, *_: at, pipeline_mode=pl.Buffered(1))


def takes(microseconds):
    return pl.CostEstimate(flops=int(microseconds * 1e9), bytes_accessed=0, transcendentals=0)


def params(mib):
    return pltpu.CompilerParams(vmem_limit_bytes=mib * MIB, dimension_semantics=("arbitrary",))


def vec(vecs, i):
    return vecs[i:i + 1]


def vecs_spec():
    return whole((8, D))


def attention_forward(tens, lens, x, vecs, wq_own, wq_oth, wo_own, wo_oth, rows):
    scenes = rows // LAT
    rowblock = pl.BlockSpec((LAT, D), lambda i, *_: (i, 0))
    half = wo_own.shape[0]
    return pl.pallas_call(
        forward_kernel,
        grid_spec=pltpu.PrefetchScalarGridSpec(
            num_scalar_prefetch=2,
            grid=(scenes,),
            in_specs=[
                pl.BlockSpec((LAT, D), lambda i, tens, lens: (tens[0] * scenes + i, 0)),
                vecs_spec(), whole((3 * half, D)), whole((3 * half, D)), whole((half, D)), whole((half, D)),
            ],
            out_specs=[
                rowblock,
                pl.BlockSpec((1, 2, 3, half, LAT), lambda i, *_: (i, 0, 0, 0, 0)),
                pl.BlockSpec((1, 2 * half // HD, LAT, LAT), lambda i, *_: (i, 0, 0, 0)),
                pl.BlockSpec((1, D, LAT), lambda i, *_: (i, 0, 0)),
                pl.BlockSpec((1, 2 * half // HD, LAT), lambda i, *_: (i, 0, 0)),
                rowblock,
                rowblock,
            ],
            scratch_shapes=[pltpu.VMEM((2, 2 * half, LAT), BF)],
        ),
        out_shape=[
            pltpu.HBM((rows, D), BF),
            pltpu.HBM((scenes, 2, 3, half, LAT), BF),
            pltpu.HBM((scenes, 2 * half // HD, LAT, LAT), BF),
            pltpu.HBM((scenes, D, LAT), BF),
            pltpu.HBM((scenes, 2 * half // HD, LAT), F32),
            pltpu.HBM((rows, D), F32),
            pltpu.HBM((rows, D), BF),
        ],
        compiler_params=params(40),
        cost_estimate=takes(23),
        name="attention_forward",
    )(tens, *hbm(lens, x), vecs, *hbm(wq_own), wq_oth, *hbm(wo_own), wo_oth)


SUB = 256


def gelu_parts(z):
    cdf = 0.5 + 0.5 * lax.erf(z * 0.7071067811865476)
    return z * cdf, cdf + z * (0.3989422804014327 * jnp.exp2(z * z * (-0.5 * LOG2E)))


def put_slabs(out, at, values):
    n = values.shape[0]
    for c in range(D // 128):
        out[at + c * n:at + (c + 1) * n] = values[:, c * 128:c * 128 + 128].astype(out.dtype)


def put_row(out, at, row, count):
    parts = [row[:, c * 128:c * 128 + 128] for c in range(row.shape[1] // 128)]
    parts += [jnp.zeros((1, 128), F32)] * (count - len(parts))
    out[at:at + count] = jnp.concatenate(parts, 0).astype(out.dtype)


def mlp_kernel(
    tens, n2_ref, cot_ref, up_own, down_own, up_oth, down_oth, vecs_oth, vecs, h1_ref, att_ref, rl_ref, wo_own, wo_oth,
    act_ref, gh_ref, doa_ref, own_ref, oth_ref, cols_ref, dub_ref, acc_up, acc_down, acc_ub, acc_wo,
):
    @pl.when(pl.program_id(0) == 0)
    def _():
        acc_up[...] = jnp.zeros_like(acc_up)
        acc_down[...] = jnp.zeros_like(acc_down)
        acc_ub[...] = jnp.zeros_like(acc_ub)
        acc_wo[...] = jnp.zeros_like(acc_wo)
        cols_ref[...] = jnp.zeros_like(cols_ref)

    n2, cot = n2_ref[...], cot_ref[...]
    units = up_own.shape[0]
    per = units // SUB

    def place(j):
        side, at = divmod(j, per)
        ups, downs, rows = ((up_own, down_own, vecs), (up_oth, down_oth, vecs_oth))[side]
        at = slice(at * SUB, at * SUB + SUB)
        first = at.start // D
        return ups[at], downs[at], vec(rows, 6 + first)[:, at.start - first * D:at.stop - first * D]

    def before(j):
        u, d, b = place(j)
        return nt(n2, u) + b, nt(cot, d)

    def between(pre, grad_act):
        act, slope = gelu_parts(pre)
        return act.astype(BF), (grad_act * slope).astype(BF)

    def after(j, act, dpre):
        u, _, _ = place(j)
        at = slice(j * SUB, j * SUB + SUB)
        act_ref[:, at] = act
        acc_down[at] += tn(act, cot)
        acc_up[at] += tn(dpre, n2)
        acc_ub[:, at] += jnp.sum(dpre.astype(F32), 0, keepdims=True)
        return nn(dpre, u)

    back = 0.0
    first, second = [], []
    for j in range(2 * per + 2):
        if j < 2 * per:
            first.append(before(j))
        if j >= 2:
            back += after(j - 2, *second.pop(0))
        if 1 <= j <= 2 * per:
            second.append(between(*first.pop(0)))
    xh, r = normalised(h1_ref[...])
    cot32 = cot.astype(F32)
    gh = cot32 + norm_back(back * vec(vecs, 3), xh, r)
    gh_ref[...] = gh
    gb = gh.astype(BF)
    half = wo_own.shape[0]
    heads = half // HD
    zeros = jnp.zeros((AUG - 3, LAT), F32)
    for side, w in enumerate((wo_own, wo_oth)):
        do = nt(w[...], gb)
        for h in range(heads):
            hh = side * heads + h
            scaled = (do[h * HD:h * HD + HD] * rl_ref[0, hh:hh + 1]).astype(BF)
            doa_ref[0, hh, :HD] = scaled
            delta = -jnp.sum(scaled.astype(F32) * att_ref[0, hh * HD:hh * HD + HD].astype(F32), 0, keepdims=True)
            high = delta.astype(BF).astype(F32)
            low = (delta - high).astype(BF).astype(F32)
            doa_ref[0, hh, HD:] = jnp.concatenate([high, low, delta - high - low, zeros], 0).astype(BF)
    acc_wo[...] += nn(att_ref[0], gb)
    cols_ref[...] += jnp.concatenate(
        [jnp.sum(v, 0, keepdims=True) for v in (back * xh, back, gh, cot32)] + [jnp.zeros((4, D), F32)], 0
    )

    @pl.when(pl.program_id(0) == pl.num_programs(0) - 1)
    def _():
        base = 8 * units + 4 * half
        for side, ref in enumerate((own_ref, oth_ref)):
            put_slabs(ref, 0, acc_up.at[side * units:(side + 1) * units])
            put_slabs(ref, 4 * units, acc_down.at[side * units:(side + 1) * units])
            put_slabs(ref, 8 * units, acc_wo.at[side * half:(side + 1) * half])
            if ref.shape[0] > base:
                ref[base:] = jnp.zeros((ref.shape[0] - base, 128), ref.dtype)
        put_row(dub_ref, 0, acc_ub, dub_ref.shape[0])


def mlp(tens, n2, cot, up, down, up_oth, down_oth, vecs_oth, vecs, h1, att, rl, wo, wo_oth, total_rows):
    rows = n2.shape[0]
    scenes = rows // LAT
    units, half = up.shape[0], wo.shape[0]
    heads = 2 * half // HD
    rowblock = pl.BlockSpec((LAT, D), lambda i, *_: (i, 0))
    weights = whole((units, D))
    return pl.pallas_call(
        mlp_kernel,
        grid_spec=pltpu.PrefetchScalarGridSpec(
            num_scalar_prefetch=1,
            grid=(scenes,),
            in_specs=[
                rowblock,
                pl.BlockSpec((LAT, D), lambda i, tens: (tens[0] * scenes + i, 0)),
                weights, weights, weights, weights, vecs_spec(), vecs_spec(), rowblock,
                pl.BlockSpec((1, D, LAT), lambda i, *_: (i, 0, 0)),
                pl.BlockSpec((1, heads, LAT), lambda i, *_: (i, 0, 0)),
                whole((half, D)), whole((half, D)),
            ],
            out_specs=[
                pl.BlockSpec((LAT, 2 * units), lambda i, *_: (i, 0)), rowblock,
                pl.BlockSpec((1, heads, HD + AUG, LAT), lambda i, *_: (i, 0, 0, 0)),
                whole((total_rows, 128)), whole((total_rows, 128)), whole((8, D)), whole((2 * units // 128, 128)),
            ],
            scratch_shapes=[
                pltpu.VMEM((2 * units, D), F32), pltpu.VMEM((2 * units, D), F32), pltpu.VMEM((1, 2 * units), F32),
                pltpu.VMEM((2 * half, D), F32),
            ],
        ),
        out_shape=[
            pltpu.HBM((rows, 2 * units), BF),
            pltpu.HBM((rows, D), F32),
            pltpu.HBM((scenes, heads, HD + AUG, LAT), BF),
            pltpu.HBM((total_rows, 128), BF),
            pltpu.HBM((total_rows, 128), BF),
            pltpu.HBM((8, D), F32),
            pltpu.HBM((2 * units // 128, 128), F32),
        ],
        compiler_params=params(40),
        cost_estimate=takes(39),
        name="mlp",
    )(tens, *hbm(n2, cot, up, down), up_oth, down_oth, vecs_oth, vecs, *hbm(h1, att, rl, wo), wo_oth)


def block_out_kernel(tens, act_ref, down_own, down_oth, vecs, h1_ref, out_ref):
    units = down_own.shape[0]
    term = nn(act_ref[:, :units], down_own[...]) + nn(act_ref[:, units:], down_oth[...])
    out_ref[...] = (h1_ref[...] + term + vec(vecs, 5)).astype(BF)


def block_out(tens, act, down, down_oth, vecs, h1):
    rows = h1.shape[0]
    units = down.shape[0]
    rowblock = pl.BlockSpec((LAT, D), lambda i, *_: (i, 0))
    return pl.pallas_call(
        block_out_kernel,
        grid_spec=pltpu.PrefetchScalarGridSpec(
            num_scalar_prefetch=1,
            grid=(rows // LAT,),
            in_specs=[
                pl.BlockSpec((LAT, 2 * units), lambda i, *_: (i, 0)), whole((units, D)), whole((units, D)), vecs_spec(), rowblock,
            ],
            out_specs=[rowblock],
        ),
        out_shape=[pltpu.HBM((rows, D), BF)],
        compiler_params=params(24),
        cost_estimate=takes(7),
        name="block_out",
    )(tens, *vmem(act), down, down_oth, vecs, *hbm(h1))[0]


def back_kernel(tens, p_ref, doa_ref, qkv_ref, n1_ref, *refs, ends):
    starts, stops = ends
    dqkv_ref, dw_ref, acc = refs[-3:]
    groups = acc.shape[0]
    ones = jnp.ones((AUG, LAT), BF)
    count = p_ref.shape[1]

    @pl.when((pl.program_id(0) == 0) & (pl.program_id(1) == 0))
    def _():
        if starts:
            acc[...] = jnp.zeros_like(acc)
        else:
            acc[...] = refs[0][...]

    def part_of(t, h):
        return qkv_ref[0, 0, t, h * HD:h * HD + HD]

    def first(h):
        return tn(jnp.concatenate([part_of(2, h), ones], 0), doa_ref[0, h])

    def second(h, grad):
        return (p_ref[0, h].astype(F32) * grad).astype(BF)

    def third(h, ds):
        at = slice(h * HD, h * HD + HD)
        dqkv_ref[0, 0, 0, at] = (nn(part_of(1, h), ds) * HD**-0.5).astype(BF)
        dqkv_ref[0, 0, 1, at] = nt(part_of(0, h), ds).astype(BF)

    def values(h):
        dqkv_ref[0, 0, 2, h * HD:h * HD + HD] = nt(doa_ref[0, h, :HD], p_ref[0, h]).astype(BF)

    grads, scores = [], []
    for h in range(count + 1):
        if h < count:
            grads.append(first(h))
            values(h)
        if h >= 1:
            third(h - 1, scores.pop(0))
        if h < count:
            scores.append(second(h, grads.pop(0)))
    feats = count * HD
    group = pl.program_id(1)
    term = nn(dqkv_ref[0, 0].reshape(3 * feats, LAT), n1_ref[...])
    acc[group] += term.reshape(3, feats, D)

    @pl.when((pl.program_id(0) == pl.num_programs(0) - 1) & (pl.program_id(1) == groups - 1))
    def _():
        if not stops:
            dw_ref[...] = acc[...]
            return
        for c in range(D // 128):
            for t in range(3):
                for g in range(groups):
                    row = ((c * 3 + t) * groups + g) * feats
                    dw_ref[row:row + feats] = acc[g, t, :, c * 128:c * 128 + 128].astype(dw_ref.dtype)
        used = 12 * groups * feats
        if used < dw_ref.shape[0]:
            dw_ref[used:] = jnp.zeros((dw_ref.shape[0] - used, 128), dw_ref.dtype)


BACK_HEADS = 4


def attention_back(tens, p, doa, qkv, n1, dqkv, partial, side, first, count, total_rows):
    scenes, heads = p.shape[0], p.shape[1] // 2
    steps = heads // BACK_HEADS
    feats = BACK_HEADS * HD
    block = lambda i, j, *_: (first + i, side, 0, j, 0)
    head_block = lambda i, j, *_: (first + i, side * steps + j, 0, 0)
    ends = (first == 0, first + count == scenes)
    sums = (steps, 3, feats, D)
    zeros = lambda i, j, *_: (0, 0, 0, 0)
    carried, specs, aliases = [], [], {}
    if not ends[0]:
        carried.extend(vmem(partial))
        specs.append(pl.BlockSpec(sums, zeros, pipeline_mode=pl.Buffered(1)))
    if dqkv is not None:
        aliases = {5 + len(carried): 0}
        carried.extend(vmem(dqkv))
        specs.append(pl.BlockSpec(memory_space=pl.ANY))
    if ends[1]:
        dw = jax.ShapeDtypeStruct((total_rows, 128), BF if side else F32)
        dw_spec = pl.BlockSpec((total_rows, 128), lambda i, j, *_: (0, 0), pipeline_mode=pl.Buffered(1))
    else:
        dw = pltpu.VMEM(sums, F32)
        dw_spec = pl.BlockSpec(sums, zeros, pipeline_mode=pl.Buffered(1))
    return pl.pallas_call(
        functools.partial(back_kernel, ends=ends),
        grid_spec=pltpu.PrefetchScalarGridSpec(
            num_scalar_prefetch=1,
            grid=(count, steps),
            in_specs=[
                pl.BlockSpec((1, BACK_HEADS, LAT, LAT), head_block),
                pl.BlockSpec((1, BACK_HEADS, HD + AUG, LAT), head_block),
                pl.BlockSpec((1, 1, 3, feats, LAT), block),
                pl.BlockSpec((LAT, D), lambda i, j, *_: (first + i, 0)),
            ] + specs,
            out_specs=[pl.BlockSpec((1, 1, 3, feats, LAT), block), dw_spec],
            scratch_shapes=[pltpu.VMEM(sums, F32)],
        ),
        out_shape=[pltpu.VMEM(qkv.shape, BF), dw],
        input_output_aliases=aliases,
        compiler_params=pltpu.CompilerParams(vmem_limit_bytes=24 * MIB, dimension_semantics=("arbitrary", "arbitrary")),
        cost_estimate=takes(4.5 * count),
        name="attention_back",
    )(tens, *hbm(p, doa, qkv, n1), *carried)


def norm_one_back_kernel(tens, dqkv, wq_own, wq_oth, x_ref, vecs, gh_ref, cols_two, dub, gl_ref, cols_ref, give_ref, acc):
    feats = wq_own.shape[0]
    g = tn(dqkv[0, 0].reshape(feats, LAT), wq_own[...]) + tn(dqkv[0, 1].reshape(feats, LAT), wq_oth[...])
    xh, r = normalised(x_ref[...].astype(F32))
    gl_ref[...] = gh_ref[...] + norm_back(g * vec(vecs, 0), xh, r)
    sums = jnp.concatenate([jnp.sum(v, 0, keepdims=True) for v in (g * xh, g)] + [cols_two[:4], cols_two[6:]], 0)

    @pl.when(pl.program_id(0) == 0)
    def _():
        acc[...] = sums

    @pl.when(pl.program_id(0) > 0)
    def _():
        acc[:2] += sums[:2]

    @pl.when(pl.program_id(0) == pl.num_programs(0) - 1)
    def _():
        total = acc[...]
        units = dub.shape[0] // 2
        for ref, at in ((cols_ref, 0), (give_ref, units)):
            for c in range(D // 128):
                ref[c * 8:c * 8 + 8] = total[:, c * 128:c * 128 + 128]
            ref[32:] = dub[at:at + units]


def norm_one_back(tens, dqkv, wq_own, wq_oth, x, vecs, gh, cols_two, dub):
    cols = (4 * 8 + dub.shape[0] // 2, 128)
    scenes, half = dqkv.shape[0], dqkv.shape[3]
    rowblock = pl.BlockSpec((LAT, D), lambda i, *_: (i, 0))
    return pl.pallas_call(
        norm_one_back_kernel,
        grid_spec=pltpu.PrefetchScalarGridSpec(
            num_scalar_prefetch=1,
            grid=(scenes,),
            in_specs=[
                pl.BlockSpec((1, 2, 3, half, LAT), lambda i, *_: (i, 0, 0, 0, 0)),
                whole((3 * half, D)), whole((3 * half, D)),
                pl.BlockSpec((LAT, D), lambda i, tens: (tens[0] * scenes + i, 0)),
                vecs_spec(),
                rowblock,
                whole((8, D)), whole(dub.shape),
            ],
            out_specs=[rowblock, whole(cols), whole(cols)],
            scratch_shapes=[pltpu.VMEM((8, D), F32)],
        ),
        out_shape=[pltpu.HBM((scenes * LAT, D), F32), jax.ShapeDtypeStruct(cols, F32), jax.ShapeDtypeStruct(cols, F32)],
        compiler_params=params(28),
        cost_estimate=takes(10),
        name="norm_one_back",
    )(tens, *vmem(dqkv), wq_own, wq_oth, *hbm(x), vecs, *vmem(gh), cols_two, dub)


def tie(value, *after):
    return lax.optimization_barrier((value, *after))[0]


def swap(v):
    return lax.ppermute(v, "tensor", SWAP)


class Stage:
    def __init__(self, count, bits, distances=None):
        self.count, self.bits = count, bits
        self.size = 1 << len(bits[0])
        each = list(range(1, self.size))
        self.distances = distances or (each, each)
        at = lax.axis_index("dp")
        core = lax.axis_index("tensor")

        def value(t, v):
            return sum((jnp.right_shift(v, b) & 1) << k for k, b in enumerate(bits[t]))

        self.place = jnp.where(core == 0, value(0, at), value(1, at)).astype(jnp.int32)
        met = [jnp.where(core == 0, self.distances[0][k], self.distances[1][k]) ^ self.place for k in range(self.size - 1)]
        self.scalars = jnp.stack([self.place] + met).astype(jnp.int32)

    def exchange(self, values):
        out = []
        for k, v in enumerate(values):
            pairs = []
            for i in range(self.count):
                for t in range(2):
                    d = self.distances[t][k]
                    flip = sum(((d >> j) & 1) << b for j, b in enumerate(self.bits[t]))
                    pairs.append((i * 2 + t, (i ^ flip) * 2 + t))
            out.append(lax.ppermute(v, ("dp", "tensor"), pairs))
        return out


def small_call(kernel, out_shape, name, scalars, *arrays, scratch=(), mib=16):
    return pl.pallas_call(
        kernel,
        in_specs=[pl.BlockSpec(memory_space=pltpu.SMEM)] + [pl.BlockSpec(memory_space=pltpu.VMEM)] * len(arrays),
        out_specs=[pl.BlockSpec(memory_space=pltpu.VMEM)] * len(out_shape),
        out_shape=out_shape,
        scratch_shapes=list(scratch),
        compiler_params=pltpu.CompilerParams(vmem_limit_bytes=mib * MIB),
        cost_estimate=takes(0.5),
        name=name,
    )(scalars, *arrays)


def rows_kernel(*refs):
    count = (len(refs) - 2) // 2
    ins, out, held, sem = refs[:count], refs[count], refs[count + 1:-1], refs[-1]
    copies = [pltpu.make_async_copy(r, h, sem.at[k]) for k, (r, h) in enumerate(zip(ins, held))]
    for c in copies:
        c.start()
    for c in copies:
        c.wait()
    parts = []
    for h in held:
        v = h[...].astype(F32)
        parts += [v[i:i + D].reshape(1, D) for i in range(0, v.shape[0], D)]
    out[...] = jnp.concatenate(parts + [jnp.zeros((1, D), F32)] * (out.shape[0] - len(parts)), 0)


def rows_of(*vectors):
    count = -(-sum(v.shape[0] for v in vectors) // (8 * D)) * 8
    return pl.pallas_call(
        rows_kernel,
        in_specs=[pl.BlockSpec(memory_space=pl.ANY)] * len(vectors),
        out_shape=jax.ShapeDtypeStruct((count, D), F32),
        scratch_shapes=[pltpu.VMEM(v.shape, BF) for v in vectors] + [pltpu.SemaphoreType.DMA((len(vectors),))],
        compiler_params=pltpu.CompilerParams(vmem_limit_bytes=16 * MIB),
        name="rows_of",
    )(*hbm(*vectors))


def chunk(place, m):
    return pl.ds(pl.multiple_of(place * m, 16), m)


def hand_out(total, scalars, keep_out, sends):
    m = keep_out.shape[0]
    keep_out[...] = total[chunk(scalars[0], m)]
    for k, out in enumerate(sends):
        out[...] = total[chunk(scalars[1 + k], m)].astype(BF)


def split_kernel(scalars, *refs, count):
    (keep, *recvs), (keep_out, *sends), total = refs[:count], refs[count:-1], refs[-1]
    v = keep[...]
    for r in recvs:
        v = v + r[...].astype(F32)
    total[...] = v
    hand_out(total, scalars, keep_out, sends)


def pieces(stage, rows):
    m = rows // stage.size
    return [jax.ShapeDtypeStruct((m, 128), F32)] + [jax.ShapeDtypeStruct((m, 128), BF)] * (stage.size - 1)


def split(keep, recvs, stage):
    keep, *sends = small_call(
        functools.partial(split_kernel, count=1 + len(recvs)), pieces(stage, keep.shape[0]), "split", stage.scalars, keep,
        *recvs, scratch=[pltpu.VMEM(keep.shape, F32)],
    )
    return keep, sends


def settle_kernel(scalars, keep, *refs):
    v = keep[...]
    for r in refs[:-1]:
        v = v + r[...].astype(F32)
    refs[-1][...] = v.astype(BF)


def settle(keep, recvs, stage):
    return small_call(settle_kernel, [jax.ShapeDtypeStruct(keep.shape, BF)], "settle", stage.scalars, keep, *recvs)[0]


def fill(full, scalars, own, recvs):
    m = full.shape[0] // (1 + len(recvs))
    full[chunk(scalars[0], m)] = own[:m]
    for k, r in enumerate(recvs):
        full[chunk(scalars[1 + k], m)] = r[:m]


def join_kernel(scalars, own, *refs):
    fill(refs[-1], scalars, own, refs[:-1])


def join(own, recvs, stage):
    return small_call(
        join_kernel, [jax.ShapeDtypeStruct((stage.size * own.shape[0], 128), BF)], "join", stage.scalars, own, *recvs
    )[0]


def split_mlp_kernel(scalars, own, recv, keep_out, *sends):
    m = keep_out.shape[0]
    at = chunk(scalars[0], m)
    keep_out[...] = own[at].astype(F32) + recv[at].astype(F32)
    for k, out in enumerate(sends):
        at = chunk(scalars[1 + k], m)
        out[...] = (own[at].astype(F32) + recv[at].astype(F32)).astype(BF)


def split_mlp(own, recv, stage):
    keep, *sends = small_call(
        split_mlp_kernel, pieces(stage, own.shape[0]), "split_mlp", stage.scalars, *hbm(own), recv, mib=24,
    )
    return keep, sends


def finish_mlp_kernel(scalars, *refs):
    (own, *recvs), (dup, ddown, dwo), full = refs[:-4], refs[-4:-1], refs[-1]
    fill(full, scalars, own, recvs)
    units, half = dup.shape[0], dwo.shape[0]
    for c in range(D // 128):
        at = slice(c * 128, c * 128 + 128)
        dup[:, at] = full[c * units:(c + 1) * units].astype(F32)
        ddown[:, at] = full[(4 + c) * units:(5 + c) * units].astype(F32)
        dwo[:, at] = full[8 * units + c * half:8 * units + (c + 1) * half].astype(F32)


def finish_mlp(own, recvs, stage, units, half):
    return small_call(
        finish_mlp_kernel,
        [
            jax.ShapeDtypeStruct((units, D), F32), jax.ShapeDtypeStruct((units, D), F32),
            jax.ShapeDtypeStruct((half, D), F32),
        ],
        "finish_mlp", stage.scalars, own, *recvs, scratch=[pltpu.VMEM((stage.size * own.shape[0], 128), BF)],
    )


def parts_of(v):
    high = v.astype(BF)
    return jnp.concatenate([high, (v - high.astype(F32)).astype(BF)], 0)


def whole_of(v):
    m = v.shape[0] // 2
    return v[:m].astype(F32) + v[m:].astype(F32)


def settle_cols_kernel(scalars, keep, *refs):
    *recvs, cols, cols_recv, out = refs
    m = keep.shape[0]
    v = keep[...]
    for r in recvs:
        v = v + r[...].astype(F32)
    out[:m] = v.astype(BF)
    out[m:] = parts_of(cols[...] + cols_recv[...])


def settle_cols(keep, recvs, cols, cols_recv, stage):
    shape = (keep.shape[0] + 2 * cols.shape[0], 128)
    return small_call(
        settle_cols_kernel, [jax.ShapeDtypeStruct(shape, BF)], "settle_cols", stage.scalars, keep, *recvs, cols, cols_recv
    )[0]


def sum_cols(scalars, own, recvs, m, held):
    held[scalars[0]] = whole_of(own[m:])
    for k, r in enumerate(recvs):
        held[scalars[1 + k]] = whole_of(r[m:])
    total = held[0]
    for k in range(1, held.shape[0]):
        total = total + held[k]
    return total


def join_cols_kernel(scalars, *refs):
    (own, *recvs), out, held = refs[:-2], refs[-2], refs[-1]
    size = 1 + len(recvs)
    m = own.shape[0] - 2 * held.shape[1]
    fill(out.at[pl.ds(0, size * m)], scalars, own, recvs)
    out[size * m:] = parts_of(sum_cols(scalars, own, recvs, m, held))


def join_cols(own, recvs, stage, extra):
    m = own.shape[0] - extra
    return small_call(
        join_cols_kernel, [jax.ShapeDtypeStruct((stage.size * m + extra, 128), BF)], "join_cols", stage.scalars, own, *recvs,
        scratch=[pltpu.VMEM((stage.size, extra // 2, 128), F32)],
    )[0]


def finish_qkv_kernel(scalars, *refs):
    (own, *recvs), (out, cols, dub), (full, held) = refs[:-5], refs[-5:-2], refs[-2:]
    m = full.shape[0] // (1 + len(recvs))
    fill(full, scalars, own, recvs)
    total = sum_cols(scalars, own, recvs, m, held)
    cols[...] = total[:cols.shape[0]]
    dub[...] = total[cols.shape[0]:]
    half = out.shape[1]
    for c in range(D // 128):
        for t in range(3):
            row = (c * 3 + t) * half
            out[t, :, c * 128:c * 128 + 128] = full[row:row + half].astype(F32)


def finish_qkv(own, recvs, stage, half, extra):
    m = own.shape[0] - extra
    return small_call(
        finish_qkv_kernel,
        [
            jax.ShapeDtypeStruct((3, half, D), F32), jax.ShapeDtypeStruct((32, 128), F32),
            jax.ShapeDtypeStruct((extra // 2 - 32, 128), F32),
        ],
        "finish_qkv", stage.scalars, own, *recvs,
        scratch=[pltpu.VMEM((stage.size * m, 128), BF), pltpu.VMEM((stage.size, extra // 2, 128), F32)],
    )


def advance(steps, token):
    try:
        return steps.send(token), None
    except StopIteration as end:
        return token, end.value


def body(
    latents, scene_len, attn_gain, attn_shift, qkv_weight, out_weight, out_bias, mlp_gain, mlp_shift,
    up_weight, up_bias, down_weight, down_bias, cotangent,
):
    rows = latents.shape[0] // lax.axis_size("tensor")
    units, half = up_weight.shape[0], out_weight.shape[0]
    heads = half // HD
    tens = lax.axis_index("tensor").astype(jnp.int32).reshape(1)
    count = lax.axis_size("dp")
    steps = count.bit_length() - 1
    assert 1 << steps == count and steps > 1
    lower, upper = list(range(steps - 2)), [steps - 2, steps - 1]
    turned = [b ^ 1 if b ^ 1 < steps - 2 else b for b in lower]
    group = Stage(count, (upper, upper), ([1, 2, 3], [2, 1, 3]))
    pairs = [Stage(count, ([a], [b])) for a, b in zip(lower, turned)]
    mlp_stages = pairs + [group]
    if len(lower) % 2:
        qkv_stages = mlp_stages
    else:
        qkv_stages = [
            Stage(count, (lower[i:i + 2],) * 2, ([1, 2, 3], [2, 1, 3])) for i in range(0, len(lower), 2)
        ] + [group]

    wq = qkv_weight.reshape(3 * half, D)
    wq_oth, wo_oth = swap(wq), swap(out_weight)
    vecs = rows_of(attn_gain, attn_shift, out_bias, mlp_gain, mlp_shift, down_bias, up_bias)
    vecs_oth = swap(vecs)
    up_oth, down_oth = swap(up_weight), swap(down_weight)

    n1, qkv, p, att, rl, h1, n2 = attention_forward(
        tens, scene_len, latents, vecs, wq, wq_oth, out_weight, wo_oth, rows
    )
    need = 8 * units + 4 * half
    total_rows = -(-need // (16 * count)) * 16 * count
    act, gh, doa, grads_own, grads_oth, cols_two, grad_ub = mlp(
        tens, n2, cotangent, up_weight, down_weight, up_oth, down_oth, vecs_oth, vecs, h1, att, rl, out_weight, wo_oth, total_rows
    )
    from_peer = swap(grads_oth)

    def exchanges(stages, keep, sends, settled, joined):
        for s, stage in enumerate(stages):
            recvs = stage.exchange(sends)
            token = yield sends[-1]
            recvs = [tie(r, token) for r in recvs]
            if s + 1 < len(stages):
                keep, sends = split(keep, recvs, stages[s + 1])
            else:
                have = settled(keep, recvs, stage)
        for s in range(len(stages) - 1, -1, -1):
            recvs = stages[s].exchange([have] * (stages[s].size - 1))
            token = yield have
            recvs = [tie(r, token) for r in recvs]
            if s:
                have = joined(have, recvs, stages[s])
        return have, recvs

    qkv_rows = -(-12 * half // (16 * count)) * 16 * count
    extra = 2 * (4 * 8 + units // 128)
    dqkv, dw, qkv_peer = None, None, None
    token = grads_oth
    chains, results = {}, {}
    cols = []

    def step(name):
        if name not in results:
            after, result = advance(chains[name], token)
            if result is not None:
                results[name] = result
            return after
        return token

    for action, *rest in PLAN:
        if action == "back":
            side, first, number = rest
            dqkv, dw = attention_back(tie(tens, token), p, doa, qkv, n1, dqkv, dw, side, first, number, qkv_rows)
            token = dw
            if side and first + number == rows // LAT:
                qkv_peer = swap(dw)
        elif action == "mlp":
            chains["mlp"] = exchanges(
                mlp_stages, *split_mlp(grads_own, tie(from_peer, token), mlp_stages[0]), settle, join
            )
            token = next(chains["mlp"])
        elif action == "qkv":
            chains["qkv"] = exchanges(
                qkv_stages, *split(tie(dw, token), [qkv_peer], qkv_stages[0]),
                lambda keep, recvs, stage: settle_cols(keep, recvs, *cols, stage),
                lambda own, recvs, stage: join_cols(own, recvs, stage, extra),
            )
            token = next(chains["qkv"])
        elif action == "norm":
            grad_latents, cols_one, cols_give = norm_one_back(
                tie(tens, token), dqkv, wq, wq_oth, latents, vecs, gh, cols_two, grad_ub
            )
            cols.extend((cols_one, swap(cols_give)))
            token = cols_one
        elif action == "out":
            out = block_out(tie(tens, token), act, down_weight, down_oth, vecs, h1)
            token = out
        elif action == "end":
            while "mlp" not in results:
                token = step("mlp")
            have, recvs = results["mlp"]
            dup, ddown, dwo = finish_mlp(tie(have, token), recvs, mlp_stages[0], units, half)
            token = dwo
        else:
            token = step(action[:3])
    while "qkv" not in results:
        token = step("qkv")
    dwq, shared, dub = finish_qkv(*results["qkv"], qkv_stages[0], half, extra)
    shared = shared.reshape(D // 128, 8, 128).transpose(1, 0, 2).reshape(8, D)
    return (
        out, grad_latents, shared[0], shared[1], dwq, dwo, shared[4],
        shared[2], shared[3], dup, dub.reshape(units), ddown, shared[5],
    )


def solution(mesh):
    placed = (
        P("dp", None), P("dp"), P(), P(), P(None, "tensor", None), P("tensor", None), P(), P(), P(),
        P("tensor", None), P("tensor"), P("tensor", None), P(), P("dp", None),
    )
    return jax.shard_map(
        body,
        mesh=mesh,
        in_specs=placed,
        out_specs=(
            P(("dp", "tensor"), None), P(("dp", "tensor"), None), P(), P(), P(None, "tensor", None),
            P("tensor", None), P(), P(), P(), P("tensor", None), P("tensor"), P("tensor", None), P(),
        ),
        check_vma=False,
    )
```
